32 devices in a mesh: ctx: 4 (over y, x), fsdp: 8 (over z, core).
Axes of the slice: x: 2, y: 2, z: 4, core: 2. Of those that a mesh axis runs over, the one named last changes fastest.
Arguments:
- inputs: bfloat16 [8, 1024, 2048], P('fsdp', 'ctx'), may hold values from -6 to 6
- cotangent: bfloat16 [8, 1024, 2048], P('fsdp', 'ctx'), may hold values from -13 to 13
- gains: float32 [2, 2048], replicated, may hold values from 0.5 to 1.5
- gain_moment: float32 [2, 2048], replicated, may hold values from -192 to 192
- gain_second: float32 [2, 2048], replicated, may hold values from 4096 to 16384
- w_query: float32 [2048, 2048], P('fsdp'), may hold values from -0.125 to 0.125
- w_key: float32 [2048, 256], P(None, 'fsdp'), may hold values from -0.125 to 0.125
- w_value: float32 [2048, 256], P(None, 'fsdp'), may hold values from -0.125 to 0.125
- w_out: float32 [2048, 2048], P('fsdp'), may hold values from -1 to 1
- w_gate: float32 [2048, 5632], P('fsdp'), may hold values from -0.125 to 0.125
- w_up: float32 [2048, 5632], P('fsdp'), may hold values from -0.125 to 0.125
- w_down: float32 [5632, 2048], P(None, 'fsdp'), may hold values from -0.078125 to 0.078125
- m_query: float32 [2048, 2048], P('fsdp', 'ctx'), may hold values from -1176.6257 to 1176.6257
- m_key: float32 [2048, 256], P('ctx', 'fsdp'), may hold values from -1176.6257 to 1176.6257
- m_value: float32 [2048, 256], P('ctx', 'fsdp'), may hold values from -3529.877 to 3529.877
- m_out: float32 [2048, 2048], P('fsdp', 'ctx'), may hold values from -181.01934 to 181.01934
- m_gate: float32 [2048, 5632], P('fsdp', 'ctx'), may hold values from -1176.6257 to 1176.6257
- m_up: float32 [2048, 5632], P('fsdp', 'ctx'), may hold values from -1176.6257 to 1176.6257
- m_down: float32 [5632, 2048], P('ctx', 'fsdp'), may hold values from -1176.6257 to 1176.6257
Outputs:
- block_out: bfloat16 [8, 1024, 2048], P('fsdp', 'ctx')
- input_grad: float32 [8, 1024, 2048], P('fsdp', 'ctx')
- gain_grad: float32 [2, 2048], replicated
- gain_moment_new: float32 [2, 2048], replicated
- gain_second_new: float32 [2, 2048], replicated
- gains_new: float32 [2, 2048], replicated
- grad_query: float32 [2048, 2048], P('fsdp', 'ctx')
- moment_query: float32 [2048, 2048], P('fsdp', 'ctx')
- new_query: float32 [2048, 2048], P('fsdp')
- grad_key: float32 [2048, 256], P('ctx', 'fsdp')
- moment_key: float32 [2048, 256], P('ctx', 'fsdp')
- new_key: float32 [2048, 256], P(None, 'fsdp')
- grad_value: float32 [2048, 256], P('ctx', 'fsdp')
- moment_value: float32 [2048, 256], P('ctx', 'fsdp')
- new_value: float32 [2048, 256], P(None, 'fsdp')
- grad_out: float32 [2048, 2048], P('fsdp', 'ctx')
- moment_out: float32 [2048, 2048], P('fsdp', 'ctx')
- new_out: float32 [2048, 2048], P('fsdp')
- grad_gate: float32 [2048, 5632], P('fsdp', 'ctx')
- moment_gate: float32 [2048, 5632], P('fsdp', 'ctx')
- new_gate: float32 [2048, 5632], P('fsdp')
- grad_up: float32 [2048, 5632], P('fsdp', 'ctx')
- moment_up: float32 [2048, 5632], P('fsdp', 'ctx')
- new_up: float32 [2048, 5632], P('fsdp')
- grad_down: float32 [5632, 2048], P('ctx', 'fsdp')
- moment_down: float32 [5632, 2048], P('ctx', 'fsdp')
- new_down: float32 [5632, 2048], P(None, 'fsdp')
The draws below stay inside these ranges and needn't reach their ends.
All inputs are finite; a program needn't handle non-finite values.
Results may differ from the reference program's by a relative error of at most 0.024.
Values may be sent and summed in bfloat16 or wider, within the bound.
A program may use at most 448 MiB of HBM per device.

```python
import math
import jax
import jax.numpy as jnp
from jax import lax

D = 2048
H = 32
KV = 4
HD = 64
FF = 5632
NS = 5
STEP = 10
SEQ = 1024
SEQS = 8


def ramp_table(rows, cols, ramp):
    row_part = jnp.arange(rows, dtype=jnp.float32) / max(rows - 1, 1)
    col_part = jnp.arange(cols, dtype=jnp.float32) / max(cols - 1, 1)
    return jnp.exp(math.log(ramp) * (row_part[:, None] + col_part[None, :] - 1.0))


def draw_cotangent(key, part):
    key = jax.random.fold_in(key, 5)
    noise = jax.random.truncated_normal(key, -4.0, 4.0, (SEQS, SEQ, D), jnp.float32)
    ramp = 3.0
    return (noise * ramp_table(SEQS, SEQ, ramp)[:, :, None]).astype(jnp.bfloat16)


def moment_noise(key, rows, cols, factor, ramp, spread_law):
    return spread_law * ramp_table(rows, cols, ramp) * factor * (SEQ * SEQS) ** 0.5


def draw_m_query(key, part):
    key = jax.random.fold_in(key, 11)
    noise = jax.random.truncated_normal(key, -4.0, 4.0, (D, H * HD), jnp.float32)
    ramp = 3.0
    return moment_noise(key, D, H * HD, 1.0, ramp, noise)


def draw_m_key(key, part):
    key = jax.random.fold_in(key, 12)
    noise = jax.random.truncated_normal(key, -4.0, 4.0, (D, KV * HD), jnp.float32)
    ramp = 3.0
    return moment_noise(key, D, KV * HD, 1.0, ramp, noise)


def draw_m_value(key, part):
    key = jax.random.fold_in(key, 13)
    noise = jax.random.truncated_normal(key, -4.0, 4.0, (D, KV * HD), jnp.float32)
    ramp = 3.0
    return moment_noise(key, D, KV * HD, 3.0, ramp, noise)


def draw_m_out(key, part):
    key = jax.random.fold_in(key, 14)
    noise = jax.random.truncated_normal(key, -4.0, 4.0, (H * HD, D), jnp.float32)
    ramp = 3.0
    return moment_noise(key, H * HD, D, 0.15, ramp, noise)


def draw_m_gate(key, part):
    key = jax.random.fold_in(key, 15)
    noise = jax.random.truncated_normal(key, -4.0, 4.0, (D, FF), jnp.float32)
    ramp = 3.0
    return moment_noise(key, D, FF, 1.0, ramp, noise)


def draw_m_up(key, part):
    key = jax.random.fold_in(key, 16)
    noise = jax.random.truncated_normal(key, -4.0, 4.0, (D, FF), jnp.float32)
    ramp = 3.0
    return moment_noise(key, D, FF, 1.0, ramp, noise)


def draw_m_down(key, part):
    key = jax.random.fold_in(key, 17)
    noise = jax.random.truncated_normal(key, -4.0, 4.0, (FF, D), jnp.float32)
    ramp = 3.0
    return moment_noise(key, FF, D, 1.0, ramp, noise)


def level_of(own_key, extent, split, least, largest):
    gain = 1.0
    for dim, blocks in split:
        draws = jax.random.uniform(jax.random.fold_in(jax.random.fold_in(own_key, 6), dim), (blocks,), jnp.float32, least / len(split), largest / len(split))
        gain = gain * jnp.repeat(jnp.exp(draws), extent[dim] // blocks).reshape((-1,) + (1,) * (len(extent) - 1 - dim))
    return gain


def centred(rng, extent, deviation, reach, shards=(), held_as=jnp.bfloat16):
    array = jax.random.normal(rng, extent, jnp.float32) * deviation
    if len(shards) > 0:
        array = level_of(rng, extent, shards, -0.22, 0.18) * array
    return jnp.clip(array, min=-reach, max=reach).astype(held_as)


def setup_inputs(seed: int = 0) -> dict:
    streams_of = jax.random.split(jax.random.key(seed), 20)
    return {
        "inputs": centred(streams_of[0], (SEQS, SEQ, D), 1.0, 6.0, ((0, 8), (1, 4))),
        "cotangent": draw_cotangent(jax.random.fold_in(streams_of[19], 71), 0),
        "gains": jnp.clip(1.0 + 0.1 * jax.random.normal(streams_of[2], (2, D), jnp.float32), 0.5, 1.5),
        "gain_moment": centred(streams_of[3], (2, D), ((SEQ * SEQS) ** 0.5 / 3), 192.0, (), jnp.float32),
        "gain_second": jnp.clip(jnp.exp(jax.random.uniform(streams_of[4], (2, D), jnp.float32, math.log(4096.0), math.log(16384.0))), 4096.0, 16384.0),
        "w_query": centred(streams_of[5], (D, H * HD), D ** -0.5, 0.125, ((0, 8),), jnp.float32),
        "w_key": centred(streams_of[6], (D, KV * HD), D ** -0.5, 0.125, ((1, 8),), jnp.float32),
        "w_value": centred(streams_of[7], (D, KV * HD), D ** -0.5, 0.125, ((1, 8),), jnp.float32),
        "w_out": centred(streams_of[8], (H * HD, D), 32 ** -0.5, 1.0, ((0, 8),), jnp.float32),
        "w_gate": centred(streams_of[9], (D, FF), D ** -0.5, 0.125, ((0, 8),), jnp.float32),
        "w_up": centred(streams_of[10], (D, FF), D ** -0.5, 0.125, ((0, 8),), jnp.float32),
        "w_down": centred(streams_of[11], (FF, D), FF ** -0.5, 0.078125, ((1, 8),), jnp.float32),
        "m_query": draw_m_query(jax.random.fold_in(streams_of[19], 71), 0),
        "m_key": draw_m_key(jax.random.fold_in(streams_of[19], 71), 0),
        "m_value": draw_m_value(jax.random.fold_in(streams_of[19], 71), 0),
        "m_out": draw_m_out(jax.random.fold_in(streams_of[19], 71), 0),
        "m_gate": draw_m_gate(jax.random.fold_in(streams_of[19], 71), 0),
        "m_up": draw_m_up(jax.random.fold_in(streams_of[19], 71), 0),
        "m_down": draw_m_down(jax.random.fold_in(streams_of[19], 71), 0),
    }


@jax.custom_vjp
def low(v):
    return lax.optimization_barrier(v.astype(jnp.bfloat16)).astype(jnp.float32)

@jax.custom_vjp
def low_back(v):
    return v

def low_keep(v):
    return (low(v), None)

def low_pass(kept, grad):
    return (grad,)

def back_keep(v):
    return (v, None)

def back_low(kept, grad):
    return (low(grad),)
low.defvjp(low_keep, low_pass)
low_back.defvjp(back_keep, back_low)
norm_eps = 1e-05
rope_base = 10000.0
masked_score = -1e+30
poly_first = 3.4445
poly_second = -4.775
poly_third = 2.0315
momentum_decay = 0.95
muon_rate = 0.3
weight_decay = 0.1
adam_first = 0.9
adam_second = 0.95
adam_rate = 0.4
adam_eps = 1e-08
highest = lax.Precision.HIGHEST

def rope_tables(positions, head_width):
    frequency = jnp.exp(jnp.arange(head_width // 2, dtype=jnp.float32) * (-2.0 * math.log(rope_base) / head_width))
    angles = positions[:, None] * frequency[None, :]
    cos_half = jnp.cos(angles)
    sin_half = jnp.sin(angles)
    return (jnp.concatenate([cos_half, cos_half], -1), jnp.concatenate([sin_half, sin_half], -1))

def rotate(values, cos_table, sin_table):
    half_width = values.shape[-1] // 2
    turned = jnp.concatenate([-values[..., half_width:], values[..., :half_width]], -1)
    return values * cos_table[:, None, :] + turned * sin_table[:, None, :]

def rms_norm(values, gain_row):
    return values * lax.rsqrt(lax.optimization_barrier(jnp.mean(values * values, -1, keepdims=True)) + norm_eps) * gain_row

def product(first_op, second_op):
    return jnp.dot(first_op, second_op, precision=highest)

def attention(query, key_rows, values):
    block_rows = min(512, SEQ)
    block_count = SEQ // block_rows
    blocks = query.reshape(block_count, block_rows, KV, H // KV, HD)
    key_pos = jnp.arange(SEQ)

    def one_block(block_args):
        row_block, position = block_args
        scores = low_back(jnp.einsum('tkgd,skd->kgts', row_block, key_rows, precision=highest) * HD ** (-0.5))
        query_pos = position * block_rows + jnp.arange(block_rows)
        visible = key_pos[None, :] <= query_pos[:, None]
        scores = jnp.where(visible, scores, masked_score)
        row_top = lax.optimization_barrier(jnp.max(scores, -1, keepdims=True))
        weights = jnp.exp(scores - row_top)
        weights = low(weights / lax.optimization_barrier(jnp.sum(weights, -1, keepdims=True)))
        return jnp.einsum('kgts,skd->tkgd', weights, values, precision=highest)
    outputs = lax.map(jax.checkpoint(one_block), (blocks, jnp.arange(block_count)))
    return outputs.reshape(SEQ, H * HD)

def layer(stream, gains, w_query, w_key, w_value, w_out, w_gate, w_up, w_down):
    cos_table, sin_table = rope_tables(jnp.arange(SEQ, dtype=jnp.float32), HD)
    normed = low(rms_norm(stream, gains[0]))
    query = low_back(product(normed, low(w_query)))
    key_rows = low_back(product(normed, low(w_key)))
    values = low(low_back(product(normed, low(w_value))))
    query = low(rotate(query.reshape(SEQ, H, HD), cos_table, sin_table)).reshape(SEQ, KV, H // KV, HD)
    key_rows = low(rotate(key_rows.reshape(SEQ, KV, HD), cos_table, sin_table))
    mixed_rows = low(low_back(attention(query, key_rows, values.reshape(SEQ, KV, HD))))
    middle = stream + low_back(product(mixed_rows, low(w_out)))
    normed_two = low(rms_norm(middle, gains[1]))
    gate_pre = low_back(product(normed_two, low(w_gate)))
    upper = low_back(product(normed_two, low(w_up)))
    hidden = low(jax.nn.silu(gate_pre) * upper)
    return middle + low_back(product(hidden, low(w_down)))

def muon(weight, grad_sum, moment, transposed, spread):
    moment_new = momentum_decay * moment + grad_sum
    matrix = moment_new.T if transposed else moment_new
    matrix = low(matrix / (jnp.sqrt(jnp.sum(moment_new * moment_new)) + 1e-07))
    for sweep in range(NS):
        gram_rows = low(jnp.dot(matrix, matrix.T, precision=highest))
        first_pass = low(jnp.dot(gram_rows, matrix, precision=highest))
        second_pass = jnp.dot(gram_rows, first_pass, precision=highest)
        matrix = low(poly_first * matrix + poly_second * first_pass + poly_third * second_pass)
    orthogonal = matrix.T if transposed else matrix
    step_size = muon_rate * spread * math.sqrt(max(weight.shape))
    return (grad_sum, moment_new, weight * (1.0 - muon_rate * weight_decay) - step_size * orthogonal)

def reference(inputs, cotangent, gains, gain_moment, gain_second, w_query, w_key, w_value, w_out, w_gate, w_up, w_down, m_query, m_key, m_value, m_out, m_gate, m_up, m_down):
    weights = (w_query, w_key, w_value, w_out, w_gate, w_up, w_down)

    def per_sequence(totals, seq_pair):
        stream, back_rows = seq_pair
        output, pullback = jax.vjp(layer, stream.astype(jnp.float32), gains, *weights)
        gradients = pullback(back_rows.astype(jnp.float32))
        totals = tuple((total_now + grad_now for total_now, grad_now in zip(totals, gradients[1:])))
        return (totals, (output.astype(jnp.bfloat16), gradients[0]))
    start_sums = tuple((jnp.zeros_like(weight) for weight in (gains,) + weights))
    totals, (block_out, input_grad) = lax.scan(per_sequence, start_sums, (inputs, cotangent))
    gain_grad = totals[0]
    moment_one = adam_first * gain_moment + (1.0 - adam_first) * gain_grad
    moment_two = adam_second * gain_second + (1.0 - adam_second) * gain_grad * gain_grad
    adam_ratio = moment_one / (1.0 - adam_first ** STEP) / (jnp.sqrt(moment_two / (1.0 - adam_second ** STEP)) + adam_eps)
    gains_new = gains - adam_rate * adam_ratio
    spreads = (D ** (-0.5), D ** (-0.5), D ** (-0.5), 32 ** (-0.5), D ** (-0.5), D ** (-0.5), FF ** (-0.5))
    flips = (False, True, True, False, False, False, True)
    moments = (m_query, m_key, m_value, m_out, m_gate, m_up, m_down)
    results = []
    for position in range(7):
        results.extend(muon(weights[position], totals[position + 1], moments[position], flips[position], spreads[position]))
    return (block_out, input_grad, gain_grad, moment_one, moment_two, gains_new, results[0], results[1], results[2], results[3], results[4], results[5], results[6], results[7], results[8], results[9], results[10], results[11], results[12], results[13], results[14], results[15], results[16], results[17], results[18], results[19], results[20])
```

```python
import functools
import math

import jax
import jax.numpy as jnp
from jax import lax
from jax.experimental import pallas as pl
from jax.experimental.pallas import tpu as pltpu
from jax.sharding import Mesh
from jax.sharding import PartitionSpec as P

D = 2048
H = 32
KV = 4
HD = 64
FF = 5632
NS = 5
STEP = 10


norm_eps = 1e-05
rope_base = 10000.0
masked_score = -1e30
poly_first = 3.4445
poly_second = -4.775
poly_third = 2.0315
momentum_decay = 0.95
muon_rate = 0.3
weight_decay = 0.1
adam_first = 0.9
adam_second = 0.95
adam_rate = 0.4
adam_eps = 1e-08

MESH = pl.DeviceIdType.MESH
CTX = ("ctx_hi", "ctx_lo")
PLANES = ("z_hi", "z_lo")
PLANE = ("core",) + CTX
EVERY = CTX + PLANES + ("core",)


def rope_tables(positions, head_width):
    frequency = jnp.exp(
        jnp.arange(head_width // 2, dtype=jnp.float32) * (-2.0 * math.log(rope_base) / head_width)
    )
    angles = positions[:, None] * frequency[None, :]
    cos_half = jnp.cos(angles)
    sin_half = jnp.sin(angles)
    return (jnp.concatenate([cos_half, cos_half], -1), jnp.concatenate([sin_half, sin_half], -1))


def turn(values):
    half_width = values.shape[-1] // 2
    return jnp.concatenate([-values[..., half_width:], values[..., :half_width]], -1)


def norm_forward(values, gain_row):
    inverse = lax.rsqrt(jnp.mean(values * values, -1, keepdims=True) + norm_eps)
    return (values * inverse * gain_row, inverse)


def norm_backward(values, inverse, gain_row, gradients):
    scaled = gradients * gain_row
    inner_mean = jnp.mean(scaled * values, -1, keepdims=True)
    return (
        inverse * scaled - values * inverse**3 * inner_mean,
        jnp.sum(gradients * values * inverse, 0),
    )


def matmul(first_op, second_op):
    return jnp.dot(first_op, second_op, preferred_element_type=jnp.float32)


def contract_rows(first_op, second_op):
    return lax.dot_general(
        first_op, second_op, (((0,), (0,)), ((), ())), preferred_element_type=jnp.float32
    )


def contract_cols(first_op, second_op):
    return lax.dot_general(
        first_op, second_op, (((1,), (1,)), ((), ())), preferred_element_type=jnp.float32
    )


def low(values):
    return values.astype(jnp.bfloat16)


def orthogonal_kernel(
    shape,
    m_ref,
    x_ref,
    y_ref,
    a_ref,
    part,
    from_core,
    from_ctx,
    gathered,
    scale,
    core_out,
    core_in,
    ctx_out,
    ctx_in,
    back_core_out,
    back_core_in,
    back_out,
    back_in,
):
    n_ctx, n_lo, n_planes, halved = shape
    stages = n_ctx.bit_length() - 1
    blocks = 2 * n_ctx
    side = D // blocks
    reach = blocks // 2 + 1
    ctx = lax.axis_index("ctx_hi") * n_lo + lax.axis_index("ctx_lo")
    core = lax.axis_index("core")
    z_lo = lax.axis_size("z_lo")
    plane = lax.axis_index("z_hi") * z_lo + lax.axis_index("z_lo")
    half = plane // (n_planes - 1) if halved else 0
    turned = core * (1 - half)
    deltas = []
    for s in range(1, stages + 1):
        step = turned * 2 ** (stages - s) + (1 - turned) * 2 ** (s - 1)
        deltas.append(step * (1 - 2 * ((ctx // step) % 2)))

    def partner(s):
        there = ctx + deltas[s - 1]
        return {"ctx_hi": there // n_lo, "ctx_lo": there % n_lo}

    other_core = {"core": 1 - core}

    def place(own_core, idx):
        where = ctx
        for s in range(1, stages + 1):
            where = where + ((idx // 2 ** (stages - s)) % 2) * deltas[s - 1]
        return 2 * where + (core if own_core else 1 - core)

    def across(idx):
        mirrored = 0
        for s in range(stages):
            mirrored = mirrored + ((idx // 2**s) % 2) * 2 ** (stages - 1 - s)
        return half * idx + (1 - half) * mirrored

    def rows_of(block):
        return pl.ds(pl.multiple_of(block * side, side), side)

    def whole(flag, run):
        if halved:
            pl.when(half == flag)(run)
        elif flag == 0:
            run()

    barrier = pltpu.get_barrier_semaphore()
    pl.semaphore_signal(barrier, inc=1, device_id=other_core, device_id_type=MESH)
    for s in range(1, stages + 1):
        pl.semaphore_signal(barrier, inc=1, device_id=partner(s), device_id_type=MESH)
    pl.semaphore_wait(barrier, 1 + stages)

    def core_copy(idx):
        slot = across(idx)
        return pltpu.make_async_remote_copy(
            src_ref=part.at[1, idx],
            dst_ref=from_core.at[slot],
            send_sem=core_out.at[idx],
            recv_sem=core_in.at[slot],
            device_id=other_core,
            device_id_type=MESH,
        )

    def ctx_copy(s, idx):
        return pltpu.make_async_remote_copy(
            src_ref=part.at[0, idx],
            dst_ref=from_ctx.at[idx],
            send_sem=ctx_out.at[idx],
            recv_sem=ctx_in.at[idx],
            device_id=partner(s),
            device_id_type=MESH,
        )

    def back_copy(s, idx):
        there = idx + 2 ** (stages - s)
        block = place(True, idx)
        return pltpu.make_async_remote_copy(
            src_ref=gathered.at[block],
            dst_ref=gathered.at[block],
            send_sem=back_out.at[there],
            recv_sem=back_in.at[there],
            device_id=partner(s),
            device_id_type=MESH,
        )

    def back_core_copy(idx):
        block = place(True, idx)
        return pltpu.make_async_remote_copy(
            src_ref=gathered.at[block],
            dst_ref=gathered.at[block],
            send_sem=back_core_out.at[idx],
            recv_sem=back_core_in.at[across(idx)],
            device_id=other_core,
            device_id_type=MESH,
        )

    def gram_piece(own_core, idx):
        block = place(own_core, idx)
        left = x_ref[rows_of(block), :]
        for offset in range(reach):
            right = x_ref[rows_of((block + offset) % blocks), :]
            part[0 if own_core else 1, idx, offset] = low(contract_cols(left, right))

    def summed(idx, sources, target):
        def one(offset, carry):
            total = part[0, idx, offset].astype(jnp.float32)
            total = total + from_core[idx, offset].astype(jnp.float32)
            for source in sources:
                total = total + from_ctx[source, offset].astype(jnp.float32)
            target[offset] = low(total)
            return carry

        lax.fori_loop(0, reach, one, 0)

    def spread(block):
        for offset in range(reach):
            column = (block + offset) % blocks
            piece = gathered[block, offset]
            a_ref[rows_of(block), rows_of(column)] = piece
            if 0 < offset < reach - 1:
                a_ref[rows_of(column), rows_of(block)] = piece.T

    def sweep_body(sweep, carry):
        def send_piece(idx, inner):
            gram_piece(False, idx)
            core_copy(idx).start()
            return inner

        lax.fori_loop(0, n_ctx, send_piece, 0)

        def keep_piece(turn_index, inner):
            gram_piece(True, n_ctx - 1 - turn_index)
            return inner

        lax.fori_loop(0, n_ctx, keep_piece, 0)

        def core_arrived(idx):
            pltpu.make_async_remote_copy(
                src_ref=part.at[1, idx],
                dst_ref=from_core.at[idx],
                send_sem=core_out.at[idx],
                recv_sem=core_in.at[idx],
                device_id=other_core,
                device_id_type=MESH,
            ).wait_recv()

        def incoming(s, idx):
            return idx + 2 ** (stages - s)

        for s in range(1, stages + 1):
            upper = 2 ** (stages - s)
            for idx in range(2 * upper - 1, upper - 1, -1):
                core_arrived(idx)
                for t in range(1, s):
                    ctx_copy(t, incoming(t, idx)).wait_recv()
                summed(idx, [incoming(t, idx) for t in range(1, s)], part.at[0, idx])
                if s < stages:
                    ctx_copy(s, idx).start()
                else:
                    whole(0, lambda s=s, idx=idx: ctx_copy(s, idx).start())
        core_arrived(0)
        for t in range(1, stages):
            ctx_copy(t, incoming(t, 0)).wait_recv()
        early = [incoming(t, 0) for t in range(1, stages)]
        own = place(True, 0)

        def finish_whole():
            ctx_copy(stages, 1).wait_recv()
            summed(0, early + [1], gathered.at[own])

        def finish_half():
            summed(0, early, gathered.at[own])

            def one(offset, inner):
                gathered[place(True, 1), offset] = part[0, 1, offset]
                return inner

            lax.fori_loop(0, reach, one, 0)

        whole(0, finish_whole)
        whole(1, finish_half)

        def announce(idx):
            for s in range(stages, 0, -1):
                if idx < 2 ** (stages - s):
                    if s < stages:
                        back_copy(s, idx).start()
                    else:
                        whole(0, lambda s=s: back_copy(s, idx).start())
            back_core_copy(idx).start()

        def arrived(idx):
            s = stages + 1 - idx.bit_length()
            block = place(True, idx)
            pltpu.make_async_remote_copy(
                src_ref=gathered.at[block],
                dst_ref=gathered.at[block],
                send_sem=back_out.at[idx],
                recv_sem=back_in.at[idx],
                device_id=partner(s),
                device_id_type=MESH,
            ).wait_recv()

        def core_back_arrived(idx):
            block = place(False, idx)
            pltpu.make_async_remote_copy(
                src_ref=gathered.at[block],
                dst_ref=gathered.at[block],
                send_sem=back_core_out.at[idx],
                recv_sem=back_core_in.at[idx],
                device_id=other_core,
                device_id_type=MESH,
            ).wait_recv()

        announce(0)
        for idx in range(1, n_ctx):
            if idx == 1:
                whole(0, lambda: arrived(1))
            else:
                arrived(idx)
            announce(idx)
        for idx in range(n_ctx):
            core_back_arrived(idx)

        def spread_one(block, inner):
            spread(block)
            return inner

        lax.fori_loop(0, blocks, spread_one, 0)

        def norm_now():
            def one(block, total):
                rows = lax.broadcasted_iota(jnp.int32, (side, side), 0)
                cols = lax.broadcasted_iota(jnp.int32, (side, side), 1)
                piece = gathered[block, 0].astype(jnp.float32)
                piece = jnp.where(rows == cols, piece, 0.0)
                return total + jnp.sum(jnp.sum(piece, 0, keepdims=True), 1, keepdims=True)

            trace = lax.fori_loop(0, blocks, one, jnp.zeros((1, 1), jnp.float32))
            scale[...] = jnp.broadcast_to(1.0 / (jnp.sqrt(trace) + 1e-07), scale.shape)

        def norm_done():
            scale[...] = jnp.ones(scale.shape, jnp.float32)

        pl.when(sweep == 0)(norm_now)
        pl.when(sweep > 0)(norm_done)
        factor = scale[0:1, 0:1]
        tall = 512

        def first_product(step, inner):
            rows = pl.ds(pl.multiple_of(step * tall, tall), tall)
            y_ref[rows, :] = low(matmul(a_ref[rows, :], x_ref[...]) * (factor * factor * factor))
            return inner

        lax.fori_loop(0, D // tall, first_product, 0)

        def second_product(step, inner):
            rows = pl.ds(pl.multiple_of(step * tall, tall), tall)
            second = matmul(a_ref[rows, :], y_ref[...])
            x_ref[rows, :] = low(
                (poly_first * factor) * x_ref[rows, :].astype(jnp.float32)
                + poly_second * y_ref[rows, :].astype(jnp.float32)
                + (poly_third * factor * factor) * second
            )
            return inner

        lax.fori_loop(0, D // tall, second_product, 0)

        for idx in range(n_ctx):
            core_copy(idx).wait_send()
            back_core_copy(idx).wait_send()
        for s in range(1, stages + 1):
            upper = 2 ** (stages - s)
            for idx in range(upper, 2 * upper):
                if s < stages:
                    ctx_copy(s, idx).wait_send()
                else:
                    whole(0, lambda s=s, idx=idx: ctx_copy(s, idx).wait_send())
            for idx in range(upper):
                if s < stages:
                    back_copy(s, idx).wait_send()
                else:
                    whole(0, lambda s=s, idx=idx: back_copy(s, idx).wait_send())
        return carry

    x_ref[...] = m_ref[...]
    lax.fori_loop(0, NS, sweep_body, 0)


def orthogonal(matrix, n_ctx, n_lo, n_planes, halved):
    rows, columns = matrix.shape
    blocks = 2 * n_ctx
    side = rows // blocks
    reach = blocks // 2 + 1
    piece = (reach, side, side)
    dma = pltpu.SemaphoreType.DMA((n_ctx,))
    flops = NS * 5 * rows * rows * columns
    return pl.pallas_call(
        functools.partial(orthogonal_kernel, (n_ctx, n_lo, n_planes, halved)),
        out_shape=jax.ShapeDtypeStruct((rows, columns), jnp.bfloat16),
        in_specs=[pl.BlockSpec(memory_space=pltpu.VMEM)],
        out_specs=pl.BlockSpec(memory_space=pltpu.VMEM),
        scratch_shapes=[
            pltpu.VMEM((rows, columns), jnp.bfloat16),
            pltpu.VMEM((rows, rows), jnp.bfloat16),
            pltpu.VMEM((2, n_ctx) + piece, jnp.bfloat16),
            pltpu.VMEM((n_ctx,) + piece, jnp.bfloat16),
            pltpu.VMEM((n_ctx,) + piece, jnp.bfloat16),
            pltpu.VMEM((blocks,) + piece, jnp.bfloat16),
            pltpu.VMEM((8, 128), jnp.float32),
        ]
        + [dma] * 8,
        compiler_params=pltpu.CompilerParams(
            collective_id=0, has_side_effects=True, vmem_limit_bytes=56 * 2**20
        ),
        cost_estimate=pl.CostEstimate(flops=flops, bytes_accessed=8 * rows * columns, transcendentals=0),
        name="orthogonal",
    )(matrix)


def swap_core(values):
    return lax.ppermute(values, "core", [(0, 1), (1, 0)])


def split_cores(values, core):
    mine = jnp.where(core == 0, values[0], values[1])
    theirs = jnp.where(core == 0, values[1], values[0])
    got = swap_core(theirs)
    return jnp.stack([jnp.where(core == 0, mine, got), jnp.where(core == 0, got, mine)])


def causal_blocks(length):
    width = math.gcd(length, 512)
    return [(start, width, start + width) for start in range(0, length, width)]


def visible(start, width, stop):
    return (jnp.arange(stop)[None, :] <= (start + jnp.arange(width))[:, None])[None, None]


def attention_forward(query, keys, values, scale):
    outs, logs = [], []
    for start, width, stop in causal_blocks(query.shape[1]):
        rows = query[:, start:stop]
        scores = jnp.einsum("nthd,nsd->nhts", rows, keys[:, :stop], preferred_element_type=jnp.float32) * scale
        scores = jnp.where(visible(start, width, stop), scores, masked_score)
        top = jnp.max(scores, -1, keepdims=True)
        expo = jnp.exp(scores - top)
        total = jnp.sum(expo, -1, keepdims=True)
        out = jnp.einsum("nhts,nsd->nhtd", low(expo), values[:, :stop], preferred_element_type=jnp.float32)
        outs.append(jnp.transpose(out / total, (0, 2, 1, 3)))
        logs.append((top + jnp.log(total))[..., 0])
    return jnp.concatenate(outs, 1), jnp.concatenate(logs, 2)


def attention_backward(query, keys, values, mixed, logs, d_mixed, scale):
    d_query, d_keys, d_values = [], 0.0, 0.0
    length = query.shape[1]
    for start, width, stop in causal_blocks(length):
        rows, d_rows = query[:, start:stop], d_mixed[:, start:stop]
        scores = jnp.einsum("nthd,nsd->nhts", rows, keys[:, :stop], preferred_element_type=jnp.float32) * scale
        probs = jnp.exp(scores - logs[:, :, start:stop, None])
        probs = jnp.where(visible(start, width, stop), probs, 0.0)
        d_probs = jnp.einsum("nthd,nsd->nhts", d_rows, values[:, :stop], preferred_element_type=jnp.float32)
        delta = jnp.transpose(jnp.sum(d_rows.astype(jnp.float32) * mixed[:, start:stop], -1), (0, 2, 1))
        d_scores = low(probs * (d_probs - delta[..., None]))
        d_query.append(
            jnp.einsum("nhts,nsd->nthd", d_scores, keys[:, :stop], preferred_element_type=jnp.float32) * scale
        )
        more_keys = jnp.einsum("nhts,nthd->nsd", d_scores, rows, preferred_element_type=jnp.float32) * scale
        more_values = jnp.einsum("nhts,nthd->nsd", low(probs), d_rows, preferred_element_type=jnp.float32)
        pad = ((0, 0), (0, length - stop), (0, 0))
        d_keys = d_keys + jnp.pad(more_keys, pad)
        d_values = d_values + jnp.pad(more_values, pad)
    return jnp.concatenate(d_query, 1), d_keys, d_values


def small_newton_schulz(matrices):
    wide = matrices.astype(jnp.float32)
    norm = jnp.sqrt(jnp.sum(wide * wide, (1, 2), keepdims=True))
    current = low(wide / (norm + 1e-07))
    for sweep in range(NS):
        gram = low(jnp.einsum("nij,nkj->nik", current, current, preferred_element_type=jnp.float32))
        first = low(jnp.einsum("nik,nkj->nij", gram, current, preferred_element_type=jnp.float32))
        second = jnp.einsum("nik,nkj->nij", gram, first, preferred_element_type=jnp.float32)
        current = low(
            poly_first * current.astype(jnp.float32) + poly_second * first.astype(jnp.float32) + poly_third * second
        )
    return current


def body(
    inputs,
    cotangent,
    gains,
    gain_moment,
    gain_second,
    w_query,
    w_key,
    w_value,
    w_out,
    w_gate,
    w_up,
    w_down,
    m_query,
    m_key,
    m_value,
    m_out,
    m_gate,
    m_up,
    m_down,
):
    n_ctx = lax.axis_size("ctx_hi") * lax.axis_size("ctx_lo")
    n_lo = lax.axis_size("ctx_lo")
    n_planes = lax.axis_size("z_hi") * lax.axis_size("z_lo")
    ctx, core = lax.axis_index(CTX), lax.axis_index("core")
    plane = lax.axis_index(PLANES)
    halved = n_planes == 4
    ranks = 2 * n_ctx
    tokens = inputs.shape[1]
    length = tokens * n_ctx
    rows_here = w_query.shape[0]
    heads = H // ranks
    sharers = ranks // KV
    head_cols, ff_cols = D // ranks, FF // ranks
    scale = HD ** (-0.5)
    transpose_pairs = [(c * n_planes + z, z * n_planes + c) for c in range(n_ctx) for z in range(n_planes)]

    def transposed(values):
        return lax.ppermute(values, CTX + PLANES, transpose_pairs)

    def own_columns(weight, columns):
        part = lax.dynamic_slice_in_dim(weight, ctx * 2 * columns, 2 * columns, 1)
        part = jnp.transpose(low(part).reshape(rows_here, 2, columns), (1, 0, 2))
        return split_cores(part, core).reshape(2 * rows_here, columns)

    def over_planes(values):
        return lax.all_gather(values, PLANES, axis=0, tiled=True)

    key_value = jnp.stack([low(w_key), low(w_value)], 1)
    key_value = lax.all_gather(key_value, PLANES + ("core",), axis=0, tiled=False)
    own_head = lax.dynamic_slice_in_dim(key_value, (2 * ctx + core) // sharers * sharers, sharers, 0)
    wide_kv = jnp.transpose(own_head, (1, 2, 0, 3)).reshape(D, 2 * HD)
    wide_query = over_planes(own_columns(w_query, head_cols))
    wide_qkv = jnp.concatenate([wide_query, wide_kv], 1)
    out_part = transposed(low(lax.dynamic_slice_in_dim(w_out, ctx * (D // n_ctx), D // n_ctx, 1)))
    wide_out = lax.all_gather(out_part, PLANES, axis=1, tiled=True)
    wide_gate = over_planes(own_columns(w_gate, ff_cols))
    wide_up = over_planes(own_columns(w_up, ff_cols))
    wide_down = over_planes(own_columns(w_down.T, ff_cols))

    def over_plane(values):
        return lax.all_gather(values, PLANE, axis=0, tiled=True)

    def sum_plane(values):
        return lax.psum_scatter(low(values), PLANE, scatter_dimension=0, tiled=True).astype(jnp.float32)

    cos_table, sin_table = rope_tables(jnp.arange(length, dtype=jnp.float32), HD)
    stream = inputs[0].astype(jnp.float32)
    normed, inverse_one = norm_forward(stream, gains[0])
    all_normed = over_plane(low(normed))
    all_cotangent = over_plane(cotangent[0])
    projected = matmul(all_normed, wide_qkv).reshape(2, length, heads + 2, HD)
    roped = projected[:, :, : heads + 1]
    roped = low(roped * cos_table[:, None, :] + turn(roped) * sin_table[:, None, :])
    query_rot, key_rot = roped[:, :, :heads], roped[:, :, heads]
    value_low = low(projected[:, :, heads + 1])
    attn_float, logs = attention_forward(query_rot, key_rot, value_low, scale)
    mixed_low = low(attn_float).reshape(2 * length, head_cols)
    middle = stream + sum_plane(matmul(mixed_low, wide_out))
    normed_two, inverse_two = norm_forward(middle, gains[1])
    all_two = over_plane(low(normed_two))
    gate_pre = matmul(all_two, wide_gate)
    upper = matmul(all_two, wide_up)
    sigmoid_gate = jax.nn.sigmoid(gate_pre)
    silu_gate = gate_pre * sigmoid_gate
    hidden_low = low(silu_gate * upper)
    block_out = low(middle + sum_plane(contract_cols(hidden_low, wide_down)))[None]

    d_hidden = matmul(all_cotangent, wide_down)
    d_up = low(d_hidden * silu_gate)
    d_gate = low(d_hidden * upper * sigmoid_gate * (1.0 + gate_pre * (1.0 - sigmoid_gate)))
    d_normed_two = sum_plane(contract_cols(d_gate, wide_gate) + contract_cols(d_up, wide_up))
    d_mid_norm, gain_two = norm_backward(middle, inverse_two, gains[1], d_normed_two)
    d_middle = cotangent[0].astype(jnp.float32) + d_mid_norm
    all_branch = over_plane(low(d_middle))
    d_mixed = low(contract_cols(all_branch, wide_out)).reshape(2, length, heads, HD)
    d_query_rot, d_key_rot, d_value = attention_backward(
        query_rot, key_rot, value_low, attn_float, logs, d_mixed, scale
    )
    d_rot = jnp.concatenate([d_query_rot, d_key_rot[:, :, None]], 2)
    d_rot = d_rot * cos_table[:, None, :] - turn(d_rot) * sin_table[:, None, :]
    d_qkv = low(jnp.concatenate([d_rot, d_value[:, :, None]], 2)).reshape(2 * length, head_cols + 2 * HD)
    d_normed = sum_plane(contract_cols(d_qkv, wide_qkv))
    d_in_norm, gain_one = norm_backward(stream, inverse_one, gains[0], d_normed)
    input_grad = (d_middle + d_in_norm)[None]

    def sum_planes(values, dimension=0):
        return lax.psum_scatter(low(values), PLANES, scatter_dimension=dimension, tiled=True)

    def to_shard(values):
        columns = values.shape[1]
        both = split_cores(values.reshape(2, rows_here, columns), core)
        return jnp.transpose(both, (1, 0, 2)).reshape(rows_here, 2 * columns)

    grad_down = to_shard(sum_planes(contract_rows(all_cotangent, hidden_low))).astype(jnp.float32)
    grad_gate = to_shard(sum_planes(contract_rows(all_two, d_gate))).astype(jnp.float32)
    grad_up = to_shard(sum_planes(contract_rows(all_two, d_up))).astype(jnp.float32)
    grad_out = transposed(sum_planes(contract_rows(mixed_low, all_branch), 1)).astype(jnp.float32)
    grad_qkv = sum_planes(contract_rows(all_normed, d_qkv))
    grad_query = to_shard(grad_qkv[:, :head_cols]).astype(jnp.float32)
    grad_kv = transposed(grad_qkv[:, head_cols:]).reshape(-1, 2, HD)
    grad_kv = lax.psum_scatter(grad_kv.astype(jnp.float32), ("z_lo", "core"), scatter_dimension=2, tiled=True)
    grad_key, grad_value = grad_kv[:, 0], grad_kv[:, 1]

    def momentum(moment, gradient):
        return momentum_decay * moment + gradient

    new_m_query = momentum(m_query, grad_query)
    new_m_key = momentum(m_key, grad_key)
    new_m_value = momentum(m_value, grad_value)
    new_m_out = momentum(m_out, grad_out)
    new_m_gate = momentum(m_gate, grad_gate)
    new_m_up = momentum(m_up, grad_up)
    grad_down = grad_down.T
    new_m_down = momentum(m_down, grad_down)

    gain_grad = lax.psum(jnp.stack([gain_one, gain_two]), EVERY)
    moment_one = adam_first * gain_moment + (1.0 - adam_first) * gain_grad
    moment_two = adam_second * gain_second + (1.0 - adam_second) * gain_grad * gain_grad
    adam_ratio = (
        moment_one
        / (1.0 - adam_first**STEP)
        / (jnp.sqrt(moment_two / (1.0 - adam_second**STEP)) + adam_eps)
    )
    gains_new = gains - adam_rate * adam_ratio

    def to_rank(values):
        columns = values.shape[1] // 2
        both = jnp.transpose(low(values).reshape(rows_here, 2, columns), (1, 0, 2))
        return split_cores(both, core).reshape(2 * rows_here, columns)

    def pad_columns(values):
        return jnp.pad(values, ((0, 0), (0, ff_cols - values.shape[1])))

    half_pairs = [(c, (c + n_ctx // 2) % n_ctx) for c in range(n_ctx)]
    lower = ctx < n_ctx // 2

    def two_halves(first, second):
        got = lax.ppermute(jnp.where(lower, second, first), CTX, half_pairs)
        kept = jnp.where(lower, first, second)
        return jnp.concatenate([jnp.where(lower, kept, got), jnp.where(lower, got, kept)], 1)

    def two_whole(values):
        columns = values.shape[1] // 2
        left, right = values[:, :columns], values[:, columns:]
        got = lax.ppermute(jnp.where(lower, right, left), CTX, half_pairs)
        kept = jnp.where(lower, left, right)
        return jnp.where(lower, kept, got), jnp.where(lower, got, kept)

    rank_query, rank_out = to_rank(new_m_query), to_rank(new_m_out)
    slots = [to_rank(new_m_gate), to_rank(new_m_up), to_rank(new_m_down.T)]
    if halved:
        slots.append(pad_columns(two_halves(rank_query, rank_out)))
    else:
        slots += [pad_columns(rank_query), pad_columns(rank_out)]
        slots += [jnp.zeros_like(slots[0])] * (n_planes - len(slots))
    matrix = lax.all_to_all(jnp.stack(slots), PLANES, split_axis=0, concat_axis=0, tiled=True)
    polar = orthogonal(matrix.reshape(D, ff_cols), n_ctx, n_lo, n_planes, halved)
    polar = polar.reshape(n_planes, 2 * rows_here, ff_cols)
    polar = lax.all_to_all(polar, PLANES, split_axis=0, concat_axis=0, tiled=True)
    if halved:
        polar_query, polar_out = two_whole(polar[3][:, : 2 * head_cols])
    else:
        polar_query, polar_out = polar[3][:, :head_cols], polar[4][:, :head_cols]
    polar = jnp.concatenate([polar[0], polar[1], polar[2], polar_query, polar_out], 1)
    polar = split_cores(polar.reshape(2, rows_here, -1), core)
    polar = lax.all_gather(polar, CTX, axis=0, tiled=True)

    def whole_rows(start, columns):
        part = polar[:, :, start : start + columns]
        return jnp.transpose(part, (1, 0, 2)).reshape(rows_here, ranks * columns).astype(jnp.float32)

    moment_kv = low(jnp.stack([new_m_key, new_m_value], 0))
    moment_kv = lax.all_gather(moment_kv, CTX + PLANES + ("core",), axis=0, tiled=False)
    moment_kv = moment_kv.reshape((n_ctx, 2 * n_planes) + moment_kv.shape[1:])
    moment_kv = jnp.transpose(moment_kv, (2, 1, 4, 0, 3)).reshape(2, KV * HD, D)
    polar_kv = small_newton_schulz(moment_kv)
    kv_cols = w_key.shape[1]
    polar_kv = lax.dynamic_slice_in_dim(polar_kv, (2 * plane + core) * kv_cols, kv_cols, 1)
    polar_kv = jnp.transpose(polar_kv, (0, 2, 1)).astype(jnp.float32)

    def updated(weight, spread, widest, direction):
        return weight * (1.0 - muon_rate * weight_decay) - (muon_rate * spread * math.sqrt(widest)) * direction

    new_query = updated(w_query, D ** (-0.5), max(D, H * HD), whole_rows(3 * ff_cols, head_cols))
    new_key = updated(w_key, D ** (-0.5), max(D, KV * HD), polar_kv[0])
    new_value = updated(w_value, D ** (-0.5), max(D, KV * HD), polar_kv[1])
    new_out = updated(w_out, 32 ** (-0.5), max(H * HD, D), whole_rows(3 * ff_cols + head_cols, head_cols))
    new_gate = updated(w_gate, D ** (-0.5), max(D, FF), whole_rows(0, ff_cols))
    new_up = updated(w_up, D ** (-0.5), max(D, FF), whole_rows(ff_cols, ff_cols))
    new_down = updated(w_down, FF ** (-0.5), max(FF, D), whole_rows(2 * ff_cols, ff_cols).T)
    return (
        block_out,
        input_grad,
        gain_grad,
        moment_one,
        moment_two,
        gains_new,
        grad_query,
        new_m_query,
        new_query,
        grad_key,
        new_m_key,
        new_key,
        grad_value,
        new_m_value,
        new_value,
        grad_out,
        new_m_out,
        new_out,
        grad_gate,
        new_m_gate,
        new_gate,
        grad_up,
        new_m_up,
        new_up,
        grad_down,
        new_m_down,
        new_down,
    )


def solution(mesh):
    n_ctx, n_fsdp = mesh.shape["ctx"], mesh.shape["fsdp"]
    n_lo = 2 * n_ctx // KV // 2
    n_planes = n_fsdp // 2
    finer = Mesh(
        mesh.devices.reshape(n_ctx // n_lo, n_lo, n_planes // n_lo, n_lo, 2),
        CTX + PLANES + ("core",),
    )
    fsdp = PLANES + ("core",)
    tokens, whole = P(fsdp, CTX, None), P()
    rows, columns = P(fsdp, None), P(None, fsdp)
    row_block, column_block = P(fsdp, CTX), P(CTX, fsdp)
    matrix, transposed = (row_block, row_block, rows), (column_block, column_block, columns)
    return jax.shard_map(
        body,
        mesh=finer,
        in_specs=(tokens, tokens, whole, whole, whole)
        + (rows, columns, columns, rows, rows, rows, columns)
        + (row_block, column_block, column_block, row_block, row_block, row_block, column_block),
        out_specs=(tokens, tokens, whole, whole, whole, whole)
        + matrix
        + transposed
        + transposed
        + matrix
        + matrix
        + matrix
        + transposed,
        check_vma=False,
    )
```

```python
import functools
import math

import jax
import jax.numpy as jnp
from jax import lax
from jax.experimental import pallas as pl
from jax.experimental.pallas import tpu as pltpu
from jax.sharding import Mesh
from jax.sharding import PartitionSpec as P

D = 2048
H = 32
KV = 4
HD = 64
FF = 5632
NS = 5
STEP = 10


norm_eps = 1e-05
rope_base = 10000.0
masked_score = -1e30
poly_first = 3.4445
poly_second = -4.775
poly_third = 2.0315
momentum_decay = 0.95
muon_rate = 0.3
weight_decay = 0.1
adam_first = 0.9
adam_second = 0.95
adam_rate = 0.4
adam_eps = 1e-08

MESH = pl.DeviceIdType.MESH
CTX = ("ctx_hi", "ctx_lo")
PLANES = ("z_hi", "z_lo")


def rope_tables(positions, head_width):
    frequency = jnp.exp(
        jnp.arange(head_width // 2, dtype=jnp.float32) * (-2.0 * math.log(rope_base) / head_width)
    )
    angles = positions[:, None] * frequency[None, :]
    cos_half = jnp.cos(angles)
    sin_half = jnp.sin(angles)
    return (jnp.concatenate([cos_half, cos_half], -1), jnp.concatenate([sin_half, sin_half], -1))


def turn(values):
    half_width = values.shape[-1] // 2
    return jnp.concatenate([-values[..., half_width:], values[..., :half_width]], -1)


def norm_forward(values, gain_row):
    inverse = lax.rsqrt(jnp.mean(values * values, -1, keepdims=True) + norm_eps)
    return (values * inverse * gain_row, inverse)


def norm_backward(values, inverse, gain_row, gradients):
    scaled = gradients * gain_row
    inner_mean = jnp.mean(scaled * values, -1, keepdims=True)
    return (
        inverse * scaled - values * inverse**3 * inner_mean,
        jnp.sum(gradients * values * inverse, 0),
    )


def matmul(first_op, second_op):
    return jnp.dot(first_op, second_op, preferred_element_type=jnp.float32)


def contract_rows(first_op, second_op):
    return lax.dot_general(
        first_op, second_op, (((0,), (0,)), ((), ())), preferred_element_type=jnp.float32
    )


def contract_cols(first_op, second_op):
    return lax.dot_general(
        first_op, second_op, (((1,), (1,)), ((), ())), preferred_element_type=jnp.float32
    )


def low(values):
    return values.astype(jnp.bfloat16)


class Exchange:
    def __init__(self, shape, sems, half=0, halved=False):
        self.n_ctx, self.n_lo = shape
        self.stages = self.n_ctx.bit_length() - 1
        self.ranks = 2 * self.n_ctx
        self.half, self.halved = half, halved
        self.ctx = lax.axis_index("ctx_hi") * self.n_lo + lax.axis_index("ctx_lo")
        self.core = lax.axis_index("core")
        self.other_core = {"core": 1 - self.core}
        turned = self.core * (1 - half)
        self.deltas = []
        for s in range(1, self.stages + 1):
            step = turned * 2 ** (self.stages - s) + (1 - turned) * 2 ** (s - 1)
            self.deltas.append(step * (1 - 2 * ((self.ctx // step) % 2)))
        (
            self.core_out,
            self.core_in,
            self.ctx_out,
            self.ctx_in,
            self.back_core_out,
            self.back_core_in,
            self.back_out,
            self.back_in,
        ) = sems

    def partner(self, s):
        there = self.ctx + self.deltas[s - 1]
        return {"ctx_hi": there // self.n_lo, "ctx_lo": there % self.n_lo}

    def place(self, other, idx):
        where = self.ctx
        for s in range(1, self.stages + 1):
            where = where + ((idx // 2 ** (self.stages - s)) % 2) * self.deltas[s - 1]
        return 2 * where + self.core + other * (1 - 2 * self.core)

    def across(self, idx):
        mirrored = 0
        for s in range(self.stages):
            mirrored = mirrored + ((idx // 2**s) % 2) * 2 ** (self.stages - 1 - s)
        return self.half * idx + (1 - self.half) * mirrored

    def whole(self, flag, run):
        if self.halved:
            pl.when(self.half == flag)(run)
        elif flag == 0:
            run()

    def greet(self):
        barrier = pltpu.get_barrier_semaphore()
        pl.semaphore_signal(barrier, inc=1, device_id=self.other_core, device_id_type=MESH)
        for s in range(1, self.stages + 1):
            pl.semaphore_signal(barrier, inc=1, device_id=self.partner(s), device_id_type=MESH)
        pl.semaphore_wait(barrier, 1 + self.stages)

    def copy(self, source, target, send, receive, device):
        return pltpu.make_async_remote_copy(
            src_ref=source,
            dst_ref=target,
            send_sem=send,
            recv_sem=receive,
            device_id=device,
            device_id_type=MESH,
        )


    def core_copy(self, idx):
        slot = self.across(idx)
        return self.copy(
            self.part.at[1, idx], self.from_core.at[slot], self.core_out.at[idx], self.core_in.at[slot], self.other_core
        )

    def core_arrived(self, idx):
        self.copy(
            self.part.at[1, idx], self.from_core.at[idx], self.core_out.at[idx], self.core_in.at[idx], self.other_core
        ).wait_recv()

    def ctx_copy(self, s, idx):
        return self.copy(
            self.part.at[0, idx], self.from_ctx.at[idx], self.ctx_out.at[idx], self.ctx_in.at[idx], self.partner(s)
        )

    def incoming(self, s, idx):
        return idx + 2 ** (self.stages - s)

    def add(self, idx, sources, target):
        def one(chunk, carry):
            total = self.part[0, idx, chunk].astype(jnp.float32)
            total = total + self.from_core[idx, chunk].astype(jnp.float32)
            for source in sources:
                total = total + self.from_ctx[source, chunk].astype(jnp.float32)
            target[chunk] = total.astype(target.dtype)
            return carry

        lax.fori_loop(0, self.part.shape[2], one, 0)

    def sum_pieces(self, part, from_core, from_ctx, make, target):
        self.part, self.from_core, self.from_ctx = part, from_core, from_ctx
        n_ctx, stages = self.n_ctx, self.stages

        def fill(step, carry):
            other = 1 - step // n_ctx
            idx = other * (step % n_ctx) + (1 - other) * (n_ctx - 1 - step % n_ctx)
            make(other, idx)
            pl.when(step < n_ctx)(lambda: self.core_copy(idx).start())
            return carry

        lax.fori_loop(0, 2 * n_ctx, fill, 0)
        for s in range(1, stages + 1):
            upper = 2 ** (stages - s)
            for idx in range(2 * upper - 1, upper - 1, -1):
                self.core_arrived(idx)
                for t in range(1, s):
                    self.ctx_copy(t, self.incoming(t, idx)).wait_recv()
                self.add(idx, [self.incoming(t, idx) for t in range(1, s)], part.at[0, idx])
                if s < stages:
                    self.ctx_copy(s, idx).start()
                else:
                    self.whole(0, lambda s=s, idx=idx: self.ctx_copy(s, idx).start())
        self.core_arrived(0)
        for t in range(1, stages):
            self.ctx_copy(t, self.incoming(t, 0)).wait_recv()
        early = [self.incoming(t, 0) for t in range(1, stages)]

        def finish_whole():
            self.ctx_copy(stages, 1).wait_recv()
            self.add(0, early + [1], target)

        self.whole(0, finish_whole)
        self.whole(1, lambda: self.add(0, early, target))

    def sums_sent(self):
        for idx in range(self.n_ctx):
            self.core_copy(idx).wait_send()
        for s in range(1, self.stages + 1):
            upper = 2 ** (self.stages - s)
            for idx in range(upper, 2 * upper):
                if s < self.stages:
                    self.ctx_copy(s, idx).wait_send()
                else:
                    self.whole(0, lambda s=s, idx=idx: self.ctx_copy(s, idx).wait_send())


    def back_copy(self, s, idx):
        there = idx + 2 ** (self.stages - s)
        block = self.gathered.at[self.place(0, idx)]
        return self.copy(block, block, self.back_out.at[there], self.back_in.at[there], self.partner(s))

    def back_core_copy(self, idx):
        block = self.gathered.at[self.place(0, idx)]
        return self.copy(
            block, block, self.back_core_out.at[idx], self.back_core_in.at[self.across(idx)], self.other_core
        )

    def announce(self, idx):
        for s in range(self.stages, 0, -1):
            if idx < 2 ** (self.stages - s):
                if s < self.stages:
                    self.back_copy(s, idx).start()
                else:
                    self.whole(0, lambda s=s: self.back_copy(s, idx).start())
        self.back_core_copy(idx).start()

    def arrived(self, idx):
        block = self.gathered.at[self.place(0, idx)]
        self.copy(block, block, self.back_out.at[idx], self.back_in.at[idx], self.other_core).wait_recv()

    def core_back_arrived(self, idx):
        block = self.gathered.at[self.place(1, idx)]
        self.copy(block, block, self.back_core_out.at[idx], self.back_core_in.at[idx], self.other_core).wait_recv()

    def gather_pieces(self, gathered, use):
        self.gathered = gathered
        self.announce(0)

        def visit(step, carry):
            idx, other = step // 2, step % 2

            def on_arrival(v):
                if v == 1:
                    self.whole(0, lambda: self.arrived(1))
                else:
                    self.arrived(v)
                self.announce(v)

            for v in range(1, self.n_ctx):
                pl.when(step == 2 * v)(functools.partial(on_arrival, v))
            idx = (1 - other) * idx + other * self.across(idx)
            pl.when(other == 1)(lambda: self.core_back_arrived(idx))
            use(self.place(other, idx))
            return carry

        lax.fori_loop(0, 2 * self.n_ctx, visit, 0)

    def gathers_sent(self):
        for idx in range(self.n_ctx):
            self.back_core_copy(idx).wait_send()
        for s in range(1, self.stages + 1):
            for idx in range(2 ** (self.stages - s)):
                if s < self.stages:
                    self.back_copy(s, idx).wait_send()
                else:
                    self.whole(0, lambda s=s, idx=idx: self.back_copy(s, idx).wait_send())


def exchange_sems(n_ctx):
    return [pltpu.SemaphoreType.DMA((n_ctx,))] * 8


def muon_kernel(
    shape,
    slots_ref,
    pair_ref,
    earlier_ref,
    earlier_too_ref,
    out_ref,
    x_ref,
    y_ref,
    a_ref,
    part,
    from_core,
    from_ctx,
    gathered,
    landed,
    scale,
    slots_out,
    pair_out,
    blocks_in,
    rows_out,
    rows_in,
    spread_out,
    spread_in,
    kept,
    *sems,
):
    del earlier_ref, earlier_too_ref
    n_ctx, n_lo, n_planes, z_lo, halved = shape
    plane = lax.axis_index("z_hi") * z_lo + lax.axis_index("z_lo")
    ex = Exchange((n_ctx, n_lo), sems, plane // (n_planes - 1) if halved else 0, halved)
    even = Exchange((n_ctx, n_lo), sems)
    ctx, core = ex.ctx, ex.core
    own = 2 * plane + core
    shards = 2 * n_planes
    tall = D // shards
    blocks = ex.ranks
    side = D // blocks
    reach = blocks // 2 + 1
    devices = n_ctx * shards

    def device(at_ctx, at_plane, at_core):
        return {
            "ctx_hi": at_ctx // n_lo,
            "ctx_lo": at_ctx % n_lo,
            "z_hi": at_plane // z_lo,
            "z_lo": at_plane % z_lo,
            "core": at_core,
        }

    x_ref[...] = jnp.zeros(x_ref.shape, x_ref.dtype)
    barrier = pltpu.get_barrier_semaphore()
    here = ctx * shards + own

    def greet(offset, carry):
        there = (here + offset) % devices
        shard = there % shards
        pl.semaphore_signal(
            barrier, inc=1, device_id=device(there // shards, shard // 2, shard % 2), device_id_type=MESH
        )
        return carry

    lax.fori_loop(1, devices, greet, 0)
    pl.semaphore_wait(barrier, devices - 1)

    def rows_of(block):
        return pl.ds(pl.multiple_of(block * side, side), side)

    def shard_rows(shard):
        return pl.ds(pl.multiple_of(shard * tall, tall), tall)

    def send(source, target, out_sem, in_sem, at_ctx, at_plane, at_core, begin):
        same = (at_ctx * n_planes + at_plane) * 2 + at_core == here
        far = ex.copy(source, target, out_sem, in_sem, device(at_ctx, at_plane, at_core))
        near = pltpu.make_async_copy(source, target, in_sem)

        def other():
            far.start() if begin else far.wait_send()

        def this():
            if begin:
                near.start()

        pl.when(same)(this)
        pl.when(jnp.logical_not(same))(other)

    mains = slots_ref.shape[0]
    pair_columns = pair_ref.shape[2]

    def send_blocks(begin):
        for offset in range(mains):
            for to_core in range(2):
                slot = (plane + offset) % mains
                send(
                    slots_ref.at[slot, to_core],
                    x_ref.at[shard_rows(own), :],
                    slots_out.at[slot, to_core],
                    blocks_in.at[own],
                    ctx,
                    slot,
                    to_core,
                    begin,
                )
        if halved:
            for which in range(2):
                send(
                    pair_ref.at[which],
                    x_ref.at[shard_rows(own), pl.ds(0, pair_columns)],
                    pair_out.at[which],
                    blocks_in.at[own],
                    ctx % (n_ctx // 2) + which * (n_ctx // 2),
                    n_planes - 1,
                    ctx // (n_ctx // 2),
                    begin,
                )

    def wait_blocks(columns):
        def one(shard, carry):
            target = x_ref.at[shard_rows(shard), pl.ds(0, columns)]
            pltpu.make_async_copy(target, target, blocks_in.at[shard]).wait()
            return carry

        lax.fori_loop(0, shards, one, 0)

    send_blocks(True)
    ex.whole(0, lambda: wait_blocks(x_ref.shape[1]))
    ex.whole(1, lambda: wait_blocks(pair_columns))
    send_blocks(False)

    def gram_piece(other, idx):
        block = ex.place(other, idx)
        left = x_ref[rows_of(block), :]
        for offset in range(reach):
            right = x_ref[rows_of((block + offset) % blocks), :]
            part[other, idx, offset] = low(contract_cols(left, right))

    def spread(block):
        for offset in range(reach):
            column = (block + offset) % blocks
            piece = gathered[block, offset]
            a_ref[rows_of(block), rows_of(column)] = piece
            if 0 < offset < reach - 1:
                a_ref[rows_of(column), rows_of(block)] = piece.T

    def sweep_body(sweep, carry):
        ex.sum_pieces(part, from_core, from_ctx, gram_piece, gathered.at[ex.place(0, 0)])

        def second_own():
            def one(offset, inner):
                gathered[ex.place(0, 1), offset] = part[0, 1, offset]
                return inner

            lax.fori_loop(0, reach, one, 0)

        ex.whole(1, second_own)
        ex.gather_pieces(gathered, spread)

        def norm_now():
            def one(block, total):
                rows = lax.broadcasted_iota(jnp.int32, (side, side), 0)
                cols = lax.broadcasted_iota(jnp.int32, (side, side), 1)
                piece = gathered[block, 0].astype(jnp.float32)
                piece = jnp.where(rows == cols, piece, 0.0)
                return total + jnp.sum(jnp.sum(piece, 0, keepdims=True), 1, keepdims=True)

            trace = lax.fori_loop(0, blocks, one, jnp.zeros((1, 1), jnp.float32))
            scale[...] = jnp.broadcast_to(1.0 / (jnp.sqrt(trace) + 1e-07), scale.shape)

        def norm_done():
            scale[...] = jnp.ones(scale.shape, jnp.float32)

        pl.when(sweep == 0)(norm_now)
        pl.when(sweep > 0)(norm_done)
        factor = scale[0:1, 0:1]
        high = 512

        def first_product(step, inner):
            rows = pl.ds(pl.multiple_of(step * high, high), high)
            y_ref[rows, :] = low(matmul(a_ref[rows, :], x_ref[...]) * (factor * factor * factor))
            return inner

        lax.fori_loop(0, D // high, first_product, 0)

        def second_product(step, inner):
            rows = pl.ds(pl.multiple_of(step * high, high), high)
            second = matmul(a_ref[rows, :], y_ref[...])
            x_ref[rows, :] = low(
                (poly_first * factor) * x_ref[rows, :].astype(jnp.float32)
                + poly_second * y_ref[rows, :].astype(jnp.float32)
                + (poly_third * factor * factor) * second
            )
            return inner

        lax.fori_loop(0, D // high, second_product, 0)
        ex.sums_sent()
        ex.gathers_sent()
        return carry

    lax.fori_loop(0, NS, sweep_body, 0)

    def send_rows(begin):
        for offset in range(n_planes):
            to_plane = (plane + offset) % n_planes
            for to_core in range(2):
                shard = 2 * to_plane + to_core
                send(
                    x_ref.at[shard_rows(shard), :],
                    landed.at[ctx, plane, core],
                    rows_out.at[shard],
                    rows_in.at[own],
                    ctx,
                    to_plane,
                    to_core,
                    begin,
                )

    send_rows(True)
    stages = even.stages

    def spread_copy(s, idx, where, shard):
        block = landed.at[where, shard // 2, shard % 2]
        there = idx + 2 ** (stages - s)
        return even.copy(
            block, block, spread_out.at[there, shard], spread_in.at[there, shard], even.partner(s)
        )

    def keep(where, shard, idx):
        place = (where, shard // 2, shard % 2)
        return pltpu.make_async_copy(landed.at[place], out_ref.at[place], kept.at[idx, shard])

    def owner(idx):
        return even.place(0, idx) // 2

    def pass_on(idx, shard):
        block = landed.at[owner(idx), shard // 2, shard % 2]
        if idx == 0:
            pltpu.make_async_copy(block, block, rows_in.at[shard]).wait()
        else:
            pltpu.make_async_copy(block, block, spread_in.at[idx, shard]).wait()
        for s in range(stages, 0, -1):
            if idx < 2 ** (stages - s):
                spread_copy(s, idx, owner(idx), shard).start()
        keep(owner(idx), shard, idx).start()

    def in_order(step):
        return 2 * ((plane + step // 2) % n_planes) + step % 2

    def arrive(step, carry):
        pl.when(step < shards)(lambda: pass_on(0, in_order(step)))
        for idx in range(1, n_ctx):
            lag = idx.bit_length()
            now = step - lag
            pl.when(jnp.logical_and(now >= 0, now < shards))(
                functools.partial(pass_on, idx, in_order(jnp.maximum(now, 0)))
            )
        return carry

    lax.fori_loop(0, shards + stages, arrive, 0)
    send_rows(False)

    def finish(shard, carry):
        for idx in range(n_ctx):
            keep(owner(idx), shard, idx).wait()
            for s in range(stages, 0, -1):
                if idx < 2 ** (stages - s):
                    spread_copy(s, idx, owner(idx), shard).wait_send()
        return carry

    lax.fori_loop(0, shards, finish, 0)


def in_vmem(count):
    return [pl.BlockSpec(memory_space=pltpu.VMEM)] * count


def anywhere(count):
    return [pl.BlockSpec(memory_space=pl.ANY)] * count


def cost(flops, micros):
    return pl.CostEstimate(flops=flops, bytes_accessed=int(micros * 3.0e6), transcendentals=0)


def muon(slots, pair, earlier, earlier_too, shape):
    n_ctx, _, n_planes, _, halved = shape
    rows_here, columns = slots.shape[2:]
    blocks = 2 * n_ctx
    side = D // blocks
    piece = (blocks // 2 + 1, side, side)
    dma = pltpu.SemaphoreType.DMA
    landed = (n_ctx, n_planes, 2, rows_here, columns)
    return pl.pallas_call(
        functools.partial(muon_kernel, shape),
        out_shape=jax.ShapeDtypeStruct(landed, jnp.bfloat16),
        in_specs=anywhere(4),
        out_specs=pl.BlockSpec(memory_space=pl.ANY),
        scratch_shapes=[
            pltpu.VMEM((D, columns), jnp.bfloat16),
            pltpu.VMEM((D, columns), jnp.bfloat16),
            pltpu.VMEM((D, D), jnp.bfloat16),
            pltpu.VMEM((2, n_ctx) + piece, jnp.bfloat16),
            pltpu.VMEM((n_ctx,) + piece, jnp.bfloat16),
            pltpu.VMEM((n_ctx,) + piece, jnp.bfloat16),
            pltpu.VMEM((blocks,) + piece, jnp.bfloat16),
            pltpu.VMEM(landed, jnp.bfloat16),
            pltpu.VMEM((8, 128), jnp.float32),
            dma((slots.shape[0], 2)),
            dma((2,)),
            dma((2 * n_planes,)),
            dma((2 * n_planes,)),
            dma((2 * n_planes,)),
            dma((n_ctx, 2 * n_planes)),
            dma((n_ctx, 2 * n_planes)),
            dma((n_ctx, 2 * n_planes)),
        ]
        + exchange_sems(n_ctx),
        compiler_params=pltpu.CompilerParams(
            collective_id=0, has_side_effects=True, vmem_limit_bytes=60 * 2**20
        ),
        cost_estimate=cost(NS * 5 * D * D * columns, 350),
        name="muon",
    )(slots, pair, earlier, earlier_too)


def update_kernel(step, columns, first, flipped, weight_ref, *refs):
    parts, out_ref = refs[:-1], refs[-1]
    direction = parts[0][...].reshape(parts[0].shape[-2:])[:, :first]
    if len(parts) > 1:
        second = parts[1][...].reshape(parts[1].shape[-2:])[:, : columns - first]
        direction = jnp.concatenate([direction, second], 1)
    direction = direction.astype(jnp.float32)
    if flipped:
        direction = direction.T
    out_ref[...] = weight_ref[...] * (1.0 - muon_rate * weight_decay) - step * direction


def update(weight, polar, step, columns, first, flipped, place):
    tall, wide = polar.shape[-2:]
    count = weight.shape[0 if flipped else 1] // columns
    if flipped:
        block = pl.BlockSpec((columns, tall), lambda chip: (chip, 0))
    else:
        block = pl.BlockSpec((tall, columns), lambda chip: (0, chip))
    parts = [
        pl.BlockSpec((1, 1, 1, tall, wide), lambda chip, part=part: tuple(place(chip, part)) + (0, 0))
        for part in range(1 if first == columns else 2)
    ]
    return pl.pallas_call(
        functools.partial(update_kernel, step, columns, first, flipped),
        grid=(count,),
        out_shape=jax.ShapeDtypeStruct(weight.shape, jnp.float32),
        in_specs=[block] + parts,
        out_specs=block,
        compiler_params=pltpu.CompilerParams(vmem_limit_bytes=48 * 2**20),
        name="update",
    )(weight, *([polar] * len(parts)))


def scatter_kernel(shape, kinds, n_earlier, *refs):
    count = len(kinds)
    lhs, rhs = refs[:count], refs[count : 2 * count]
    out, part, from_core, from_ctx = refs[2 * count + n_earlier : 2 * count + n_earlier + 4]
    ex = Exchange(shape, refs[2 * count + n_earlier + 4 :])
    ex.greet()
    chunks, tall, wide = out.shape

    def make(other, idx):
        block = ex.place(other, idx)
        start = ((block % 2) * ex.n_ctx + block // 2) * chunks * tall
        rows = pl.ds(pl.multiple_of(start, chunks * tall), chunks * tall)
        total = None
        for left, right, kind in zip(lhs, rhs, kinds):
            term = kind(left[rows, :], right[...])
            total = term if total is None else total + term
        part[other, idx] = low(total).reshape(chunks, tall, wide)

    ex.sum_pieces(part, from_core, from_ctx, make, out)
    ex.sums_sent()


def product_scatter(lhs, rhs, kinds, shape, tokens, collective_id, name, earlier=()):
    n_ctx = shape[0]
    piece = (tokens // 32, 32, D)
    flops = sum(2 * a.shape[0] * a.shape[1] * D for a in lhs)
    out = pl.pallas_call(
        functools.partial(scatter_kernel, shape, kinds, len(earlier)),
        out_shape=jax.ShapeDtypeStruct(piece, jnp.float32),
        in_specs=in_vmem(2 * len(lhs)) + anywhere(len(earlier)),
        out_specs=pl.BlockSpec(memory_space=pltpu.VMEM),
        scratch_shapes=[
            pltpu.VMEM((2, n_ctx) + piece, jnp.bfloat16),
            pltpu.VMEM((n_ctx,) + piece, jnp.bfloat16),
            pltpu.VMEM((n_ctx,) + piece, jnp.bfloat16),
        ]
        + exchange_sems(n_ctx),
        compiler_params=pltpu.CompilerParams(
            collective_id=collective_id, has_side_effects=True, vmem_limit_bytes=56 * 2**20
        ),
        cost_estimate=cost(flops, 40),
        name=name,
    )(*lhs, *rhs, *earlier)
    return out.reshape(tokens, D)


def gather_kernel(shape, finish, n_weights, n_outs, n_earlier, block_ref, *refs):
    weights = refs[:n_weights]
    refs = refs[:n_weights] + refs[n_weights + n_earlier :]
    gathered_out = refs[n_weights]
    outs = refs[n_weights + 1 : n_weights + 1 + n_outs]
    gathered, out_sems = refs[n_weights + 1 + n_outs : n_weights + 3 + n_outs]
    ex = Exchange(shape, refs[n_weights + 3 + n_outs :])
    ex.greet()
    tokens = block_ref.shape[0]
    gathered[ex.place(0, 0)] = block_ref[...]

    def keep(block):
        row = (block % 2) * ex.n_ctx + block // 2
        return pltpu.make_async_copy(gathered.at[block], gathered_out.at[row], out_sems.at[block]), row

    def use(block):
        copy, row = keep(block)
        copy.start()
        rows = pl.ds(pl.multiple_of(row * tokens, tokens), tokens)
        finish(rows, gathered[block], weights, outs)

    ex.gather_pieces(gathered, use)
    ex.gathers_sent()
    for block in range(ex.ranks):
        keep(block)[0].wait()


def gather_product(block, weights, finish, outs, shape, collective_id, name, earlier=()):
    tokens = block.shape[0]
    ranks = 2 * shape[0]
    flops = sum(2 * ranks * tokens * w.shape[0] * w.shape[1] for w in weights)
    result = pl.pallas_call(
        functools.partial(gather_kernel, shape, finish, len(weights), len(outs), len(earlier)),
        out_shape=[jax.ShapeDtypeStruct((ranks, tokens, D), jnp.bfloat16)] + outs,
        in_specs=in_vmem(1 + len(weights)) + anywhere(len(earlier)),
        out_specs=[pl.BlockSpec(memory_space=pl.ANY)] + in_vmem(len(outs)),
        scratch_shapes=[
            pltpu.VMEM((ranks, tokens, D), jnp.bfloat16),
            pltpu.SemaphoreType.DMA((ranks,)),
        ]
        + exchange_sems(shape[0]),
        compiler_params=pltpu.CompilerParams(
            collective_id=collective_id, has_side_effects=True, vmem_limit_bytes=56 * 2**20
        ),
        cost_estimate=cost(flops, 40),
        name=name,
    )(block, *weights, *earlier)
    return [result[0].reshape(ranks * tokens, D)] + list(result[1:])


def finish_nothing(rows, block, weights, outs):
    del rows, block, weights, outs


def finish_hidden(rows, block, weights, outs):
    gate_pre = matmul(block, weights[0][...])
    outs[0][rows, :] = gate_pre
    upper = matmul(block, weights[1][...])
    outs[1][rows, :] = upper
    outs[2][rows, :] = low(gate_pre * jax.nn.sigmoid(gate_pre) * upper)


def finish_mixed(rows, block, weights, outs):
    outs[0][rows, :] = low(contract_cols(block, weights[0][...]))


def all_sum_kernel(shape, x_ref, out_ref, near, far, near_out, near_in, far_out, far_in):
    n_ctx, n_lo, n_planes, z_lo = shape
    ranks = 2 * n_ctx
    core = lax.axis_index("core")
    rank = 2 * (lax.axis_index("ctx_hi") * n_lo + lax.axis_index("ctx_lo")) + core
    plane = lax.axis_index("z_hi") * z_lo + lax.axis_index("z_lo")

    def rank_id(offset):
        there = (rank + offset) % ranks
        return {"ctx_hi": there // 2 // n_lo, "ctx_lo": there // 2 % n_lo, "core": there % 2}

    def plane_id(offset):
        there = (plane + offset) % n_planes
        return {"z_hi": there // z_lo, "z_lo": there % z_lo}

    barrier = pltpu.get_barrier_semaphore()
    for offset in range(1, ranks):
        pl.semaphore_signal(barrier, inc=1, device_id=rank_id(offset), device_id_type=MESH)
    for offset in range(1, n_planes):
        pl.semaphore_signal(barrier, inc=1, device_id=plane_id(offset), device_id_type=MESH)
    pl.semaphore_wait(barrier, ranks + n_planes - 2)

    def exchange(slots, own, count, device, send, receive):
        copies = []
        for offset in range(1, count):
            copies.append(
                pltpu.make_async_remote_copy(
                    src_ref=slots.at[own],
                    dst_ref=slots.at[own],
                    send_sem=send.at[offset],
                    recv_sem=receive.at[own],
                    device_id=device(offset),
                    device_id_type=MESH,
                )
            )
            copies[-1].start()
        for offset in range(1, count):
            there = (own + offset) % count
            pltpu.make_async_remote_copy(
                src_ref=slots.at[there],
                dst_ref=slots.at[there],
                send_sem=send.at[offset],
                recv_sem=receive.at[there],
                device_id=device(offset),
                device_id_type=MESH,
            ).wait_recv()
        total = slots[0]
        for index in range(1, count):
            total = total + slots[index]
        for copy in copies:
            copy.wait_send()
        return total

    near[rank] = x_ref[...]
    far[plane] = exchange(near, rank, ranks, rank_id, near_out, near_in)
    out_ref[...] = exchange(far, plane, n_planes, plane_id, far_out, far_in)


def all_sum(values, shape, collective_id):
    n_ctx, n_lo, n_planes, z_lo = shape
    ranks = 2 * n_ctx
    flat = values.reshape(8, -1)
    dma = pltpu.SemaphoreType.DMA
    out = pl.pallas_call(
        functools.partial(all_sum_kernel, shape),
        out_shape=jax.ShapeDtypeStruct(flat.shape, jnp.float32),
        in_specs=in_vmem(1),
        out_specs=pl.BlockSpec(memory_space=pltpu.VMEM),
        scratch_shapes=[
            pltpu.VMEM((ranks,) + flat.shape, jnp.float32),
            pltpu.VMEM((n_planes,) + flat.shape, jnp.float32),
            dma((ranks,)),
            dma((ranks,)),
            dma((n_planes,)),
            dma((n_planes,)),
        ],
        compiler_params=pltpu.CompilerParams(collective_id=collective_id, has_side_effects=True),
        cost_estimate=cost(0, 8),
        name="all_sum",
    )(flat)
    return out.reshape(values.shape)


def nothing_kernel(*refs):
    del refs


def after(values, *others):
    return pl.pallas_call(
        nothing_kernel,
        out_shape=jax.ShapeDtypeStruct(values.shape, values.dtype),
        in_specs=anywhere(1 + len(others)),
        out_specs=pl.BlockSpec(memory_space=pl.ANY),
        input_output_aliases={0: 0},
        name="after",
    )(values, *others)


def swap_core(values):
    return lax.ppermute(values, "core", [(0, 1), (1, 0)])


def split_cores(values, core):
    mine = jnp.where(core == 0, values[0], values[1])
    theirs = jnp.where(core == 0, values[1], values[0])
    got = swap_core(theirs)
    return jnp.stack([jnp.where(core == 0, mine, got), jnp.where(core == 0, got, mine)])


def causal_blocks(length):
    width = math.gcd(length, 512)
    return [(start, width, start + width) for start in range(0, length, width)]


def visible(start, width, stop):
    return (jnp.arange(stop)[None, :] <= (start + jnp.arange(width))[:, None])[None, None]


def attention_forward(query, keys, values, scale):
    outs, logs = [], []
    for start, width, stop in causal_blocks(query.shape[1]):
        rows = query[:, start:stop]
        scores = jnp.einsum("nthd,nsd->nhts", rows, keys[:, :stop], preferred_element_type=jnp.float32) * scale
        scores = jnp.where(visible(start, width, stop), scores, masked_score)
        top = jnp.max(scores, -1, keepdims=True)
        expo = jnp.exp(scores - top)
        total = jnp.sum(expo, -1, keepdims=True)
        out = jnp.einsum("nhts,nsd->nhtd", low(expo), values[:, :stop], preferred_element_type=jnp.float32)
        outs.append(jnp.transpose(out / total, (0, 2, 1, 3)))
        logs.append((top + jnp.log(total))[..., 0])
    return jnp.concatenate(outs, 1), jnp.concatenate(logs, 2)


def attention_backward(query, keys, values, mixed, logs, d_mixed, scale):
    d_query, d_keys, d_values = [], 0.0, 0.0
    length = query.shape[1]
    for start, width, stop in causal_blocks(length):
        rows, d_rows = query[:, start:stop], d_mixed[:, start:stop]
        scores = jnp.einsum("nthd,nsd->nhts", rows, keys[:, :stop], preferred_element_type=jnp.float32) * scale
        probs = jnp.exp(scores - logs[:, :, start:stop, None])
        probs = jnp.where(visible(start, width, stop), probs, 0.0)
        d_probs = jnp.einsum("nthd,nsd->nhts", d_rows, values[:, :stop], preferred_element_type=jnp.float32)
        delta = jnp.transpose(jnp.sum(d_rows.astype(jnp.float32) * mixed[:, start:stop], -1), (0, 2, 1))
        d_scores = low(probs * (d_probs - delta[..., None]))
        d_query.append(
            jnp.einsum("nhts,nsd->nthd", d_scores, keys[:, :stop], preferred_element_type=jnp.float32) * scale
        )
        more_keys = jnp.einsum("nhts,nthd->nsd", d_scores, rows, preferred_element_type=jnp.float32) * scale
        more_values = jnp.einsum("nhts,nthd->nsd", low(probs), d_rows, preferred_element_type=jnp.float32)
        pad = ((0, 0), (0, length - stop), (0, 0))
        d_keys = d_keys + jnp.pad(more_keys, pad)
        d_values = d_values + jnp.pad(more_values, pad)
    return jnp.concatenate(d_query, 1), d_keys, d_values


def small_newton_schulz(matrices):
    wide = matrices.astype(jnp.float32)
    norm = jnp.sqrt(jnp.sum(wide * wide, (1, 2), keepdims=True))
    current = low(wide / (norm + 1e-07))
    for sweep in range(NS):
        gram = low(jnp.einsum("nij,nkj->nik", current, current, preferred_element_type=jnp.float32))
        first = low(jnp.einsum("nik,nkj->nij", gram, current, preferred_element_type=jnp.float32))
        second = jnp.einsum("nik,nkj->nij", gram, first, preferred_element_type=jnp.float32)
        current = low(
            poly_first * current.astype(jnp.float32) + poly_second * first.astype(jnp.float32) + poly_third * second
        )
    return current


def body(
    inputs,
    cotangent,
    gains,
    gain_moment,
    gain_second,
    w_query,
    w_key,
    w_value,
    w_out,
    w_gate,
    w_up,
    w_down,
    m_query,
    m_key,
    m_value,
    m_out,
    m_gate,
    m_up,
    m_down,
):
    n_ctx = lax.axis_size("ctx_hi") * lax.axis_size("ctx_lo")
    n_lo = lax.axis_size("ctx_lo")
    n_planes = lax.axis_size("z_hi") * lax.axis_size("z_lo")
    ctx, core = lax.axis_index(CTX), lax.axis_index("core")
    plane = lax.axis_index(PLANES)
    halved = n_planes == 4
    ranks = 2 * n_ctx
    tokens = inputs.shape[1]
    length = tokens * n_ctx
    rows_here = w_query.shape[0]
    heads = H // ranks
    sharers = ranks // KV
    head_cols = D // ranks
    chip_ff, chip_model = FF // n_ctx, D // n_ctx
    ff_cols = -(-chip_ff // 256) * 128
    scale = HD ** (-0.5)
    transpose_pairs = [(c * n_planes + z, z * n_planes + c) for c in range(n_ctx) for z in range(n_planes)]

    def transposed(values):
        return lax.ppermute(values, CTX + PLANES, transpose_pairs)

    def for_cores(values, first, padded):
        parts = (values[:, :first], values[:, first:])
        return jnp.stack([jnp.pad(part, ((0, 0), (0, padded - part.shape[1]))) for part in parts])

    def own_columns(weight, columns, first, padded):
        part = lax.dynamic_slice_in_dim(weight, ctx * columns, columns, 1)
        return split_cores(for_cores(low(part), first, padded), core).reshape(2 * rows_here, padded)

    def over_planes(values):
        return lax.all_gather(values, PLANES, axis=0, tiled=True)

    key_value = jnp.stack([low(w_key), low(w_value)], 1)
    key_value = lax.all_gather(key_value, PLANES + ("core",), axis=0, tiled=False)
    own_head = lax.dynamic_slice_in_dim(key_value, (2 * ctx + core) // sharers * sharers, sharers, 0)
    wide_kv = jnp.transpose(own_head, (1, 2, 0, 3)).reshape(D, 2 * HD)
    wide_query = over_planes(own_columns(w_query, chip_model, head_cols, head_cols))
    wide_qkv = jnp.concatenate([wide_query, wide_kv], 1)
    out_part = transposed(low(lax.dynamic_slice_in_dim(w_out, ctx * (D // n_ctx), D // n_ctx, 1)))
    wide_out = lax.all_gather(out_part, PLANES, axis=1, tiled=True)
    wide_gate = over_planes(own_columns(w_gate, chip_ff, ff_cols, ff_cols))
    wide_up = over_planes(own_columns(w_up, chip_ff, ff_cols, ff_cols))

    shape = (n_ctx, n_lo)
    every = 2 * length

    def sum_planes(values, dimension=0):
        return lax.psum_scatter(low(values), PLANES, scatter_dimension=dimension, tiled=True)

    def to_shard(values, columns):
        padded = values.shape[1]
        both = split_cores(values.reshape(2, rows_here, padded), core)
        return jnp.concatenate([both[0], both[1, :, : columns - padded]], 1).astype(jnp.float32)

    cos_table, sin_table = rope_tables(jnp.arange(length, dtype=jnp.float32), HD)
    stream = inputs[0].astype(jnp.float32)
    normed, inverse_one = norm_forward(stream, gains[0])
    all_normed = gather_product(low(normed), [], finish_nothing, [], shape, 1, "gather_normed")[0]
    all_cotangent = gather_product(
        cotangent[0], [], finish_nothing, [], shape, 8, "gather_cotangent", [all_normed]
    )[0]
    wide_down = over_planes(after(own_columns(w_down.T, chip_ff, ff_cols, ff_cols), all_normed))
    projected = matmul(all_normed, wide_qkv).reshape(2, length, heads + 2, HD)
    roped = projected[:, :, : heads + 1]
    roped = low(roped * cos_table[:, None, :] + turn(roped) * sin_table[:, None, :])
    query_rot, key_rot = roped[:, :, :heads], roped[:, :, heads]
    value_low = low(projected[:, :, heads + 1])
    attn_float, logs = attention_forward(query_rot, key_rot, value_low, scale)
    mixed_low = low(attn_float).reshape(2 * length, head_cols)
    middle = stream + product_scatter([mixed_low], [wide_out], [matmul], shape, tokens, 2, "scatter_mixed", [all_cotangent])
    normed_two, inverse_two = norm_forward(middle, gains[1])
    all_two, gate_pre, upper, hidden_low = gather_product(
        low(normed_two),
        [wide_gate, wide_up],
        finish_hidden,
        [jax.ShapeDtypeStruct((every, ff_cols), jnp.float32)] * 2
        + [jax.ShapeDtypeStruct((every, ff_cols), jnp.bfloat16)],
        shape,
        3,
        "gather_hidden",
    )
    sigmoid_gate = jax.nn.sigmoid(gate_pre)
    silu_gate = gate_pre * sigmoid_gate
    part_down = low(contract_rows(all_cotangent, hidden_low))
    sum_down = sum_planes(part_down)
    down_sum = product_scatter(
        [hidden_low], [wide_down], [contract_cols], shape, tokens, 4, "scatter_hidden", [part_down]
    )
    block_out = low(middle + down_sum)[None]

    d_hidden = matmul(all_cotangent, wide_down)
    d_up = low(d_hidden * silu_gate)
    d_gate = low(d_hidden * upper * sigmoid_gate * (1.0 + gate_pre * (1.0 - sigmoid_gate)))
    part_gate = low(contract_rows(all_two, d_gate))
    part_up = low(contract_rows(all_two, d_up))
    sum_gate, sum_up = sum_planes(part_gate), sum_planes(part_up)
    d_normed_two = product_scatter(
        [d_gate, d_up],
        [wide_gate, wide_up],
        [contract_cols] * 2,
        shape,
        tokens,
        5,
        "scatter_d_hidden",
        [part_gate, part_up, down_sum, sum_down],
    )
    d_mid_norm, gain_two = norm_backward(middle, inverse_two, gains[1], d_normed_two)
    d_middle = cotangent[0].astype(jnp.float32) + d_mid_norm
    all_branch, d_mixed = gather_product(
        low(d_middle),
        [wide_out],
        finish_mixed,
        [jax.ShapeDtypeStruct((every, head_cols), jnp.bfloat16)],
        shape,
        6,
        "gather_d_mixed",
        [sum_gate],
    )
    part_out = low(contract_rows(mixed_low, all_branch))
    sum_out = sum_planes(part_out, 1)
    d_mixed = after(d_mixed, part_out).reshape(2, length, heads, HD)
    d_query_rot, d_key_rot, d_value = attention_backward(
        query_rot, key_rot, value_low, attn_float, logs, d_mixed, scale
    )
    d_rot = jnp.concatenate([d_query_rot, d_key_rot[:, :, None]], 2)
    d_rot = d_rot * cos_table[:, None, :] - turn(d_rot) * sin_table[:, None, :]
    d_qkv = low(jnp.concatenate([d_rot, d_value[:, :, None]], 2)).reshape(2 * length, head_cols + 2 * HD)
    part_qkv = low(contract_rows(all_normed, d_qkv))
    sum_kv, sum_query = sum_planes(part_qkv[:, head_cols:]), sum_planes(part_qkv[:, :head_cols])
    d_normed = product_scatter(
        [d_qkv], [wide_qkv], [contract_cols], shape, tokens, 7, "scatter_d_project", [part_qkv, sum_up]
    )
    d_in_norm, gain_one = norm_backward(stream, inverse_one, gains[0], d_normed)
    input_grad = (d_middle + d_in_norm)[None]
    gain_grad = all_sum(jnp.stack([gain_one, gain_two]), shape + (n_planes, n_lo), 9)

    grad_down = to_shard(sum_down, chip_ff)
    grad_gate = to_shard(sum_gate, chip_ff)
    grad_up = to_shard(sum_up, chip_ff)
    grad_out = transposed(sum_out).astype(jnp.float32)
    grad_query = to_shard(sum_query, chip_model)
    grad_kv = transposed(sum_kv).reshape(-1, 2, HD)
    grad_kv = grad_kv.reshape(-1, 2, n_lo, 2, HD // sharers)
    theirs = swap_core(jnp.where(core == 0, grad_kv[:, :, :, 1], grad_kv[:, :, :, 0]))
    mine = jnp.where(core == 0, grad_kv[:, :, :, 0], grad_kv[:, :, :, 1])
    grad_kv = mine.astype(jnp.float32) + theirs.astype(jnp.float32)
    if n_lo > 1:
        grad_kv = lax.psum_scatter(grad_kv, "z_lo", scatter_dimension=2, tiled=True)
    grad_kv = grad_kv[:, :, 0]
    grad_key, grad_value = grad_kv[:, 0], grad_kv[:, 1]

    def momentum(moment, gradient):
        return momentum_decay * moment + gradient

    new_m_query = momentum(m_query, grad_query)
    new_m_key = momentum(m_key, grad_key)
    new_m_value = momentum(m_value, grad_value)
    new_m_out = momentum(m_out, grad_out)
    new_m_gate = momentum(m_gate, grad_gate)
    new_m_up = momentum(m_up, grad_up)
    grad_down = grad_down.T
    new_m_down = momentum(m_down, grad_down)

    moment_one = adam_first * gain_moment + (1.0 - adam_first) * gain_grad
    moment_two = adam_second * gain_second + (1.0 - adam_second) * gain_grad * gain_grad
    adam_ratio = (
        moment_one
        / (1.0 - adam_first**STEP)
        / (jnp.sqrt(moment_two / (1.0 - adam_second**STEP)) + adam_eps)
    )
    gains_new = gains - adam_rate * adam_ratio

    moment_kv = low(jnp.stack([new_m_key.T, new_m_value.T]))
    moment_kv = lax.all_gather(moment_kv, CTX + PLANES + ("core",), axis=0, tiled=False)
    kv_cols = w_key.shape[1]
    moment_kv = moment_kv.reshape(n_ctx, 2 * n_planes, 2, kv_cols, D // n_ctx)
    moment_kv = jnp.transpose(moment_kv, (2, 1, 3, 0, 4)).reshape(2, KV * HD, D)

    slots = [for_cores(low(values), ff_cols, ff_cols) for values in (new_m_gate, new_m_up, new_m_down.T)]
    pair = jnp.stack([low(new_m_query), low(new_m_out)])
    if not halved:
        slots += [for_cores(low(values), chip_model // 2, ff_cols) for values in (new_m_query, new_m_out)]
        slots += [jnp.zeros_like(slots[0])] * (n_planes - len(slots))
    polar = muon(jnp.stack(slots), pair, d_normed, moment_kv, shape + (n_planes, n_lo, halved))

    polar_kv = small_newton_schulz(moment_kv)
    polar_kv = lax.dynamic_slice_in_dim(polar_kv, (2 * plane + core) * kv_cols, kv_cols, 1)
    polar_kv = jnp.transpose(polar_kv, (0, 2, 1)).astype(jnp.float32)
    half_ctx = n_ctx // 2

    def step_of(spread, widest):
        return muon_rate * spread * math.sqrt(widest)

    def updated(weight, spread, widest, direction):
        return weight * (1.0 - muon_rate * weight_decay) - step_of(spread, widest) * direction

    def in_parts(weight, spread, widest, columns, first, flipped, place):
        parts = 1 if first == columns else 2
        if columns % 128 == 0:
            return update(weight, polar, step_of(spread, widest), columns, first, flipped, place)
        chips = []
        for chip in range(n_ctx):
            for part in range(parts):
                width = first if part == 0 else columns - first
                chips.append(polar[place(chip, part)][:, :width])
        direction = jnp.concatenate(chips, 1).astype(jnp.float32)
        return updated(weight, spread, widest, direction.T if flipped else direction)

    def ff_update(weight, spread, slot, flipped=False):
        return in_parts(
            weight, spread, max(D, FF), chip_ff, ff_cols, flipped, lambda chip, part: (chip, slot, part)
        )

    def model_update(weight, spread, which):
        if halved:
            return in_parts(
                weight,
                spread,
                D,
                chip_model,
                chip_model,
                False,
                lambda chip, part: (chip % half_ctx + which * half_ctx, n_planes - 1, chip // half_ctx),
            )
        return in_parts(
            weight, spread, D, chip_model, chip_model // 2, False, lambda chip, part: (chip, 3 + which, part)
        )

    new_query = model_update(w_query, D ** (-0.5), 0)
    new_key = updated(w_key, D ** (-0.5), max(D, KV * HD), polar_kv[0])
    new_value = updated(w_value, D ** (-0.5), max(D, KV * HD), polar_kv[1])
    new_out = model_update(w_out, 32 ** (-0.5), 1)
    new_gate = ff_update(w_gate, D ** (-0.5), 0)
    new_up = ff_update(w_up, D ** (-0.5), 1)
    new_down = ff_update(w_down, FF ** (-0.5), 2, True)
    return (
        block_out,
        input_grad,
        gain_grad,
        moment_one,
        moment_two,
        gains_new,
        grad_query,
        new_m_query,
        new_query,
        grad_key,
        new_m_key,
        new_key,
        grad_value,
        new_m_value,
        new_value,
        grad_out,
        new_m_out,
        new_out,
        grad_gate,
        new_m_gate,
        new_gate,
        grad_up,
        new_m_up,
        new_up,
        grad_down,
        new_m_down,
        new_down,
    )


def solution(mesh):
    n_ctx, n_fsdp = mesh.shape["ctx"], mesh.shape["fsdp"]
    n_lo = 2 * n_ctx // KV // 2
    n_planes = n_fsdp // 2
    finer = Mesh(
        mesh.devices.reshape(n_ctx // n_lo, n_lo, n_planes // n_lo, n_lo, 2),
        CTX + PLANES + ("core",),
    )
    fsdp = PLANES + ("core",)
    tokens, whole = P(fsdp, CTX, None), P()
    rows, columns = P(fsdp, None), P(None, fsdp)
    row_block, column_block = P(fsdp, CTX), P(CTX, fsdp)
    matrix, transposed = (row_block, row_block, rows), (column_block, column_block, columns)
    return jax.shard_map(
        body,
        mesh=finer,
        in_specs=(tokens, tokens, whole, whole, whole)
        + (rows, columns, columns, rows, rows, rows, columns)
        + (row_block, column_block, column_block, row_block, row_block, row_block, column_block),
        out_specs=(tokens, tokens, whole, whole, whole, whole)
        + matrix
        + transposed
        + transposed
        + matrix
        + matrix
        + matrix
        + transposed,
        check_vma=False,
    )
```

```python
import functools
import math

import jax
import jax.numpy as jnp
from jax import lax
from jax.experimental import pallas as pl
from jax.experimental.pallas import tpu as pltpu
from jax.sharding import Mesh
from jax.sharding import PartitionSpec as P

D = 2048
H = 32
KV = 4
HD = 64
FF = 5632
NS = 5
STEP = 10


norm_eps = 1e-05
rope_base = 10000.0
masked_score = -1e30
poly_first = 3.4445
poly_second = -4.775
poly_third = 2.0315
momentum_decay = 0.95
muon_rate = 0.3
weight_decay = 0.1
adam_first = 0.9
adam_second = 0.95
adam_rate = 0.4
adam_eps = 1e-08

MESH = pl.DeviceIdType.MESH
CTX = ("ctx_hi", "ctx_lo")
PLANES = ("z_hi", "z_lo")


def rope_tables(positions, head_width):
    frequency = jnp.exp(
        jnp.arange(head_width // 2, dtype=jnp.float32) * (-2.0 * math.log(rope_base) / head_width)
    )
    angles = positions[:, None] * frequency[None, :]
    cos_half = jnp.cos(angles)
    sin_half = jnp.sin(angles)
    return (jnp.concatenate([cos_half] * 4, -1), jnp.concatenate([-sin_half, sin_half] * 2, -1))


def norm_forward(values, gain_row):
    inverse = lax.rsqrt(jnp.mean(values * values, -1, keepdims=True) + norm_eps)
    return (values * inverse * gain_row, inverse)


def norm_backward(values, inverse, gain_row, gradients):
    scaled = gradients * gain_row
    inner_mean = jnp.mean(scaled * values, -1, keepdims=True)
    return (
        inverse * scaled - values * inverse**3 * inner_mean,
        jnp.sum(gradients * values * inverse, 0),
    )


def matmul(first_op, second_op):
    return jnp.dot(first_op, second_op, preferred_element_type=jnp.float32)


def contract_rows(first_op, second_op):
    return lax.dot_general(
        first_op, second_op, (((0,), (0,)), ((), ())), preferred_element_type=jnp.float32
    )


def contract_cols(first_op, second_op):
    return lax.dot_general(
        first_op, second_op, (((1,), (1,)), ((), ())), preferred_element_type=jnp.float32
    )


def low(values):
    return values.astype(jnp.bfloat16)


class Exchange:
    def __init__(self, shape, sems, half=0, halved=False):
        self.n_ctx, self.n_lo = shape
        self.stages = self.n_ctx.bit_length() - 1
        self.ranks = 2 * self.n_ctx
        self.half, self.halved = half, halved
        self.ctx = lax.axis_index("ctx_hi") * self.n_lo + lax.axis_index("ctx_lo")
        self.core = lax.axis_index("core")
        self.other_core = {"core": 1 - self.core}
        turned = self.core * (1 - half)
        self.deltas = []
        for s in range(1, self.stages + 1):
            step = turned * 2 ** (self.stages - s) + (1 - turned) * 2 ** (s - 1)
            self.deltas.append(step * (1 - 2 * ((self.ctx // step) % 2)))
        (
            self.core_out,
            self.core_in,
            self.ctx_out,
            self.ctx_in,
            self.back_core_out,
            self.back_core_in,
            self.back_out,
            self.back_in,
        ) = sems

    def partner(self, s):
        there = self.ctx + self.deltas[s - 1]
        return {"ctx_hi": there // self.n_lo, "ctx_lo": there % self.n_lo}

    def place(self, other, idx):
        where = self.ctx
        for s in range(1, self.stages + 1):
            where = where + ((idx // 2 ** (self.stages - s)) % 2) * self.deltas[s - 1]
        return 2 * where + self.core + other * (1 - 2 * self.core)

    def across(self, idx):
        mirrored = 0
        for s in range(self.stages):
            mirrored = mirrored + ((idx // 2**s) % 2) * 2 ** (self.stages - 1 - s)
        return self.half * idx + (1 - self.half) * mirrored

    def whole(self, flag, run):
        if self.halved:
            pl.when(self.half == flag)(run)
        elif flag == 0:
            run()

    def greet(self, more=0):
        barrier = pltpu.get_barrier_semaphore()
        pl.semaphore_signal(barrier, inc=1, device_id=self.other_core, device_id_type=MESH)
        for s in range(1, self.stages + 1):
            pl.semaphore_signal(barrier, inc=1, device_id=self.partner(s), device_id_type=MESH)
        pl.semaphore_wait(barrier, 1 + self.stages + more)

    def copy(self, source, target, send, receive, device):
        return pltpu.make_async_remote_copy(
            src_ref=source,
            dst_ref=target,
            send_sem=send,
            recv_sem=receive,
            device_id=device,
            device_id_type=MESH,
        )


    def core_copy(self, idx):
        slot = self.across(idx)
        return self.copy(
            self.part.at[1, idx], self.from_core.at[slot], self.core_out.at[idx], self.core_in.at[slot], self.other_core
        )

    def core_arrived(self, idx):
        self.copy(
            self.part.at[1, idx], self.from_core.at[idx], self.core_out.at[idx], self.core_in.at[idx], self.other_core
        ).wait_recv()

    def ctx_copy(self, s, idx):
        return self.copy(
            self.part.at[0, idx], self.from_ctx.at[idx], self.ctx_out.at[idx], self.ctx_in.at[idx], self.partner(s)
        )

    def incoming(self, s, idx):
        return idx + 2 ** (self.stages - s)

    def add(self, idx, sources, target):
        def one(chunk, carry):
            total = self.part[0, idx, chunk].astype(jnp.float32)
            total = total + self.from_core[idx, chunk].astype(jnp.float32)
            for source in sources:
                total = total + self.from_ctx[source, chunk].astype(jnp.float32)
            target[chunk] = total.astype(target.dtype)
            return carry

        lax.fori_loop(0, self.part.shape[2], one, 0)

    def sum_pieces(self, part, from_core, from_ctx, make, target):
        self.part, self.from_core, self.from_ctx = part, from_core, from_ctx
        n_ctx, stages = self.n_ctx, self.stages

        def pass_on(idx):
            s = stages + 1 - idx.bit_length()
            self.core_arrived(idx)
            for t in range(1, s):
                self.ctx_copy(t, self.incoming(t, idx)).wait_recv()
            self.add(idx, [self.incoming(t, idx) for t in range(1, s)], part.at[0, idx])
            if s < stages:
                self.ctx_copy(s, idx).start()
            else:
                self.whole(0, lambda: self.ctx_copy(s, idx).start())

        def fill(step, carry):
            idx = n_ctx - 1 - step
            theirs = self.across(idx)
            make(1, theirs)
            self.core_copy(theirs).start()
            make(0, idx)
            for early in range(n_ctx // 2, n_ctx):
                pl.when(idx == early)(functools.partial(pass_on, early))
            return carry

        lax.fori_loop(0, n_ctx, fill, 0)
        for idx in range(n_ctx // 2 - 1, 0, -1):
            pass_on(idx)
        self.core_arrived(0)
        for t in range(1, stages):
            self.ctx_copy(t, self.incoming(t, 0)).wait_recv()
        early = [self.incoming(t, 0) for t in range(1, stages)]

        def finish_whole():
            self.ctx_copy(stages, 1).wait_recv()
            self.add(0, early + [1], target)

        self.whole(0, finish_whole)
        self.whole(1, lambda: self.add(0, early, target))

    def sums_sent(self):
        for idx in range(self.n_ctx):
            self.core_copy(idx).wait_send()
        for s in range(1, self.stages + 1):
            upper = 2 ** (self.stages - s)
            for idx in range(upper, 2 * upper):
                if s < self.stages:
                    self.ctx_copy(s, idx).wait_send()
                else:
                    self.whole(0, lambda s=s, idx=idx: self.ctx_copy(s, idx).wait_send())


    def back_copy(self, s, idx):
        there = idx + 2 ** (self.stages - s)
        block = self.gathered.at[self.place(0, idx)]
        return self.copy(block, block, self.back_out.at[there], self.back_in.at[there], self.partner(s))

    def back_core_copy(self, idx):
        block = self.gathered.at[self.place(0, idx)]
        return self.copy(
            block, block, self.back_core_out.at[idx], self.back_core_in.at[self.across(idx)], self.other_core
        )

    def announce(self, idx):
        for s in range(self.stages, 0, -1):
            if idx < 2 ** (self.stages - s):
                if s < self.stages:
                    self.back_copy(s, idx).start()
                else:
                    self.whole(0, lambda s=s: self.back_copy(s, idx).start())
        self.back_core_copy(idx).start()

    def arrived(self, idx):
        block = self.gathered.at[self.place(0, idx)]
        self.copy(block, block, self.back_out.at[idx], self.back_in.at[idx], self.other_core).wait_recv()

    def core_back_arrived(self, idx):
        block = self.gathered.at[self.place(1, idx)]
        self.copy(block, block, self.back_core_out.at[idx], self.back_core_in.at[idx], self.other_core).wait_recv()

    def gather_pieces(self, gathered, use):
        self.gathered = gathered
        self.announce(0)

        def visit(step, carry):
            idx, other = step // 2, step % 2

            def on_arrival(v):
                if v == 1:
                    self.whole(0, lambda: self.arrived(1))
                else:
                    self.arrived(v)
                self.announce(v)

            for v in range(1, self.n_ctx):
                pl.when(step == 2 * v)(functools.partial(on_arrival, v))
            idx = (1 - other) * idx + other * self.across(idx)
            pl.when(other == 1)(lambda: self.core_back_arrived(idx))
            use(self.place(other, idx), step)
            return carry

        lax.fori_loop(0, 2 * self.n_ctx, visit, 0)

    def gathers_sent(self):
        for idx in range(self.n_ctx):
            self.back_core_copy(idx).wait_send()
        for s in range(1, self.stages + 1):
            for idx in range(2 ** (self.stages - s)):
                if s < self.stages:
                    self.back_copy(s, idx).wait_send()
                else:
                    self.whole(0, lambda s=s, idx=idx: self.back_copy(s, idx).wait_send())


def exchange_sems(n_ctx):
    return [pltpu.SemaphoreType.DMA((n_ctx,))] * 8


def muon_kernel(shape, mains, *refs):
    n_ctx, n_lo, n_planes, z_lo, halved, widths = shape
    slot_refs, refs = refs[:mains], refs[mains:]
    pair_ref, gains_ref, out_ref, gains_out_ref = refs[:4]
    x_ref, y_ref, a_ref, part, from_core, from_ctx, both_gathered, landed, scale, strip, near, far = refs[4:16]
    gathered, gathered_beside = both_gathered.at[0], both_gathered.at[1]
    slots_out, pair_out, blocks_in, rows_out, rows_in, spread_out, spread_in, kept = refs[16:24]
    near_out, near_in, far_out, far_in = refs[24:28]
    sems = refs[28:]
    plane = lax.axis_index("z_hi") * z_lo + lax.axis_index("z_lo")
    ex = Exchange((n_ctx, n_lo), sems[:8], plane // (n_planes - 1) if halved else 0, halved)
    ex_beside = Exchange((n_ctx, n_lo), sems[:4] + sems[8:12], ex.half, halved)
    even = Exchange((n_ctx, n_lo), sems[:8])
    ctx, core = ex.ctx, ex.core
    own = 2 * plane + core
    shards = 2 * n_planes
    tall = D // shards
    blocks = ex.ranks
    side = D // blocks
    reach = blocks // 2 + 1
    devices = n_ctx * shards

    def device(at_ctx, at_plane, at_core):
        return {
            "ctx_hi": at_ctx // n_lo,
            "ctx_lo": at_ctx % n_lo,
            "z_hi": at_plane // z_lo,
            "z_lo": at_plane % z_lo,
            "core": at_core,
        }

    least = min(widths) if halved else min(widths[:2])
    if least < x_ref.shape[1]:
        x_ref[:, least:] = jnp.zeros((D, x_ref.shape[1] - least), x_ref.dtype)
    barrier = pltpu.get_barrier_semaphore()
    here = ctx * shards + own

    def greet(offset, carry):
        there = (here + offset) % devices
        shard = there % shards
        pl.semaphore_signal(
            barrier, inc=1, device_id=device(there // shards, shard // 2, shard % 2), device_id_type=MESH
        )
        return carry

    lax.fori_loop(1, devices, greet, 0)
    pl.semaphore_wait(barrier, devices - 1)

    def rows_of(block):
        return pl.ds(pl.multiple_of(block * side, side), side)

    def shard_rows(shard):
        return pl.ds(pl.multiple_of(shard * tall, tall), tall)

    def send(source, target, out_sem, in_sem, at_ctx, at_plane, at_core, begin):
        same = (at_ctx * n_planes + at_plane) * 2 + at_core == here
        far = ex.copy(source, target, out_sem, in_sem, device(at_ctx, at_plane, at_core))
        near = pltpu.make_async_copy(source, target, in_sem)

        def other():
            far.start() if begin else far.wait_send()

        def this():
            if begin:
                near.start()

        pl.when(same)(this)
        pl.when(jnp.logical_not(same))(other)

    def by_width(pair, at_core, run):
        if halved:
            pl.when(pair == 1)(lambda: run(widths[2]))
        for which in range(2):
            pl.when(jnp.logical_and(pair == 0, at_core == which))(functools.partial(run, widths[which]))

    def send_pair(begin):
        for which in range(2):
            send(
                pair_ref.at[which],
                x_ref.at[shard_rows(own), pl.ds(0, widths[2])],
                pair_out.at[which],
                blocks_in.at[own],
                ctx % (n_ctx // 2) + which * (n_ctx // 2),
                n_planes - 1,
                ctx // (n_ctx // 2),
                begin,
            )

    def send_blocks(begin):
        for slot in range(mains):
            for to_core in range(2):
                columns = pl.ds(0, widths[to_core])
                send(
                    slot_refs[slot].at[to_core, :, columns],
                    x_ref.at[shard_rows(own), columns],
                    slots_out.at[slot, to_core],
                    blocks_in.at[own],
                    ctx,
                    slot,
                    to_core,
                    begin,
                )

    def wait_blocks(columns):
        def one(shard, carry):
            target = x_ref.at[shard_rows(shard), pl.ds(0, columns)]
            pltpu.make_async_copy(target, target, blocks_in.at[shard]).wait()
            return carry

        lax.fori_loop(0, shards, one, 0)

    gains = AllSum(ex, n_planes, z_lo, near, far, near_out, near_in, far_out, far_in)
    if halved:
        send_pair(True)
        send_pair(False)
    send_blocks(True)
    gains.begin(gains_ref[...])
    by_width(ex.half, core, wait_blocks)
    send_blocks(False)

    def gram_piece(other, idx):
        block = ex.place(other, idx)
        left = x_ref[rows_of(block), :]
        for offset in range(reach):
            right = x_ref[rows_of((block + offset) % blocks), :]
            part[other, idx, offset] = low(contract_cols(left, right))

    def spread(block, step, pieces=gathered):
        del step
        for offset in range(reach):
            column = (block + offset) % blocks
            piece = pieces[block, offset]
            a_ref[rows_of(block), rows_of(column)] = piece
            if 0 < offset < reach - 1:
                a_ref[rows_of(column), rows_of(block)] = piece.T

    def gram():
        ex.sum_pieces(part, from_core, from_ctx, gram_piece, gathered.at[ex.place(0, 0)])

        def second_own():
            def one(offset, inner):
                gathered[ex.place(0, 1), offset] = part[0, 1, offset]
                return inner

            lax.fori_loop(0, reach, one, 0)

        ex.whole(1, second_own)
        ex.gather_pieces(gathered, spread)
        ex.sums_sent()
        ex.gathers_sent()

    high = 512
    halfway = D // high

    def update_step(step):
        factor = scale[0:1, 0:1]

        def first_product():
            rows = pl.ds(pl.multiple_of(step * high, high), high)
            y_ref[rows, :] = low(matmul(a_ref[rows, :], x_ref[...]) * (factor * factor * factor))

        def second_product():
            rows = pl.ds(pl.multiple_of((step - halfway) * high, high), high)
            second = matmul(a_ref[rows, :], y_ref[...])
            x_ref[rows, :] = low(
                (poly_first * factor) * x_ref[rows, :].astype(jnp.float32)
                + poly_second * y_ref[rows, :].astype(jnp.float32)
                + (poly_third * factor * factor) * second
            )

        pl.when(step < halfway)(first_product)
        pl.when(jnp.logical_and(step >= halfway, step < 2 * halfway))(second_product)

    def update_all():
        def one(step, carry):
            update_step(step)
            return carry

        lax.fori_loop(0, 2 * halfway, one, 0)

    def norm_now():
        def one(block, total):
            rows = lax.broadcasted_iota(jnp.int32, (side, side), 0)
            cols = lax.broadcasted_iota(jnp.int32, (side, side), 1)
            piece = gathered[block, 0].astype(jnp.float32)
            piece = jnp.where(rows == cols, piece, 0.0)
            return total + jnp.sum(jnp.sum(piece, 0, keepdims=True), 1, keepdims=True)

        trace = lax.fori_loop(0, blocks, one, jnp.zeros((1, 1), jnp.float32))
        scale[...] = jnp.broadcast_to(1.0 / (jnp.sqrt(trace) + 1e-07), scale.shape)

    def norm_done():
        scale[...] = jnp.ones(scale.shape, jnp.float32)

    def next_gram_rows(block):
        factor = scale[0:1, 0:1] * scale[0:1, 0:1]
        wide = 512

        def product(source, target, finish):
            def one(step, carry):
                columns = pl.ds(pl.multiple_of(step * wide, wide), wide)
                strip[target, :, columns] = low(finish(matmul(source(), a_ref[:, columns]), columns))
                return carry

            lax.fori_loop(0, D // wide, one, 0)

        def own_rows(columns=slice(None)):
            return a_ref[rows_of(block), columns]

        product(own_rows, 0, lambda value, columns: value * (factor * factor))
        product(
            lambda: strip[0],
            1,
            lambda value, columns: (poly_first * factor) * own_rows(columns).astype(jnp.float32)
            + poly_second * strip[0, :, columns].astype(jnp.float32)
            + (poly_third * factor) * value,
        )
        product(lambda: strip[1], 0, lambda value, columns: value * factor)

        def last(offset, carry):
            columns = rows_of((block + offset) % blocks)
            value = matmul(strip[0], a_ref[:, columns])
            gathered_beside[block, offset] = low(
                poly_first * strip[1, :, columns].astype(jnp.float32)
                + poly_second * strip[0, :, columns].astype(jnp.float32)
                + (poly_third * factor) * value
            )
            return carry

        lax.fori_loop(0, reach, last, 0)

    def two_sweeps(pair, carry):
        gram()
        pl.when(pair == 0)(norm_now)
        pl.when(pair == 0)(gains.between)
        pl.when(pair > 0)(norm_done)
        next_gram_rows(ex.place(0, 0))

        def update_beside(block, step):
            del block
            pl.when(step == 0)(lambda: ex.whole(1, lambda: next_gram_rows(ex.place(0, 1))))
            update_step(step)

        ex_beside.gather_pieces(gathered_beside, update_beside)
        norm_done()

        def spread_one(block, inner):
            spread(block, 0, gathered_beside)
            return inner

        lax.fori_loop(0, blocks, spread_one, 0)
        update_all()
        ex_beside.gathers_sent()
        return carry

    lax.fori_loop(0, NS // 2, two_sweeps, 0)
    if NS % 2:
        gram()
        update_all()

    gains_out_ref[...] = gains.end()

    def send_rows(begin):
        def run(width):
            columns = pl.ds(0, width)
            for offset in range(n_planes):
                to_plane = (plane + offset) % n_planes
                for to_core in range(2):
                    shard = 2 * to_plane + to_core
                    send(
                        x_ref.at[shard_rows(shard), columns],
                        landed.at[ctx, plane, core, :, columns],
                        rows_out.at[shard],
                        rows_in.at[own],
                        ctx,
                        to_plane,
                        to_core,
                        begin,
                    )

        by_width(ex.half, core, run)

    def with_width(shard, run):
        by_width(shard // 2 // (n_planes - 1) if halved else 0, shard % 2, run)

    send_rows(True)
    stages = even.stages

    def block_of(where, shard, width):
        return (where, shard // 2, shard % 2, slice(None), pl.ds(0, width))

    def spread_copy(s, idx, where, shard, width):
        block = landed.at[block_of(where, shard, width)]
        there = idx + 2 ** (stages - s)
        return even.copy(
            block, block, spread_out.at[there, shard], spread_in.at[there, shard], even.partner(s)
        )

    def keep(where, shard, idx, width):
        place = block_of(where, shard, width)
        return pltpu.make_async_copy(landed.at[place], out_ref.at[place], kept.at[idx, shard])

    def owner(idx):
        return even.place(0, idx) // 2

    def pass_on(idx, shard):
        def run(width):
            block = landed.at[block_of(owner(idx), shard, width)]
            if idx == 0:
                pltpu.make_async_copy(block, block, rows_in.at[shard]).wait()
            else:
                pltpu.make_async_copy(block, block, spread_in.at[idx, shard]).wait()
            for s in range(stages, 0, -1):
                if idx < 2 ** (stages - s):
                    spread_copy(s, idx, owner(idx), shard, width).start()
            keep(owner(idx), shard, idx, width).start()

        with_width(shard, run)

    rounds = n_planes - 1 if halved else n_planes

    def in_order(step):
        turn_of = step // 2
        last = turn_of // rounds
        return 2 * (last * rounds + (1 - last) * ((plane + turn_of) % rounds)) + step % 2

    def arrive(step, carry):
        pl.when(step < shards)(lambda: pass_on(0, in_order(step)))
        for idx in range(1, n_ctx):
            lag = idx.bit_length()
            now = step - lag
            pl.when(jnp.logical_and(now >= 0, now < shards))(
                functools.partial(pass_on, idx, in_order(jnp.maximum(now, 0)))
            )
        return carry

    lax.fori_loop(0, shards + stages, arrive, 0)
    send_rows(False)

    def finish(shard, carry):
        def run(width):
            for idx in range(n_ctx):
                keep(owner(idx), shard, idx, width).wait()
                for s in range(stages, 0, -1):
                    if idx < 2 ** (stages - s):
                        spread_copy(s, idx, owner(idx), shard, width).wait_send()

        with_width(shard, run)
        return carry

    lax.fori_loop(0, shards, finish, 0)


def in_vmem(count):
    return [pl.BlockSpec(memory_space=pltpu.VMEM)] * count


def anywhere(count):
    return [pl.BlockSpec(memory_space=pl.ANY)] * count


def cost(flops, micros):
    return pl.CostEstimate(flops=flops, bytes_accessed=int(micros * 3.0e6), transcendentals=0)


def muon(slots, pair, gains, shape):
    n_ctx, _, n_planes = shape[:3]
    rows_here, columns = slots[0].shape[1:]
    blocks = 2 * n_ctx
    side = D // blocks
    piece = (blocks // 2 + 1, side, side)
    dma = pltpu.SemaphoreType.DMA
    landed = (n_ctx, n_planes, 2, rows_here, columns)
    return pl.pallas_call(
        functools.partial(muon_kernel, shape, len(slots)),
        out_shape=[
            jax.ShapeDtypeStruct(landed, jnp.bfloat16),
            jax.ShapeDtypeStruct(gains.shape, jnp.float32),
        ],
        in_specs=anywhere(len(slots) + 1) + in_vmem(1),
        out_specs=anywhere(1) + in_vmem(1),
        scratch_shapes=[
            pltpu.VMEM((D, columns), jnp.bfloat16),
            pltpu.VMEM((D, columns), jnp.bfloat16),
            pltpu.VMEM((D, D), jnp.bfloat16),
            pltpu.VMEM((2, n_ctx) + piece, jnp.bfloat16),
            pltpu.VMEM((n_ctx,) + piece, jnp.bfloat16),
            pltpu.VMEM((n_ctx,) + piece, jnp.bfloat16),
            pltpu.VMEM((2, blocks) + piece, jnp.bfloat16),
            pltpu.VMEM(landed, jnp.bfloat16),
            pltpu.VMEM((8, 128), jnp.float32),
            pltpu.VMEM((2, side, D), jnp.bfloat16),
            pltpu.VMEM((blocks,) + gains.shape, jnp.float32),
            pltpu.VMEM((n_planes,) + gains.shape, jnp.float32),
            dma((len(slots), 2)),
            dma((2,)),
            dma((2 * n_planes,)),
            dma((2 * n_planes,)),
            dma((2 * n_planes,)),
            dma((n_ctx, 2 * n_planes)),
            dma((n_ctx, 2 * n_planes)),
            dma((n_ctx, 2 * n_planes)),
            dma((blocks,)),
            dma((blocks,)),
            dma((n_planes,)),
            dma((n_planes,)),
        ]
        + exchange_sems(n_ctx)
        + [dma((n_ctx,))] * 4,
        compiler_params=pltpu.CompilerParams(
            collective_id=0, has_side_effects=True, vmem_limit_bytes=60 * 2**20
        ),
        cost_estimate=cost(NS * 5 * D * D * columns, 350),
        name="muon",
    )(*slots, pair, gains)


def momentum_kernel(first, flipped, split, sum_ref, got_ref, moment_ref, grad_ref, new_ref, low_ref):
    core = lax.axis_index("core")
    tall = got_ref.shape[0]
    mine = sum_ref[pl.ds(pl.multiple_of(core * tall, tall), tall), :].astype(jnp.float32)
    got = got_ref[...].astype(jnp.float32)
    left = jnp.where(core == 0, mine, got)
    right = jnp.where(core == 0, got, mine)
    columns = moment_ref.shape[0 if flipped else 1]
    gradient = jnp.concatenate([left[:, :first], right[:, : columns - first]], 1)
    if flipped:
        grad_ref[...] = gradient.T
        new = momentum_decay * moment_ref[...] + grad_ref[...]
        new_ref[...] = new
        new = new.T
    else:
        grad_ref[...] = gradient
        new = momentum_decay * moment_ref[...] + gradient
        new_ref[...] = new
    if split:
        padded = low_ref.shape[2]
        for index, part in enumerate((low(new[:, :first]), low(new[:, first:]))):
            if part.shape[1] < padded:
                zeros = jnp.zeros((tall, padded - part.shape[1]), jnp.bfloat16)
                part = jnp.concatenate([part, zeros], 1)
            low_ref[index] = part
    else:
        low_ref[...] = low(new)


def momentum(summed, moment, first, padded, core, flipped=False, split=True):
    tall = summed.shape[0] // 2
    got = swap_core(lax.dynamic_slice_in_dim(summed, (1 - core) * tall, tall, 0))
    columns = moment.shape[0 if flipped else 1]
    out = jax.ShapeDtypeStruct(moment.shape, jnp.float32)
    low_shape = (2, tall, padded) if split else (tall, columns)
    return pl.pallas_call(
        functools.partial(momentum_kernel, first, flipped, split),
        out_shape=[out, out, jax.ShapeDtypeStruct(low_shape, jnp.bfloat16)],
        in_specs=in_vmem(3),
        out_specs=in_vmem(3),
        compiler_params=pltpu.CompilerParams(vmem_limit_bytes=48 * 2**20),
        name="momentum",
    )(summed, got, moment)


def small_kernel(shape, steps, moments_ref, key_ref, value_ref, new_key_ref, new_value_ref, x_ref, y_ref, own_ref):
    n_ctx, shards, z_lo = shape
    columns, wide = moments_ref.shape[2:]
    plane = lax.axis_index("z_hi") * z_lo + lax.axis_index("z_lo")
    own = 2 * plane + lax.axis_index("core")
    for which, (old_ref, new_ref) in enumerate(((key_ref, new_key_ref), (value_ref, new_value_ref))):
        for ctx in range(n_ctx):
            for shard in range(shards):
                x_ref[shard * columns : (shard + 1) * columns, ctx * wide : (ctx + 1) * wide] = moments_ref[
                    ctx * shards + shard, which
                ]
        start = x_ref[...].astype(jnp.float32)
        norm = jnp.sqrt(jnp.sum(jnp.sum(start * start, 0, keepdims=True), 1, keepdims=True))
        x_ref[...] = low(start * (1.0 / (norm + 1e-07)))

        def sweep(index, carry):
            gram = low(contract_cols(x_ref[...], x_ref[...]))
            y_ref[...] = low(matmul(gram, x_ref[...]))
            x_ref[...] = low(
                poly_first * x_ref[...].astype(jnp.float32)
                + poly_second * y_ref[...].astype(jnp.float32)
                + poly_third * matmul(gram, y_ref[...])
            )
            return carry

        lax.fori_loop(0, NS, sweep, 0)
        own_ref[...] = x_ref[pl.ds(pl.multiple_of(own * columns, columns), columns), :].astype(jnp.float32)
        new_ref[...] = old_ref[...] * (1.0 - muon_rate * weight_decay) - steps[which] * own_ref[...]


def small_update(moments, key, value, shape, steps):
    out = jax.ShapeDtypeStruct(key.shape, jnp.float32)
    return pl.pallas_call(
        functools.partial(small_kernel, shape, steps),
        out_shape=[out, out],
        in_specs=in_vmem(3),
        out_specs=in_vmem(2),
        scratch_shapes=[
            pltpu.VMEM((KV * HD, D), jnp.bfloat16),
            pltpu.VMEM((KV * HD, D), jnp.bfloat16),
            pltpu.VMEM(key.shape, jnp.float32),
        ],
        compiler_params=pltpu.CompilerParams(vmem_limit_bytes=48 * 2**20),
        cost_estimate=cost(0, 15),
        name="small_update",
    )(moments, key, value)


def update_kernel(step, columns, first, flipped, weight_ref, *refs):
    parts, out_ref = refs[:-2], refs[-1]
    direction = parts[0][...].reshape(parts[0].shape[-2:])[:, :first]
    if len(parts) > 1:
        second = parts[1][...].reshape(parts[1].shape[-2:])[:, : columns - first]
        direction = jnp.concatenate([direction, second], 1)
    direction = direction.astype(jnp.float32)
    if flipped:
        direction = direction.T
    out_ref[...] = weight_ref[...] * (1.0 - muon_rate * weight_decay) - step * direction


def update(weight, polar, earlier, step, columns, first, flipped, place):
    tall, wide = polar.shape[-2:]
    count = weight.shape[0 if flipped else 1] // columns
    if flipped:
        block = pl.BlockSpec((columns, tall), lambda chip: (chip, 0))
    else:
        block = pl.BlockSpec((tall, columns), lambda chip: (0, chip))
    parts = [
        pl.BlockSpec((1, 1, 1, tall, wide), lambda chip, part=part: tuple(place(chip, part)) + (0, 0))
        for part in range(1 if first == columns else 2)
    ]
    return pl.pallas_call(
        functools.partial(update_kernel, step, columns, first, flipped),
        grid=(count,),
        out_shape=jax.ShapeDtypeStruct(weight.shape, jnp.float32),
        in_specs=[block] + parts + anywhere(1),
        out_specs=block,
        compiler_params=pltpu.CompilerParams(vmem_limit_bytes=48 * 2**20),
        name="update",
    )(weight, *([polar] * len(parts)), earlier)


def scatter_kernel(shape, kinds, n_earlier, *refs):
    count = len(kinds)
    lhs, rhs = refs[:count], refs[count : 2 * count]
    out, part, from_core, from_ctx = refs[2 * count + n_earlier : 2 * count + n_earlier + 4]
    ex = Exchange(shape, refs[2 * count + n_earlier + 4 :])
    ex.greet()
    chunks, tall, wide = out.shape

    def make(other, idx):
        block = ex.place(other, idx)
        start = ((block % 2) * ex.n_ctx + block // 2) * chunks * tall
        rows = pl.ds(pl.multiple_of(start, chunks * tall), chunks * tall)
        total = None
        for left, right, kind in zip(lhs, rhs, kinds):
            term = kind(left[rows, :], right[...])
            total = term if total is None else total + term
        part[other, idx] = low(total).reshape(chunks, tall, wide)

    ex.sum_pieces(part, from_core, from_ctx, make, out)
    ex.sums_sent()


def product_scatter(lhs, rhs, kinds, shape, tokens, collective_id, name, earlier=()):
    n_ctx = shape[0]
    piece = (tokens // 32, 32, D)
    flops = sum(2 * a.shape[0] * a.shape[1] * D for a in lhs)
    out = pl.pallas_call(
        functools.partial(scatter_kernel, shape, kinds, len(earlier)),
        out_shape=jax.ShapeDtypeStruct(piece, jnp.float32),
        in_specs=in_vmem(2 * len(lhs)) + anywhere(len(earlier)),
        out_specs=pl.BlockSpec(memory_space=pltpu.VMEM),
        scratch_shapes=[
            pltpu.VMEM((2, n_ctx) + piece, jnp.bfloat16),
            pltpu.VMEM((n_ctx,) + piece, jnp.bfloat16),
            pltpu.VMEM((n_ctx,) + piece, jnp.bfloat16),
        ]
        + exchange_sems(n_ctx),
        compiler_params=pltpu.CompilerParams(
            collective_id=collective_id, has_side_effects=True, vmem_limit_bytes=56 * 2**20
        ),
        cost_estimate=cost(flops, 40),
        name=name,
    )(*lhs, *rhs, *earlier)
    return out.reshape(tokens, D)


def gather_kernel(shape, finish, n_weights, n_outs, n_earlier, block_ref, *refs):
    weights = refs[:n_weights]
    refs = refs[n_weights + n_earlier :]
    gathered_out, outs = refs[0], refs[1 : 1 + n_outs]
    gathered, out_sems = refs[1 + n_outs : 3 + n_outs]
    ex = Exchange(shape, refs[3 + n_outs :])
    ex.greet()
    tokens = block_ref.shape[0]
    gathered[ex.place(0, 0)] = block_ref[...]

    def keep(block):
        row = (block % 2) * ex.n_ctx + block // 2
        return pltpu.make_async_copy(gathered.at[block], gathered_out.at[row], out_sems.at[block]), row

    def use(block, step):
        del step
        copy, row = keep(block)
        copy.start()
        rows = pl.ds(pl.multiple_of(row * tokens, tokens), tokens)
        finish(rows, gathered[block], weights, outs)

    ex.gather_pieces(gathered, use)
    ex.gathers_sent()
    for block in range(ex.ranks):
        keep(block)[0].wait()


def gather_product(block, weights, finish, outs, shape, collective_id, name, earlier=()):
    tokens = block.shape[0]
    ranks = 2 * shape[0]
    flops = sum(2 * ranks * tokens * w.shape[0] * w.shape[1] for w in weights)
    result = pl.pallas_call(
        functools.partial(gather_kernel, shape, finish, len(weights), len(outs), len(earlier)),
        out_shape=[jax.ShapeDtypeStruct((ranks, tokens, D), jnp.bfloat16)] + outs,
        in_specs=in_vmem(1 + len(weights)) + anywhere(len(earlier)),
        out_specs=anywhere(1) + in_vmem(len(outs)),
        scratch_shapes=[
            pltpu.VMEM((ranks, tokens, D), jnp.bfloat16),
            pltpu.SemaphoreType.DMA((ranks,)),
        ]
        + exchange_sems(shape[0]),
        compiler_params=pltpu.CompilerParams(
            collective_id=collective_id, has_side_effects=True, vmem_limit_bytes=56 * 2**20
        ),
        cost_estimate=cost(flops, 40),
        name=name,
    )(block, *weights, *earlier)
    return [result[0].reshape(ranks * tokens, D)] + list(result[1:])


def finish_nothing(rows, block, weights, outs):
    del rows, block, weights, outs


def finish_hidden(rows, block, weights, outs):
    gate_pre = matmul(block, weights[0][...])
    outs[0][rows, :] = gate_pre
    upper = matmul(block, weights[1][...])
    outs[1][rows, :] = upper
    outs[2][rows, :] = low(gate_pre * jax.nn.sigmoid(gate_pre) * upper)


def finish_mixed(rows, block, weights, outs):
    outs[0][rows, :] = low(contract_cols(block, weights[0][...]))


class AllSum:
    def __init__(self, ex, n_planes, z_lo, near, far, near_out, near_in, far_out, far_in):
        self.ex, self.n_planes, self.z_lo = ex, n_planes, z_lo
        self.near, self.far = near, far
        self.near_sems, self.far_sems = (near_out, near_in), (far_out, far_in)
        self.rank = 2 * ex.ctx + ex.core
        self.plane = lax.axis_index("z_hi") * z_lo + lax.axis_index("z_lo")

    def rank_id(self, offset):
        there = (self.rank + offset) % self.ex.ranks
        n_lo = self.ex.n_lo
        return {"ctx_hi": there // 2 // n_lo, "ctx_lo": there // 2 % n_lo, "core": there % 2}

    def plane_id(self, offset):
        there = (self.plane + offset) % self.n_planes
        return {"z_hi": there // self.z_lo, "z_lo": there % self.z_lo}

    def copies(self, slots, own, count, device, sems):
        return [
            self.ex.copy(slots.at[own], slots.at[own], sems[0].at[offset], sems[1].at[own], device(offset))
            for offset in range(1, count)
        ]

    def total(self, slots, own, count, device, sems):
        for offset in range(1, count):
            there = (own + offset) % count
            block = slots.at[there]
            self.ex.copy(block, block, sems[0].at[offset], sems[1].at[there], device(offset)).wait_recv()
        for copy in self.copies(slots, own, count, device, sems):
            copy.wait_send()
        total = slots[0]
        for index in range(1, count):
            total = total + slots[index]
        return total

    def begin(self, value):
        self.near[self.rank] = value
        for copy in self.copies(self.near, self.rank, self.ex.ranks, self.rank_id, self.near_sems):
            copy.start()

    def between(self):
        self.far[self.plane] = self.total(self.near, self.rank, self.ex.ranks, self.rank_id, self.near_sems)
        for copy in self.copies(self.far, self.plane, self.n_planes, self.plane_id, self.far_sems):
            copy.start()

    def end(self):
        return self.total(self.far, self.plane, self.n_planes, self.plane_id, self.far_sems)


def nothing_kernel(*refs):
    del refs


def after(values, *others):
    return pl.pallas_call(
        nothing_kernel,
        out_shape=jax.ShapeDtypeStruct(values.shape, values.dtype),
        in_specs=anywhere(1 + len(others)),
        out_specs=pl.BlockSpec(memory_space=pl.ANY),
        input_output_aliases={0: 0},
        name="after",
    )(values, *others)


def swap_core(values):
    return lax.ppermute(values, "core", [(0, 1), (1, 0)])


def split_cores(values, core):
    mine = jnp.where(core == 0, values[0], values[1])
    theirs = jnp.where(core == 0, values[1], values[0])
    got = swap_core(theirs)
    return jnp.stack([jnp.where(core == 0, mine, got), jnp.where(core == 0, got, mine)])


QUERY_ROWS = 256


def turned_pair(values):
    lane = lax.broadcasted_iota(jnp.int32, values.shape, 1)
    return jnp.where(lane % HD < HD // 2, pltpu.roll(values, 2 * HD - HD // 2, 1), pltpu.roll(values, HD // 2, 1))


def is_visible(start, stop):
    rows = lax.broadcasted_iota(jnp.int32, (QUERY_ROWS, stop), 0) + start
    return lax.broadcasted_iota(jnp.int32, (QUERY_ROWS, stop), 1) <= rows


def attention_kernel(pairs, steps, normed_ref, w_ref, cos_ref, sin_ref, mixed_ref, q_ref, k_ref, v_ref, log_ref):
    step = pl.program_id(1)
    projected = matmul(normed_ref[...], w_ref[...])
    cos, sin = cos_ref[...], sin_ref[...]
    lane = lax.broadcasted_iota(jnp.int32, (QUERY_ROWS, 2 * HD), 1)
    left = lane < HD

    def pair_of(values, pair):
        return values[:, pair * 2 * HD : (pair + 1) * 2 * HD]

    def rope(values):
        return values * cos + turned_pair(values) * sin

    both = pair_of(projected, pairs)
    keys = rope(both)
    rows = pl.ds(pl.multiple_of(step * QUERY_ROWS, QUERY_ROWS), QUERY_ROWS)
    k_ref[rows, :] = low(jnp.where(left, keys, pltpu.roll(keys, HD, 1)))
    v_ref[rows, :] = low(jnp.where(left, pltpu.roll(both, HD, 1), both))
    for pair in range(pairs):
        q_ref[:, pair * 2 * HD : (pair + 1) * 2 * HD] = low(rope(pair_of(projected, pair)))

    def attend(index):
        stop = (index + 1) * QUERY_ROWS
        seen = is_visible(index * QUERY_ROWS, stop)
        logs = jnp.zeros((QUERY_ROWS, 2 * HD), jnp.float32)
        for pair in range(pairs):
            outs = []
            for half in range(2):
                query = jnp.where(left == (half == 0), pair_of(q_ref[...], pair), 0.0)
                scores = contract_cols(low(query), k_ref[:stop, :]) * HD ** (-0.5)
                scores = jnp.where(seen, scores, masked_score)
                top = jnp.max(scores, -1, keepdims=True)
                expo = jnp.exp(scores - top)
                total = jnp.sum(expo, -1, keepdims=True)
                outs.append(matmul(low(expo), v_ref[:stop, :]) / total)
                logs = jnp.where(lane == 2 * pair + half, top + jnp.log(total), logs)
            mixed_ref[:, pair * 2 * HD : (pair + 1) * 2 * HD] = low(jnp.where(left, outs[0], outs[1]))
        log_ref[...] = logs

    for index in range(steps):
        pl.when(step == index)(functools.partial(attend, index))


def attention(normed, weight, cos, sin, length):
    every, columns = normed.shape[0], weight.shape[1]
    pairs = columns // (2 * HD) - 1
    steps = length // QUERY_ROWS
    pair = 2 * HD

    def rows(width):
        return pl.BlockSpec((QUERY_ROWS, width), lambda n, b: (n * steps + b, 0))

    def sequence():
        return pl.BlockSpec((length, pair), lambda n, b: (n, 0))

    table = pl.BlockSpec((QUERY_ROWS, pair), lambda n, b: (b, 0))
    return pl.pallas_call(
        functools.partial(attention_kernel, pairs, steps),
        grid=(every // length, steps),
        out_shape=[
            jax.ShapeDtypeStruct((every, pairs * pair), jnp.bfloat16),
            jax.ShapeDtypeStruct((every, pairs * pair), jnp.bfloat16),
            jax.ShapeDtypeStruct((every, pair), jnp.bfloat16),
            jax.ShapeDtypeStruct((every, pair), jnp.bfloat16),
            jax.ShapeDtypeStruct((every, pair), jnp.float32),
        ],
        in_specs=[rows(D), pl.BlockSpec((D, columns), lambda n, b: (0, 0)), table, table],
        out_specs=[rows(pairs * pair), rows(pairs * pair), sequence(), sequence(), rows(pair)],
        compiler_params=pltpu.CompilerParams(vmem_limit_bytes=48 * 2**20),
        cost_estimate=cost(0, 25),
        name="attention",
    )(normed, weight, cos, sin)


def attention_back_kernel(
    pairs, steps, q_ref, d_ref, k_ref, v_ref, log_ref, cos_ref, sin_ref, earlier_ref, out_ref, dk_ref, dv_ref
):
    del earlier_ref
    step = pl.program_id(1)
    lane = lax.broadcasted_iota(jnp.int32, (QUERY_ROWS, 2 * HD), 1)
    left = lane < HD

    def clear():
        dk_ref[...] = jnp.zeros(dk_ref.shape, jnp.float32)
        dv_ref[...] = jnp.zeros(dv_ref.shape, jnp.float32)

    pl.when(step == 0)(clear)

    def unrope(values, rows):
        return values * cos_ref[rows, :] - turned_pair(values) * sin_ref[rows, :]

    def attend(index):
        stop = (index + 1) * QUERY_ROWS
        rows = slice(index * QUERY_ROWS, stop)
        seen = is_visible(index * QUERY_ROWS, stop)
        for pair in range(pairs):
            at = slice(pair * 2 * HD, (pair + 1) * 2 * HD)
            parts = []
            for half in range(2):
                mine = left == (half == 0)
                query = low(jnp.where(mine, q_ref[:, at], 0.0))
                d_rows = low(jnp.where(mine, d_ref[:, at], 0.0))
                scores = contract_cols(query, k_ref[:stop, :]) * HD ** (-0.5)
                log = jnp.sum(jnp.where(lane == 2 * pair + half, log_ref[...], 0.0), -1, keepdims=True)
                probs = jnp.where(seen, jnp.exp(scores - log), 0.0)
                d_probs = contract_cols(d_rows, v_ref[:stop, :])
                delta = jnp.sum(probs * d_probs, -1, keepdims=True)
                d_scores = low(probs * (d_probs - delta))
                parts.append(matmul(d_scores, k_ref[:stop, :]) * HD ** (-0.5))
                dk_ref[:stop, :] += contract_rows(d_scores, query) * HD ** (-0.5)
                dv_ref[:stop, :] += contract_rows(low(probs), d_rows)
            out_ref[rows, at] = low(unrope(jnp.where(left, parts[0], parts[1]), rows))

    for index in range(steps):
        pl.when(step == index)(functools.partial(attend, index))

    def finish():
        def fold(chunk, carry):
            rows = pl.ds(pl.multiple_of(chunk * QUERY_ROWS, QUERY_ROWS), QUERY_ROWS)
            d_keys, d_values = dk_ref[rows, :], dv_ref[rows, :]
            d_keys = unrope(d_keys + pltpu.roll(d_keys, HD, 1), rows)
            d_values = d_values + pltpu.roll(d_values, HD, 1)
            out_ref[rows, pairs * 2 * HD :] = low(jnp.where(left, d_keys, d_values))
            return carry

        lax.fori_loop(0, steps, fold, 0)

    pl.when(step == steps - 1)(finish)


def attention_back(query, d_mixed, keys, values, logs, cos, sin, earlier, length):
    every = query.shape[0]
    pair = 2 * HD
    pairs = query.shape[1] // pair
    steps = length // QUERY_ROWS

    def rows(width):
        return pl.BlockSpec((QUERY_ROWS, width), lambda n, b: (n * steps + b, 0))

    def sequence(width):
        return pl.BlockSpec((length, width), lambda n, b: (n, 0))

    table = pl.BlockSpec((length, pair), lambda n, b: (0, 0))
    return pl.pallas_call(
        functools.partial(attention_back_kernel, pairs, steps),
        grid=(every // length, steps),
        out_shape=jax.ShapeDtypeStruct((every, (pairs + 1) * pair), jnp.bfloat16),
        in_specs=[rows(pairs * pair), rows(pairs * pair), sequence(pair), sequence(pair), rows(pair), table, table]
        + anywhere(1),
        out_specs=sequence((pairs + 1) * pair),
        scratch_shapes=[pltpu.VMEM((length, pair), jnp.float32)] * 2,
        compiler_params=pltpu.CompilerParams(vmem_limit_bytes=48 * 2**20),
        cost_estimate=cost(0, 40),
        name="attention_back",
    )(query, d_mixed, keys, values, logs, cos, sin, earlier)


def body(
    inputs,
    cotangent,
    gains,
    gain_moment,
    gain_second,
    w_query,
    w_key,
    w_value,
    w_out,
    w_gate,
    w_up,
    w_down,
    m_query,
    m_key,
    m_value,
    m_out,
    m_gate,
    m_up,
    m_down,
):
    n_ctx = lax.axis_size("ctx_hi") * lax.axis_size("ctx_lo")
    n_lo = lax.axis_size("ctx_lo")
    n_planes = lax.axis_size("z_hi") * lax.axis_size("z_lo")
    ctx, core = lax.axis_index(CTX), lax.axis_index("core")
    plane = lax.axis_index(PLANES)
    halved = n_planes == 4
    ranks = 2 * n_ctx
    tokens = inputs.shape[1]
    length = tokens * n_ctx
    rows_here = w_query.shape[0]
    sharers = ranks // KV
    head_cols = D // ranks
    chip_ff, chip_model = FF // n_ctx, D // n_ctx
    ff_cols = -(-chip_ff // 256) * 128
    transpose_pairs = [(c * n_planes + z, z * n_planes + c) for c in range(n_ctx) for z in range(n_planes)]

    def transposed(values):
        return lax.ppermute(values, CTX + PLANES, transpose_pairs)

    def for_cores(values, first, padded):
        parts = (values[:, :first], values[:, first:])
        return jnp.stack([jnp.pad(part, ((0, 0), (0, padded - part.shape[1]))) for part in parts])

    def own_columns(weight, columns, first, padded):
        part = lax.dynamic_slice_in_dim(weight, ctx * columns, columns, 1)
        return split_cores(for_cores(low(part), first, padded), core).reshape(2 * rows_here, padded)

    def over_planes(values):
        return lax.all_gather(values, PLANES, axis=0, tiled=True)

    key_value = jnp.stack([low(w_key), low(w_value)], 1)
    key_value = lax.all_gather(key_value, PLANES + ("core",), axis=0, tiled=False)
    own_head = lax.dynamic_slice_in_dim(key_value, (2 * ctx + core) // sharers * sharers, sharers, 0)
    wide_kv = jnp.transpose(own_head, (1, 2, 0, 3)).reshape(D, 2 * HD)
    wide_query = over_planes(own_columns(w_query, chip_model, head_cols, head_cols))
    wide_qkv = jnp.concatenate([wide_query, wide_kv], 1)
    out_part = transposed(low(lax.dynamic_slice_in_dim(w_out, ctx * (D // n_ctx), D // n_ctx, 1)))
    wide_out = lax.all_gather(out_part, PLANES, axis=1, tiled=True)
    wide_gate = over_planes(own_columns(w_gate, chip_ff, ff_cols, ff_cols))
    wide_up = over_planes(own_columns(w_up, chip_ff, ff_cols, ff_cols))

    shape = (n_ctx, n_lo)
    every = 2 * length

    def sum_planes(values, dimension=0):
        return lax.psum_scatter(low(values), PLANES, scatter_dimension=dimension, tiled=True)

    cos_table, sin_table = rope_tables(jnp.arange(length, dtype=jnp.float32), HD)
    stream = inputs[0].astype(jnp.float32)
    normed, inverse_one = norm_forward(stream, gains[0])
    all_normed = gather_product(low(normed), [], finish_nothing, [], shape, 1, "gather_normed")[0]
    all_cotangent = gather_product(
        cotangent[0], [], finish_nothing, [], shape, 8, "gather_cotangent", [all_normed]
    )[0]
    wide_down = over_planes(after(own_columns(w_down.T, chip_ff, ff_cols, ff_cols), all_normed))
    mixed_low, query_rot, key_rot, value_low, logs = attention(all_normed, wide_qkv, cos_table, sin_table, length)
    middle = stream + product_scatter([mixed_low], [wide_out], [matmul], shape, tokens, 2, "scatter_mixed", [all_cotangent])
    normed_two, inverse_two = norm_forward(middle, gains[1])
    all_two, gate_pre, upper, hidden_low = gather_product(
        low(normed_two),
        [wide_gate, wide_up],
        finish_hidden,
        [jax.ShapeDtypeStruct((every, ff_cols), jnp.float32)] * 2
        + [jax.ShapeDtypeStruct((every, ff_cols), jnp.bfloat16)],
        shape,
        3,
        "gather_hidden",
    )
    sigmoid_gate = jax.nn.sigmoid(gate_pre)
    silu_gate = gate_pre * sigmoid_gate
    part_down = low(contract_rows(all_cotangent, hidden_low))
    sum_down = sum_planes(part_down)
    down_sum = product_scatter(
        [hidden_low], [wide_down], [contract_cols], shape, tokens, 4, "scatter_hidden", [part_down]
    )
    block_out = low(middle + down_sum)[None]

    d_hidden = matmul(all_cotangent, wide_down)
    d_up = low(d_hidden * silu_gate)
    d_gate = low(d_hidden * upper * sigmoid_gate * (1.0 + gate_pre * (1.0 - sigmoid_gate)))
    part_gate = low(contract_rows(all_two, d_gate))
    part_up = low(contract_rows(all_two, d_up))
    sum_gate, sum_up = sum_planes(part_gate), sum_planes(part_up)
    d_normed_two = product_scatter(
        [d_gate, d_up],
        [wide_gate, wide_up],
        [contract_cols] * 2,
        shape,
        tokens,
        5,
        "scatter_d_hidden",
        [part_gate, part_up, down_sum, sum_down],
    )
    d_mid_norm, gain_two = norm_backward(middle, inverse_two, gains[1], d_normed_two)
    d_middle = cotangent[0].astype(jnp.float32) + d_mid_norm
    widths = (ff_cols, -(-(chip_ff - ff_cols) // 128) * 128, chip_model)
    grad_down, new_m_down, low_down = momentum(sum_down, m_down, ff_cols, ff_cols, core, flipped=True)
    grad_gate, new_m_gate, low_gate = momentum(sum_gate, m_gate, ff_cols, ff_cols, core)
    all_branch, d_mixed = gather_product(
        low(d_middle),
        [wide_out],
        finish_mixed,
        [jax.ShapeDtypeStruct((every, head_cols), jnp.bfloat16)],
        shape,
        6,
        "gather_d_mixed",
        [sum_gate],
    )
    grad_up, new_m_up, low_up = momentum(sum_up, m_up, ff_cols, ff_cols, core)

    part_out = low(contract_rows(all_branch, mixed_low))
    d_qkv = attention_back(
        query_rot, d_mixed, key_rot, value_low, logs, cos_table, sin_table, part_out, length
    )
    part_qkv = low(contract_rows(all_normed, d_qkv))
    part_all = jnp.concatenate([part_qkv[:, :head_cols], part_out, part_qkv[:, head_cols:]], 1)
    sum_all = sum_planes(part_all)
    d_normed = product_scatter(
        [d_qkv], [wide_qkv], [contract_cols], shape, tokens, 7, "scatter_d_project", [part_all, low_up]
    )
    sum_query = sum_all[:, :head_cols]
    grad_rest = transposed(sum_all[:, head_cols:])
    grad_out = grad_rest[:, :head_cols].T.astype(jnp.float32)
    new_m_out = momentum_decay * m_out + grad_out
    slots = [low_gate, low_down, low_up]
    if halved:
        grad_query, new_m_query, low_query = momentum(
            sum_query, m_query, head_cols, head_cols, core, split=False
        )
        pair = jnp.stack([low_query, low(new_m_out)])
    else:
        grad_query, new_m_query, low_query = momentum(sum_query, m_query, head_cols, ff_cols, core)
        slots += [low_query, for_cores(low(new_m_out), head_cols, ff_cols)]
        slots += [jnp.zeros_like(low_gate)] * (n_planes - len(slots))
        pair = jnp.zeros((2, rows_here, chip_model), jnp.bfloat16)
    d_in_norm, gain_one = norm_backward(stream, inverse_one, gains[0], d_normed)
    input_grad = (d_middle + d_in_norm)[None]

    grad_kv = grad_rest[:, head_cols:]
    grad_kv = grad_kv.reshape(-1, 2, n_lo, 2, HD // sharers)
    theirs = swap_core(jnp.where(core == 0, grad_kv[:, :, :, 1], grad_kv[:, :, :, 0]))
    mine = jnp.where(core == 0, grad_kv[:, :, :, 0], grad_kv[:, :, :, 1])
    grad_kv = mine.astype(jnp.float32) + theirs.astype(jnp.float32)
    if n_lo > 1:
        grad_kv = lax.psum_scatter(grad_kv, "z_lo", scatter_dimension=2, tiled=True)
    grad_kv = grad_kv[:, :, 0]
    grad_key, grad_value = grad_kv[:, 0], grad_kv[:, 1]
    new_m_key = momentum_decay * m_key + grad_key
    new_m_value = momentum_decay * m_value + grad_value

    moment_kv = low(jnp.stack([new_m_key.T, new_m_value.T]))
    moment_kv = lax.all_gather(moment_kv, CTX + PLANES + ("core",), axis=0, tiled=False)
    gains_here = jnp.stack([gain_one, gain_two]).reshape(8, -1)
    polar, gain_grad = muon(slots, pair, gains_here, shape + (n_planes, n_lo, halved, widths))
    gain_grad = gain_grad.reshape(gains.shape)
    moment_one = adam_first * gain_moment + (1.0 - adam_first) * gain_grad
    moment_two = adam_second * gain_second + (1.0 - adam_second) * gain_grad * gain_grad
    adam_ratio = (
        moment_one
        / (1.0 - adam_first**STEP)
        / (jnp.sqrt(moment_two / (1.0 - adam_second**STEP)) + adam_eps)
    )
    gains_new = gains - adam_rate * adam_ratio

    new_key, new_value = small_update(
        moment_kv,
        w_key.T,
        w_value.T,
        (n_ctx, 2 * n_planes, n_lo),
        [muon_rate * D ** (-0.5) * math.sqrt(max(D, KV * HD))] * 2,
    )
    new_key, new_value = new_key.T, new_value.T
    half_ctx = n_ctx // 2

    def step_of(spread, widest):
        return muon_rate * spread * math.sqrt(widest)

    def updated(weight, spread, widest, direction):
        return weight * (1.0 - muon_rate * weight_decay) - step_of(spread, widest) * direction

    def in_parts(weight, spread, widest, columns, first, flipped, place):
        parts = 1 if first == columns else 2
        if columns % 128 == 0:
            return update(weight, polar, new_key, step_of(spread, widest), columns, first, flipped, place)
        chips = []
        for chip in range(n_ctx):
            for part in range(parts):
                width = first if part == 0 else columns - first
                chips.append(polar[place(chip, part)][:, :width])
        direction = jnp.concatenate(chips, 1).astype(jnp.float32)
        return updated(weight, spread, widest, direction.T if flipped else direction)

    def ff_update(weight, spread, slot, flipped=False):
        return in_parts(
            weight, spread, max(D, FF), chip_ff, ff_cols, flipped, lambda chip, part: (chip, slot, part)
        )

    def model_update(weight, spread, which):
        if halved:
            return in_parts(
                weight,
                spread,
                D,
                chip_model,
                chip_model,
                False,
                lambda chip, part: (chip % half_ctx + which * half_ctx, n_planes - 1, chip // half_ctx),
            )
        return in_parts(
            weight, spread, D, chip_model, chip_model // 2, False, lambda chip, part: (chip, 3 + which, part)
        )

    new_query = model_update(w_query, D ** (-0.5), 0)
    new_out = model_update(w_out, 32 ** (-0.5), 1)
    new_gate = ff_update(w_gate, D ** (-0.5), 0)
    new_up = ff_update(w_up, D ** (-0.5), 2)
    new_down = ff_update(w_down, FF ** (-0.5), 1, True)
    return (
        block_out,
        input_grad,
        gain_grad,
        moment_one,
        moment_two,
        gains_new,
        grad_query,
        new_m_query,
        new_query,
        grad_key,
        new_m_key,
        new_key,
        grad_value,
        new_m_value,
        new_value,
        grad_out,
        new_m_out,
        new_out,
        grad_gate,
        new_m_gate,
        new_gate,
        grad_up,
        new_m_up,
        new_up,
        grad_down,
        new_m_down,
        new_down,
    )


def solution(mesh):
    n_ctx, n_fsdp = mesh.shape["ctx"], mesh.shape["fsdp"]
    n_lo = 2 * n_ctx // KV // 2
    n_planes = n_fsdp // 2
    finer = Mesh(
        mesh.devices.reshape(n_ctx // n_lo, n_lo, n_planes // n_lo, n_lo, 2),
        CTX + PLANES + ("core",),
    )
    fsdp = PLANES + ("core",)
    tokens, whole = P(fsdp, CTX, None), P()
    rows, columns = P(fsdp, None), P(None, fsdp)
    row_block, column_block = P(fsdp, CTX), P(CTX, fsdp)
    matrix, transposed = (row_block, row_block, rows), (column_block, column_block, columns)
    return jax.shard_map(
        body,
        mesh=finer,
        in_specs=(tokens, tokens, whole, whole, whole)
        + (rows, columns, columns, rows, rows, rows, columns)
        + (row_block, column_block, column_block, row_block, row_block, row_block, column_block),
        out_specs=(tokens, tokens, whole, whole, whole, whole)
        + matrix
        + transposed
        + transposed
        + matrix
        + matrix
        + matrix
        + transposed,
        check_vma=False,
    )
```

```python
import functools
import math

import jax
import jax.numpy as jnp
from jax import lax
from jax.experimental import pallas as pl
from jax.experimental.pallas import tpu as pltpu
from jax.sharding import Mesh
from jax.sharding import PartitionSpec as P

D = 2048
H = 32
KV = 4
HD = 64
FF = 5632
NS = 5
STEP = 10


norm_eps = 1e-05
rope_base = 10000.0
masked_score = -1e30
poly_first = 3.4445
poly_second = -4.775
poly_third = 2.0315
momentum_decay = 0.95
muon_rate = 0.3
weight_decay = 0.1
adam_first = 0.9
adam_second = 0.95
adam_rate = 0.4
adam_eps = 1e-08

MESH = pl.DeviceIdType.MESH
CTX = ("ctx_hi", "ctx_lo")
PLANES = ("z_hi", "z_lo")


def rope_tables(positions, head_width):
    frequency = jnp.exp(
        jnp.arange(head_width // 2, dtype=jnp.float32) * (-2.0 * math.log(rope_base) / head_width)
    )
    angles = positions[:, None] * frequency[None, :]
    cos_half = jnp.cos(angles)
    sin_half = jnp.sin(angles)
    return (jnp.concatenate([cos_half] * 4, -1), jnp.concatenate([-sin_half, sin_half] * 2, -1))


def norm_forward(values, gain_row):
    inverse = lax.rsqrt(jnp.mean(values * values, -1, keepdims=True) + norm_eps)
    return (values * inverse * gain_row, inverse)


def norm_backward(values, inverse, gain_row, gradients):
    scaled = gradients * gain_row
    inner_mean = jnp.mean(scaled * values, -1, keepdims=True)
    return (
        inverse * scaled - values * inverse**3 * inner_mean,
        jnp.sum(gradients * values * inverse, 0),
    )


def matmul(first_op, second_op):
    return jnp.dot(first_op, second_op, preferred_element_type=jnp.float32)


def contract_rows(first_op, second_op):
    return lax.dot_general(
        first_op, second_op, (((0,), (0,)), ((), ())), preferred_element_type=jnp.float32
    )


def contract_cols(first_op, second_op):
    return lax.dot_general(
        first_op, second_op, (((1,), (1,)), ((), ())), preferred_element_type=jnp.float32
    )


def low(values):
    return values.astype(jnp.bfloat16)


class Exchange:
    def __init__(self, shape, sems, half=0, halved=False):
        self.n_ctx, self.n_lo = shape
        self.stages = self.n_ctx.bit_length() - 1
        self.ranks = 2 * self.n_ctx
        self.half, self.halved = half, halved
        self.ctx = lax.axis_index("ctx_hi") * self.n_lo + lax.axis_index("ctx_lo")
        self.core = lax.axis_index("core")
        self.other_core = {"core": 1 - self.core}
        turned = self.core * (1 - half)
        self.deltas = []
        for s in range(1, self.stages + 1):
            step = turned * 2 ** (self.stages - s) + (1 - turned) * 2 ** (s - 1)
            self.deltas.append(step * (1 - 2 * ((self.ctx // step) % 2)))
        (
            self.core_out,
            self.core_in,
            self.ctx_out,
            self.ctx_in,
            self.back_core_out,
            self.back_core_in,
            self.back_out,
            self.back_in,
        ) = sems

    def partner(self, s):
        there = self.ctx + self.deltas[s - 1]
        return {"ctx_hi": there // self.n_lo, "ctx_lo": there % self.n_lo}

    def place(self, other, idx):
        where = self.ctx
        for s in range(1, self.stages + 1):
            where = where + ((idx // 2 ** (self.stages - s)) % 2) * self.deltas[s - 1]
        return 2 * where + self.core + other * (1 - 2 * self.core)

    def across(self, idx):
        mirrored = 0
        for s in range(self.stages):
            mirrored = mirrored + ((idx // 2**s) % 2) * 2 ** (self.stages - 1 - s)
        return self.half * idx + (1 - self.half) * mirrored

    def whole(self, flag, run):
        if self.halved:
            pl.when(self.half == flag)(run)
        elif flag == 0:
            run()

    def greet(self, more=0):
        barrier = pltpu.get_barrier_semaphore()
        pl.semaphore_signal(barrier, inc=1, device_id=self.other_core, device_id_type=MESH)
        for s in range(1, self.stages + 1):
            pl.semaphore_signal(barrier, inc=1, device_id=self.partner(s), device_id_type=MESH)
        pl.semaphore_wait(barrier, 1 + self.stages + more)

    def copy(self, source, target, send, receive, device):
        return pltpu.make_async_remote_copy(
            src_ref=source,
            dst_ref=target,
            send_sem=send,
            recv_sem=receive,
            device_id=device,
            device_id_type=MESH,
        )


    def parts(self, size):
        middle = (size + 1) // 2
        return [(0, middle), (middle, size)]


    def sum_part(self, h):
        low_end, high_end = self.parts(self.part.shape[2])[h]
        return pl.ds(low_end, high_end - low_end)

    def core_copy(self, idx, h):
        slot = self.across(idx)
        span = self.sum_part(h)
        return self.copy(
            self.part.at[1, idx, span],
            self.from_core.at[slot, span],
            self.core_out.at[idx, h],
            self.core_in.at[slot, h],
            self.other_core,
        )

    def core_arrived(self, idx, h):
        span = self.sum_part(h)
        self.copy(
            self.part.at[1, idx, span],
            self.from_core.at[idx, span],
            self.core_out.at[idx, h],
            self.core_in.at[idx, h],
            self.other_core,
        ).wait_recv()

    def ctx_copy(self, s, idx, h):
        span = self.sum_part(h)
        return self.copy(
            self.part.at[0, idx, span],
            self.from_ctx.at[idx, span],
            self.ctx_out.at[idx, h],
            self.ctx_in.at[idx, h],
            self.partner(s),
        )

    def incoming(self, s, idx):
        return idx + 2 ** (self.stages - s)

    def add(self, idx, sources, target, h):
        def one(chunk, carry):
            total = self.part[0, idx, chunk].astype(jnp.float32)
            total = total + self.from_core[idx, chunk].astype(jnp.float32)
            for source in sources:
                total = total + self.from_ctx[source, chunk].astype(jnp.float32)
            target[chunk] = total.astype(target.dtype)
            return carry

        lax.fori_loop(*self.parts(self.part.shape[2])[h], one, 0)

    def sum_pieces(self, part, from_core, from_ctx, make, target):
        self.part, self.from_core, self.from_ctx = part, from_core, from_ctx
        n_ctx, stages = self.n_ctx, self.stages

        def pass_on(idx):
            s = stages + 1 - idx.bit_length()
            for h in range(2):
                self.core_arrived(idx, h)
                for t in range(1, s):
                    self.ctx_copy(t, self.incoming(t, idx), h).wait_recv()
                self.add(idx, [self.incoming(t, idx) for t in range(1, s)], part.at[0, idx], h)
                if s < stages:
                    self.ctx_copy(s, idx, h).start()
                else:
                    self.whole(0, lambda h=h: self.ctx_copy(s, idx, h).start())

        def fill(step, carry):
            idx = n_ctx - 1 - step
            theirs = self.across(idx)
            make(1, theirs)
            for h in range(2):
                self.core_copy(theirs, h).start()
            make(0, idx)
            for early in range(n_ctx // 2, n_ctx):
                pl.when(idx == early)(functools.partial(pass_on, early))
            return carry

        lax.fori_loop(0, n_ctx, fill, 0)
        for idx in range(n_ctx // 2 - 1, 0, -1):
            pass_on(idx)
        early = [self.incoming(t, 0) for t in range(1, stages)]
        for h in range(2):
            self.core_arrived(0, h)
            for t in range(1, stages):
                self.ctx_copy(t, self.incoming(t, 0), h).wait_recv()

            def finish_whole(h=h):
                self.ctx_copy(stages, 1, h).wait_recv()
                self.add(0, early + [1], target, h)

            self.whole(0, finish_whole)
            self.whole(1, lambda h=h: self.add(0, early, target, h))

    def sums_sent(self):
        for h in range(2):
            for idx in range(self.n_ctx):
                self.core_copy(idx, h).wait_send()
            for s in range(1, self.stages + 1):
                upper = 2 ** (self.stages - s)
                for idx in range(upper, 2 * upper):
                    if s < self.stages:
                        self.ctx_copy(s, idx, h).wait_send()
                    else:
                        self.whole(0, lambda s=s, idx=idx, h=h: self.ctx_copy(s, idx, h).wait_send())


    def block(self, rank, h):
        low_end, high_end = self.parts(self.gathered.shape[1])[h]
        return self.gathered.at[rank, pl.ds(low_end, high_end - low_end)]

    def back_copy(self, s, idx, h):
        there = idx + 2 ** (self.stages - s)
        block = self.block(self.place(0, idx), h)
        return self.copy(block, block, self.back_out.at[there, h], self.back_in.at[there, h], self.partner(s))

    def back_core_copy(self, idx, h):
        block = self.block(self.place(0, idx), h)
        return self.copy(
            block, block, self.back_core_out.at[idx, h], self.back_core_in.at[self.across(idx), h], self.other_core
        )

    def announce(self, idx, h):
        for s in range(self.stages, 0, -1):
            if idx < 2 ** (self.stages - s):
                if s < self.stages:
                    self.back_copy(s, idx, h).start()
                else:
                    self.whole(0, lambda s=s: self.back_copy(s, idx, h).start())
        self.back_core_copy(idx, h).start()

    def arrived(self, idx, h):
        block = self.block(self.place(0, idx), h)
        self.copy(block, block, self.back_out.at[idx, h], self.back_in.at[idx, h], self.other_core).wait_recv()

    def core_back_arrived(self, idx, h):
        block = self.block(self.place(1, idx), h)
        self.copy(
            block, block, self.back_core_out.at[idx, h], self.back_core_in.at[idx, h], self.other_core
        ).wait_recv()

    def gather_pieces(self, gathered, use):
        self.gathered = gathered
        for h in range(2):
            self.announce(0, h)

        def visit(step, carry):
            idx, other = step // 2, step % 2

            def on_arrival(v):
                for h in range(2):
                    if v == 1:
                        self.whole(0, lambda h=h: self.arrived(1, h))
                    else:
                        self.arrived(v, h)
                    self.announce(v, h)

            for v in range(1, self.n_ctx):
                pl.when(step == 2 * v)(functools.partial(on_arrival, v))
            idx = (1 - other) * idx + other * self.across(idx)

            def on_core_arrival():
                for h in range(2):
                    self.core_back_arrived(idx, h)

            pl.when(other == 1)(on_core_arrival)
            use(self.place(other, idx), step)
            return carry

        lax.fori_loop(0, 2 * self.n_ctx, visit, 0)

    def gathers_sent(self):
        for h in range(2):
            for idx in range(self.n_ctx):
                self.back_core_copy(idx, h).wait_send()
            for s in range(1, self.stages + 1):
                for idx in range(2 ** (self.stages - s)):
                    if s < self.stages:
                        self.back_copy(s, idx, h).wait_send()
                    else:
                        self.whole(0, lambda s=s, idx=idx, h=h: self.back_copy(s, idx, h).wait_send())


def exchange_sems(n_ctx):
    return [pltpu.SemaphoreType.DMA((n_ctx, 2))] * 8


def muon_kernel(shape, mains, *refs):
    n_ctx, n_lo, n_planes, z_lo, halved, widths = shape
    slot_refs, refs = refs[:mains], refs[mains:]
    pair_ref, gains_ref, out_ref, gains_out_ref = refs[:4]
    x_ref, y_ref, a_ref, part, from_core, from_ctx, both_gathered, landed, scale, strip, near, far = refs[4:16]
    gathered, gathered_beside = both_gathered.at[0], both_gathered.at[1]
    slots_out, pair_out, blocks_in, rows_out, rows_in, spread_out, spread_in, kept = refs[16:24]
    near_out, near_in, far_out, far_in = refs[24:28]
    sems = refs[28:]
    plane = lax.axis_index("z_hi") * z_lo + lax.axis_index("z_lo")
    ex = Exchange((n_ctx, n_lo), sems[:8], plane // (n_planes - 1) if halved else 0, halved)
    ex_beside = Exchange((n_ctx, n_lo), sems[:4] + sems[8:12], ex.half, halved)
    even = Exchange((n_ctx, n_lo), sems[:8])
    ctx, core = ex.ctx, ex.core
    own = 2 * plane + core
    shards = 2 * n_planes
    tall = D // shards
    blocks = ex.ranks
    side = D // blocks
    reach = blocks // 2 + 1
    devices = n_ctx * shards

    def device(at_ctx, at_plane, at_core):
        return {
            "ctx_hi": at_ctx // n_lo,
            "ctx_lo": at_ctx % n_lo,
            "z_hi": at_plane // z_lo,
            "z_lo": at_plane % z_lo,
            "core": at_core,
        }

    least = min(widths) if halved else min(widths[:2])
    if least < x_ref.shape[1]:
        x_ref[:, least:] = jnp.zeros((D, x_ref.shape[1] - least), x_ref.dtype)
    barrier = pltpu.get_barrier_semaphore()
    here = ctx * shards + own

    def greet(offset, carry):
        there = (here + offset) % devices
        shard = there % shards
        pl.semaphore_signal(
            barrier, inc=1, device_id=device(there // shards, shard // 2, shard % 2), device_id_type=MESH
        )
        return carry

    lax.fori_loop(1, devices, greet, 0)
    pl.semaphore_wait(barrier, devices - 1)

    def rows_of(block):
        return pl.ds(pl.multiple_of(block * side, side), side)

    def shard_rows(shard):
        return pl.ds(pl.multiple_of(shard * tall, tall), tall)

    def send(source, target, out_sem, in_sem, at_ctx, at_plane, at_core, begin):
        same = (at_ctx * n_planes + at_plane) * 2 + at_core == here
        far = ex.copy(source, target, out_sem, in_sem, device(at_ctx, at_plane, at_core))
        near = pltpu.make_async_copy(source, target, in_sem)

        def other():
            far.start() if begin else far.wait_send()

        def this():
            if begin:
                near.start()

        pl.when(same)(this)
        pl.when(jnp.logical_not(same))(other)

    def by_width(pair, at_core, run):
        if halved:
            pl.when(pair == 1)(lambda: run(widths[2]))
        for which in range(2):
            pl.when(jnp.logical_and(pair == 0, at_core == which))(functools.partial(run, widths[which]))

    def send_pair(begin):
        for which in range(2):
            send(
                pair_ref.at[which],
                x_ref.at[shard_rows(own), pl.ds(0, widths[2])],
                pair_out.at[which],
                blocks_in.at[own],
                ctx % (n_ctx // 2) + which * (n_ctx // 2),
                n_planes - 1,
                ctx // (n_ctx // 2),
                begin,
            )

    def send_blocks(begin):
        for slot in range(mains):
            for to_core in range(2):
                columns = pl.ds(0, widths[to_core])
                send(
                    slot_refs[slot].at[to_core, :, columns],
                    x_ref.at[shard_rows(own), columns],
                    slots_out.at[slot, to_core],
                    blocks_in.at[own],
                    ctx,
                    slot,
                    to_core,
                    begin,
                )

    def wait_blocks(columns):
        def one(shard, carry):
            target = x_ref.at[shard_rows(shard), pl.ds(0, columns)]
            pltpu.make_async_copy(target, target, blocks_in.at[shard]).wait()
            return carry

        lax.fori_loop(0, shards, one, 0)

    gains = AllSum(ex, n_planes, z_lo, near, far, near_out, near_in, far_out, far_in)
    if halved:
        send_pair(True)
        send_pair(False)
    send_blocks(True)
    gains.begin(gains_ref[...])
    by_width(ex.half, core, wait_blocks)
    send_blocks(False)

    def in_use(run):
        ex.whole(0, lambda: run(slice(0, x_ref.shape[1])))
        ex.whole(1, lambda: run(slice(0, widths[2])))

    def gram_piece(other, idx):
        block = ex.place(other, idx)

        def run(columns):
            left = x_ref[rows_of(block), columns]
            for offset in range(reach):
                right = x_ref[rows_of((block + offset) % blocks), columns]
                part[other, idx, offset] = low(contract_cols(left, right))

        in_use(run)

    def spread(block, step, pieces=gathered):
        del step
        for offset in range(reach):
            column = (block + offset) % blocks
            piece = pieces[block, offset]
            a_ref[rows_of(block), rows_of(column)] = piece
            if 0 < offset < reach - 1:
                a_ref[rows_of(column), rows_of(block)] = piece.T

    def gram():
        ex.sum_pieces(part, from_core, from_ctx, gram_piece, gathered.at[ex.place(0, 0)])

        def second_own():
            def one(offset, inner):
                gathered[ex.place(0, 1), offset] = part[0, 1, offset]
                return inner

            lax.fori_loop(0, reach, one, 0)

        ex.whole(1, second_own)
        ex.gather_pieces(gathered, spread)
        ex.sums_sent()
        ex.gathers_sent()

    high = 512
    halfway = D // high

    def update_step(step):
        factor = scale[0:1, 0:1]

        def first_product(columns):
            rows = pl.ds(pl.multiple_of(step * high, high), high)
            y_ref[rows, columns] = low(matmul(a_ref[rows, :], x_ref[:, columns]) * (factor * factor * factor))

        def second_product(columns):
            rows = pl.ds(pl.multiple_of((step - halfway) * high, high), high)
            second = matmul(a_ref[rows, :], y_ref[:, columns])
            x_ref[rows, columns] = low(
                (poly_first * factor) * x_ref[rows, columns].astype(jnp.float32)
                + poly_second * y_ref[rows, columns].astype(jnp.float32)
                + (poly_third * factor * factor) * second
            )

        pl.when(step < halfway)(lambda: in_use(first_product))
        pl.when(jnp.logical_and(step >= halfway, step < 2 * halfway))(lambda: in_use(second_product))

    def update_all():
        def one(step, carry):
            update_step(step)
            return carry

        lax.fori_loop(0, 2 * halfway, one, 0)

    def norm_now():
        def one(block, total):
            rows = lax.broadcasted_iota(jnp.int32, (side, side), 0)
            cols = lax.broadcasted_iota(jnp.int32, (side, side), 1)
            piece = gathered[block, 0].astype(jnp.float32)
            piece = jnp.where(rows == cols, piece, 0.0)
            return total + jnp.sum(jnp.sum(piece, 0, keepdims=True), 1, keepdims=True)

        trace = lax.fori_loop(0, blocks, one, jnp.zeros((1, 1), jnp.float32))
        scale[...] = jnp.broadcast_to(1.0 / (jnp.sqrt(trace) + 1e-07), scale.shape)

    def norm_done():
        scale[...] = jnp.ones(scale.shape, jnp.float32)

    def next_gram_rows(block):
        factor = scale[0:1, 0:1] * scale[0:1, 0:1]
        wide = 512

        def product(source, target, finish):
            def one(step, carry):
                columns = pl.ds(pl.multiple_of(step * wide, wide), wide)
                strip[target, :, columns] = low(finish(matmul(source(), a_ref[:, columns]), columns))
                return carry

            lax.fori_loop(0, D // wide, one, 0)

        def own_rows(columns=slice(None)):
            return a_ref[rows_of(block), columns]

        product(own_rows, 0, lambda value, columns: value * (factor * factor))
        product(
            lambda: strip[0],
            1,
            lambda value, columns: (poly_first * factor) * own_rows(columns).astype(jnp.float32)
            + poly_second * strip[0, :, columns].astype(jnp.float32)
            + (poly_third * factor) * value,
        )
        product(lambda: strip[1], 0, lambda value, columns: value * factor)

        def last(offset, carry):
            columns = rows_of((block + offset) % blocks)
            value = matmul(strip[0], a_ref[:, columns])
            gathered_beside[block, offset] = low(
                poly_first * strip[1, :, columns].astype(jnp.float32)
                + poly_second * strip[0, :, columns].astype(jnp.float32)
                + (poly_third * factor) * value
            )
            return carry

        lax.fori_loop(0, reach, last, 0)

    def two_sweeps(pair, carry):
        gram()
        pl.when(pair == 0)(norm_now)
        pl.when(pair == 0)(gains.between)
        pl.when(pair > 0)(norm_done)
        next_gram_rows(ex.place(0, 0))

        def update_beside(block, step):
            del block
            pl.when(step == 0)(lambda: ex.whole(1, lambda: next_gram_rows(ex.place(0, 1))))
            update_step(step)

        ex_beside.gather_pieces(gathered_beside, update_beside)
        norm_done()

        def spread_one(block, inner):
            spread(block, 0, gathered_beside)
            return inner

        lax.fori_loop(0, blocks, spread_one, 0)
        update_all()
        ex_beside.gathers_sent()
        return carry

    lax.fori_loop(0, NS // 2, two_sweeps, 0)
    if NS % 2:
        gram()
        update_all()

    gains_out_ref[...] = gains.end()

    def send_rows(begin):
        def run(width):
            columns = pl.ds(0, width)
            for offset in range(n_planes):
                to_plane = (plane + offset) % n_planes
                for to_core in range(2):
                    shard = 2 * to_plane + to_core
                    send(
                        x_ref.at[shard_rows(shard), columns],
                        landed.at[ctx, plane, core, :, columns],
                        rows_out.at[shard],
                        rows_in.at[own],
                        ctx,
                        to_plane,
                        to_core,
                        begin,
                    )

        by_width(ex.half, core, run)

    def with_width(shard, run):
        by_width(shard // 2 // (n_planes - 1) if halved else 0, shard % 2, run)

    send_rows(True)
    stages = even.stages

    def block_of(where, shard, width):
        return (where, shard // 2, shard % 2, slice(None), pl.ds(0, width))

    def spread_copy(s, idx, where, shard, width):
        block = landed.at[block_of(where, shard, width)]
        there = idx + 2 ** (stages - s)
        return even.copy(
            block, block, spread_out.at[there, shard], spread_in.at[there, shard], even.partner(s)
        )

    def keep(where, shard, idx, width):
        place = block_of(where, shard, width)
        return pltpu.make_async_copy(landed.at[place], out_ref.at[place], kept.at[idx, shard])

    def owner(idx):
        return even.place(0, idx) // 2

    def pass_on(idx, shard):
        def run(width):
            block = landed.at[block_of(owner(idx), shard, width)]
            if idx == 0:
                pltpu.make_async_copy(block, block, rows_in.at[shard]).wait()
            else:
                pltpu.make_async_copy(block, block, spread_in.at[idx, shard]).wait()
            for s in range(stages, 0, -1):
                if idx < 2 ** (stages - s):
                    spread_copy(s, idx, owner(idx), shard, width).start()
            keep(owner(idx), shard, idx, width).start()

        with_width(shard, run)

    rounds = n_planes - 1 if halved else n_planes

    def in_order(step):
        turn_of = step // 2
        last = turn_of // rounds
        return 2 * (last * rounds + (1 - last) * ((plane + turn_of) % rounds)) + step % 2

    def arrive(step, carry):
        pl.when(step < shards)(lambda: pass_on(0, in_order(step)))
        for idx in range(1, n_ctx):
            lag = idx.bit_length()
            now = step - lag
            pl.when(jnp.logical_and(now >= 0, now < shards))(
                functools.partial(pass_on, idx, in_order(jnp.maximum(now, 0)))
            )
        return carry

    lax.fori_loop(0, shards + stages, arrive, 0)
    send_rows(False)

    def finish(shard, carry):
        def run(width):
            for idx in range(n_ctx):
                keep(owner(idx), shard, idx, width).wait()
                for s in range(stages, 0, -1):
                    if idx < 2 ** (stages - s):
                        spread_copy(s, idx, owner(idx), shard, width).wait_send()

        with_width(shard, run)
        return carry

    lax.fori_loop(0, shards, finish, 0)


def in_vmem(count):
    return [pl.BlockSpec(memory_space=pltpu.VMEM)] * count


def anywhere(count):
    return [pl.BlockSpec(memory_space=pl.ANY)] * count


def cost(flops, micros):
    return pl.CostEstimate(flops=flops, bytes_accessed=int(micros * 3.0e6), transcendentals=0)


def muon(slots, pair, gains, shape):
    n_ctx, _, n_planes = shape[:3]
    rows_here, columns = slots[0].shape[1:]
    blocks = 2 * n_ctx
    side = D // blocks
    piece = (blocks // 2 + 1, side, side)
    dma = pltpu.SemaphoreType.DMA
    landed = (n_ctx, n_planes, 2, rows_here, columns)
    return pl.pallas_call(
        functools.partial(muon_kernel, shape, len(slots)),
        out_shape=[
            jax.ShapeDtypeStruct(landed, jnp.bfloat16),
            jax.ShapeDtypeStruct(gains.shape, jnp.float32),
        ],
        in_specs=anywhere(len(slots) + 1) + in_vmem(1),
        out_specs=anywhere(1) + in_vmem(1),
        scratch_shapes=[
            pltpu.VMEM((D, columns), jnp.bfloat16),
            pltpu.VMEM((D, columns), jnp.bfloat16),
            pltpu.VMEM((D, D), jnp.bfloat16),
            pltpu.VMEM((2, n_ctx) + piece, jnp.bfloat16),
            pltpu.VMEM((n_ctx,) + piece, jnp.bfloat16),
            pltpu.VMEM((n_ctx,) + piece, jnp.bfloat16),
            pltpu.VMEM((2, blocks) + piece, jnp.bfloat16),
            pltpu.VMEM(landed, jnp.bfloat16),
            pltpu.VMEM((8, 128), jnp.float32),
            pltpu.VMEM((2, side, D), jnp.bfloat16),
            pltpu.VMEM((blocks,) + gains.shape, jnp.float32),
            pltpu.VMEM((n_planes,) + gains.shape, jnp.float32),
            dma((len(slots), 2)),
            dma((2,)),
            dma((2 * n_planes,)),
            dma((2 * n_planes,)),
            dma((2 * n_planes,)),
            dma((n_ctx, 2 * n_planes)),
            dma((n_ctx, 2 * n_planes)),
            dma((n_ctx, 2 * n_planes)),
            dma((blocks,)),
            dma((blocks,)),
            dma((n_planes,)),
            dma((n_planes,)),
        ]
        + exchange_sems(n_ctx)
        + [dma((n_ctx, 2))] * 4,
        compiler_params=pltpu.CompilerParams(
            collective_id=0, has_side_effects=True, vmem_limit_bytes=60 * 2**20
        ),
        cost_estimate=cost(NS * 5 * D * D * columns, 350),
        name="muon",
    )(*slots, pair, gains)


def momentum_kernel(first, flipped, split, sum_ref, got_ref, moment_ref, grad_ref, new_ref, low_ref):
    core = lax.axis_index("core")
    tall = got_ref.shape[0]
    mine = sum_ref[pl.ds(pl.multiple_of(core * tall, tall), tall), :].astype(jnp.float32)
    got = got_ref[...].astype(jnp.float32)
    left = jnp.where(core == 0, mine, got)
    right = jnp.where(core == 0, got, mine)
    columns = moment_ref.shape[0 if flipped else 1]
    gradient = jnp.concatenate([left[:, :first], right[:, : columns - first]], 1)
    if flipped:
        grad_ref[...] = gradient.T
        new = momentum_decay * moment_ref[...] + grad_ref[...]
        new_ref[...] = new
        new = new.T
    else:
        grad_ref[...] = gradient
        new = momentum_decay * moment_ref[...] + gradient
        new_ref[...] = new
    if split:
        padded = low_ref.shape[2]
        for index, part in enumerate((low(new[:, :first]), low(new[:, first:]))):
            if part.shape[1] < padded:
                zeros = jnp.zeros((tall, padded - part.shape[1]), jnp.bfloat16)
                part = jnp.concatenate([part, zeros], 1)
            low_ref[index] = part
    else:
        low_ref[...] = low(new)


def momentum(summed, moment, first, padded, core, flipped=False, split=True):
    tall = summed.shape[0] // 2
    got = swap_core(lax.dynamic_slice_in_dim(summed, (1 - core) * tall, tall, 0))
    columns = moment.shape[0 if flipped else 1]
    out = jax.ShapeDtypeStruct(moment.shape, jnp.float32)
    low_shape = (2, tall, padded) if split else (tall, columns)
    return pl.pallas_call(
        functools.partial(momentum_kernel, first, flipped, split),
        out_shape=[out, out, jax.ShapeDtypeStruct(low_shape, jnp.bfloat16)],
        in_specs=in_vmem(3),
        out_specs=in_vmem(3),
        compiler_params=pltpu.CompilerParams(vmem_limit_bytes=48 * 2**20),
        name="momentum",
    )(summed, got, moment)


def small_kernel(shape, steps, moments_ref, key_ref, value_ref, new_key_ref, new_value_ref, x_ref, y_ref, own_ref):
    n_ctx, shards, z_lo = shape
    columns, wide = moments_ref.shape[2:]
    plane = lax.axis_index("z_hi") * z_lo + lax.axis_index("z_lo")
    own = 2 * plane + lax.axis_index("core")
    for which in range(2):
        for ctx in range(n_ctx):
            for shard in range(shards):
                x_ref[which, shard * columns : (shard + 1) * columns, ctx * wide : (ctx + 1) * wide] = moments_ref[
                    ctx * shards + shard, which
                ]
        start = x_ref[which].astype(jnp.float32)
        norm = jnp.sqrt(jnp.sum(jnp.sum(start * start, 0, keepdims=True), 1, keepdims=True))
        x_ref[which] = low(start * (1.0 / (norm + 1e-07)))

    def sweep(index, carry):
        grams = [low(contract_cols(x_ref[which], x_ref[which])) for which in range(2)]
        for which in range(2):
            y_ref[which] = low(matmul(grams[which], x_ref[which]))
        for which in range(2):
            x_ref[which] = low(
                poly_first * x_ref[which].astype(jnp.float32)
                + poly_second * y_ref[which].astype(jnp.float32)
                + poly_third * matmul(grams[which], y_ref[which])
            )
        return carry

    lax.fori_loop(0, NS, sweep, 0)
    for which, (old_ref, new_ref) in enumerate(((key_ref, new_key_ref), (value_ref, new_value_ref))):
        own_ref[...] = x_ref[which, pl.ds(pl.multiple_of(own * columns, columns), columns), :].astype(jnp.float32)
        new_ref[...] = old_ref[...] * (1.0 - muon_rate * weight_decay) - steps[which] * own_ref[...]


def small_update(moments, key, value, shape, steps):
    out = jax.ShapeDtypeStruct(key.shape, jnp.float32)
    return pl.pallas_call(
        functools.partial(small_kernel, shape, steps),
        out_shape=[out, out],
        in_specs=in_vmem(3),
        out_specs=in_vmem(2),
        scratch_shapes=[
            pltpu.VMEM((2, KV * HD, D), jnp.bfloat16),
            pltpu.VMEM((2, KV * HD, D), jnp.bfloat16),
            pltpu.VMEM(key.shape, jnp.float32),
        ],
        compiler_params=pltpu.CompilerParams(vmem_limit_bytes=48 * 2**20),
        cost_estimate=cost(0, 15),
        name="small_update",
    )(moments, key, value)


def update_kernel(step, columns, first, flipped, weight_ref, *refs):
    parts, out_ref = refs[:-2], refs[-1]
    direction = parts[0][...].reshape(parts[0].shape[-2:])[:, :first]
    if len(parts) > 1:
        second = parts[1][...].reshape(parts[1].shape[-2:])[:, : columns - first]
        direction = jnp.concatenate([direction, second], 1)
    direction = direction.astype(jnp.float32)
    if flipped:
        direction = direction.T
    out_ref[...] = weight_ref[...] * (1.0 - muon_rate * weight_decay) - step * direction


def update(weight, polar, earlier, step, columns, first, flipped, place):
    tall, wide = polar.shape[-2:]
    count = weight.shape[0 if flipped else 1] // columns
    if flipped:
        block = pl.BlockSpec((columns, tall), lambda chip: (chip, 0))
    else:
        block = pl.BlockSpec((tall, columns), lambda chip: (0, chip))
    parts = [
        pl.BlockSpec((1, 1, 1, tall, wide), lambda chip, part=part: tuple(place(chip, part)) + (0, 0))
        for part in range(1 if first == columns else 2)
    ]
    return pl.pallas_call(
        functools.partial(update_kernel, step, columns, first, flipped),
        grid=(count,),
        out_shape=jax.ShapeDtypeStruct(weight.shape, jnp.float32),
        in_specs=[block] + parts + anywhere(1),
        out_specs=block,
        compiler_params=pltpu.CompilerParams(vmem_limit_bytes=48 * 2**20),
        name="update",
    )(weight, *([polar] * len(parts)), earlier)


def scatter_kernel(shape, term, n_lhs, n_earlier, *refs):
    lhs, right = refs[:n_lhs], refs[n_lhs]
    refs = refs[n_lhs + 1 + n_earlier :]
    out, part, from_core, from_ctx = refs[:4]
    ex = Exchange(shape, refs[4:])
    ex.greet()
    chunks, tall, wide = out.shape

    def make(other, idx):
        block = ex.place(other, idx)
        start = ((block % 2) * ex.n_ctx + block // 2) * chunks * tall
        rows = pl.ds(pl.multiple_of(start, chunks * tall), chunks * tall)
        total = term([left[rows, :] for left in lhs], right)
        part[other, idx] = low(total).reshape(chunks, tall, wide)

    ex.sum_pieces(part, from_core, from_ctx, make, out)
    ex.sums_sent()


def product_scatter(lhs, right, term, shape, tokens, collective_id, name, earlier=()):
    n_ctx = shape[0]
    piece = (tokens // 32, 32, D)
    flops = sum(2 * a.shape[0] * a.shape[1] * D for a in lhs)
    out = pl.pallas_call(
        functools.partial(scatter_kernel, shape, term, len(lhs), len(earlier)),
        out_shape=jax.ShapeDtypeStruct(piece, jnp.float32),
        in_specs=in_vmem(len(lhs) + 1) + anywhere(len(earlier)),
        out_specs=pl.BlockSpec(memory_space=pltpu.VMEM),
        scratch_shapes=[
            pltpu.VMEM((2, n_ctx) + piece, jnp.bfloat16),
            pltpu.VMEM((n_ctx,) + piece, jnp.bfloat16),
            pltpu.VMEM((n_ctx,) + piece, jnp.bfloat16),
        ]
        + exchange_sems(n_ctx),
        compiler_params=pltpu.CompilerParams(
            collective_id=collective_id, has_side_effects=True, vmem_limit_bytes=56 * 2**20
        ),
        cost_estimate=cost(flops, 40),
        name=name,
    )(*lhs, right, *earlier)
    return out.reshape(tokens, D)


def gather_kernel(shape, finish, n_weights, n_outs, n_earlier, block_ref, *refs):
    weights = refs[:n_weights]
    refs = refs[n_weights + n_earlier :]
    gathered_out, outs = refs[0], refs[1 : 1 + n_outs]
    gathered, out_sems = refs[1 + n_outs : 3 + n_outs]
    ex = Exchange(shape, refs[3 + n_outs :])
    ex.greet()
    tokens = block_ref.shape[0]
    gathered[ex.place(0, 0)] = block_ref[...]

    def keep(block):
        row = (block % 2) * ex.n_ctx + block // 2
        return pltpu.make_async_copy(gathered.at[block], gathered_out.at[row], out_sems.at[block]), row

    def use(block, step):
        del step
        copy, row = keep(block)
        copy.start()
        rows = pl.ds(pl.multiple_of(row * tokens, tokens), tokens)
        finish(rows, gathered[block], weights, outs)

    ex.gather_pieces(gathered, use)
    ex.gathers_sent()
    for block in range(ex.ranks):
        keep(block)[0].wait()


def gather_product(block, weights, finish, outs, shape, collective_id, name, earlier=()):
    tokens = block.shape[0]
    ranks = 2 * shape[0]
    flops = sum(2 * ranks * tokens * w.shape[0] * w.shape[1] for w in weights)
    result = pl.pallas_call(
        functools.partial(gather_kernel, shape, finish, len(weights), len(outs), len(earlier)),
        out_shape=[jax.ShapeDtypeStruct((ranks, tokens, D), jnp.bfloat16)] + outs,
        in_specs=in_vmem(1 + len(weights)) + anywhere(len(earlier)),
        out_specs=anywhere(1) + in_vmem(len(outs)),
        scratch_shapes=[
            pltpu.VMEM((ranks, tokens, D), jnp.bfloat16),
            pltpu.SemaphoreType.DMA((ranks,)),
        ]
        + exchange_sems(shape[0]),
        compiler_params=pltpu.CompilerParams(
            collective_id=collective_id, has_side_effects=True, vmem_limit_bytes=56 * 2**20
        ),
        cost_estimate=cost(flops, 40),
        name=name,
    )(block, *weights, *earlier)
    return [result[0].reshape(ranks * tokens, D)] + list(result[1:])


def finish_nothing(rows, block, weights, outs):
    del rows, block, weights, outs


def finish_hidden(rows, block, weights, outs):
    columns = outs[0].shape[1]
    gate_pre = matmul(block, weights[0][:, :columns])
    outs[0][rows, :] = gate_pre
    upper = matmul(block, weights[0][:, columns:])
    outs[1][rows, :] = upper
    outs[2][rows, :] = low(gate_pre * jax.nn.sigmoid(gate_pre) * upper)


def finish_mixed(rows, block, weights, outs):
    outs[0][rows, :] = low(matmul(block, weights[0][...]))


def term_one(lhs, right):
    return contract_cols(lhs[0], right[...])


def term_two(lhs, right):
    columns = lhs[0].shape[1]
    return contract_cols(lhs[0], right[:, :columns]) + contract_cols(lhs[1], right[:, columns:])


class AllSum:
    def __init__(self, ex, n_planes, z_lo, near, far, near_out, near_in, far_out, far_in):
        self.ex, self.n_planes, self.z_lo = ex, n_planes, z_lo
        self.near, self.far = near, far
        self.near_sems, self.far_sems = (near_out, near_in), (far_out, far_in)
        self.rank = 2 * ex.ctx + ex.core
        self.plane = lax.axis_index("z_hi") * z_lo + lax.axis_index("z_lo")

    def rank_id(self, offset):
        there = (self.rank + offset) % self.ex.ranks
        n_lo = self.ex.n_lo
        return {"ctx_hi": there // 2 // n_lo, "ctx_lo": there // 2 % n_lo, "core": there % 2}

    def plane_id(self, offset):
        there = (self.plane + offset) % self.n_planes
        return {"z_hi": there // self.z_lo, "z_lo": there % self.z_lo}

    def copies(self, slots, own, count, device, sems):
        return [
            self.ex.copy(slots.at[own], slots.at[own], sems[0].at[offset], sems[1].at[own], device(offset))
            for offset in range(1, count)
        ]

    def total(self, slots, own, count, device, sems):
        for offset in range(1, count):
            there = (own + offset) % count
            block = slots.at[there]
            self.ex.copy(block, block, sems[0].at[offset], sems[1].at[there], device(offset)).wait_recv()
        for copy in self.copies(slots, own, count, device, sems):
            copy.wait_send()
        total = slots[0]
        for index in range(1, count):
            total = total + slots[index]
        return total

    def begin(self, value):
        self.near[self.rank] = value
        for copy in self.copies(self.near, self.rank, self.ex.ranks, self.rank_id, self.near_sems):
            copy.start()

    def between(self):
        self.far[self.plane] = self.total(self.near, self.rank, self.ex.ranks, self.rank_id, self.near_sems)
        for copy in self.copies(self.far, self.plane, self.n_planes, self.plane_id, self.far_sems):
            copy.start()

    def end(self):
        return self.total(self.far, self.plane, self.n_planes, self.plane_id, self.far_sems)


def nothing_kernel(*refs):
    del refs


def after(values, *others):
    return pl.pallas_call(
        nothing_kernel,
        out_shape=jax.ShapeDtypeStruct(values.shape, values.dtype),
        in_specs=anywhere(1 + len(others)),
        out_specs=pl.BlockSpec(memory_space=pl.ANY),
        input_output_aliases={0: 0},
        name="after",
    )(values, *others)


def swap_core(values):
    return lax.ppermute(values, "core", [(0, 1), (1, 0)])


def split_cores(values, core):
    mine = jnp.where(core == 0, values[0], values[1])
    theirs = jnp.where(core == 0, values[1], values[0])
    got = swap_core(theirs)
    return jnp.stack([jnp.where(core == 0, mine, got), jnp.where(core == 0, got, mine)])


QUERY_ROWS = 256


def turned_pair(values):
    lane = lax.broadcasted_iota(jnp.int32, values.shape, 1)
    return jnp.where(lane % HD < HD // 2, pltpu.roll(values, 2 * HD - HD // 2, 1), pltpu.roll(values, HD // 2, 1))


def is_visible(start, stop):
    rows = lax.broadcasted_iota(jnp.int32, (QUERY_ROWS, stop), 0) + start
    return lax.broadcasted_iota(jnp.int32, (QUERY_ROWS, stop), 1) <= rows


def attention_kernel(pairs, steps, normed_ref, w_ref, cos_ref, sin_ref, mixed_ref, q_ref, k_ref, v_ref, log_ref):
    step = pl.program_id(1)
    projected = matmul(normed_ref[...], w_ref[...])
    cos, sin = cos_ref[...], sin_ref[...]
    lane = lax.broadcasted_iota(jnp.int32, (QUERY_ROWS, 2 * HD), 1)
    left = lane < HD

    def pair_of(values, pair):
        return values[:, pair * 2 * HD : (pair + 1) * 2 * HD]

    def rope(values):
        return values * cos + turned_pair(values) * sin

    both = pair_of(projected, pairs)
    keys = rope(both)
    rows = pl.ds(pl.multiple_of(step * QUERY_ROWS, QUERY_ROWS), QUERY_ROWS)
    k_ref[rows, :] = low(jnp.where(left, keys, pltpu.roll(keys, HD, 1)))
    v_ref[rows, :] = low(jnp.where(left, pltpu.roll(both, HD, 1), both))
    for pair in range(pairs):
        q_ref[:, pair * 2 * HD : (pair + 1) * 2 * HD] = low(rope(pair_of(projected, pair)))

    def attend(index):
        stop = (index + 1) * QUERY_ROWS
        seen = is_visible(index * QUERY_ROWS, stop)
        logs = jnp.zeros((QUERY_ROWS, 2 * HD), jnp.float32)
        for pair in range(pairs):
            outs = []
            for half in range(2):
                query = jnp.where(left == (half == 0), pair_of(q_ref[...], pair), 0.0)
                scores = contract_cols(low(query), k_ref[:stop, :]) * HD ** (-0.5)
                scores = jnp.where(seen, scores, masked_score)
                top = jnp.max(scores, -1, keepdims=True)
                expo = jnp.exp(scores - top)
                total = jnp.sum(expo, -1, keepdims=True)
                outs.append(matmul(low(expo), v_ref[:stop, :]) / total)
                logs = jnp.where(lane == 2 * pair + half, top + jnp.log(total), logs)
            mixed_ref[:, pair * 2 * HD : (pair + 1) * 2 * HD] = low(jnp.where(left, outs[0], outs[1]))
        log_ref[...] = logs

    for index in range(steps):
        pl.when(step == index)(functools.partial(attend, index))


def attention(normed, weight, cos, sin, length):
    every, columns = normed.shape[0], weight.shape[1]
    pairs = columns // (2 * HD) - 1
    steps = length // QUERY_ROWS
    pair = 2 * HD

    def rows(width):
        return pl.BlockSpec((QUERY_ROWS, width), lambda n, b: (n * steps + b, 0))

    def sequence():
        return pl.BlockSpec((length, pair), lambda n, b: (n, 0))

    table = pl.BlockSpec((QUERY_ROWS, pair), lambda n, b: (b, 0))
    return pl.pallas_call(
        functools.partial(attention_kernel, pairs, steps),
        grid=(every // length, steps),
        out_shape=[
            jax.ShapeDtypeStruct((every, pairs * pair), jnp.bfloat16),
            jax.ShapeDtypeStruct((every, pairs * pair), jnp.bfloat16),
            jax.ShapeDtypeStruct((every, pair), jnp.bfloat16),
            jax.ShapeDtypeStruct((every, pair), jnp.bfloat16),
            jax.ShapeDtypeStruct((every, pair), jnp.float32),
        ],
        in_specs=[rows(D), pl.BlockSpec((D, columns), lambda n, b: (0, 0)), table, table],
        out_specs=[rows(pairs * pair), rows(pairs * pair), sequence(), sequence(), rows(pair)],
        compiler_params=pltpu.CompilerParams(vmem_limit_bytes=48 * 2**20),
        cost_estimate=cost(0, 25),
        name="attention",
    )(normed, weight, cos, sin)


def attention_back_kernel(
    pairs, steps, q_ref, d_ref, k_ref, v_ref, log_ref, cos_ref, sin_ref, earlier_ref, out_ref, dk_ref, dv_ref
):
    del earlier_ref
    step = pl.program_id(1)
    lane = lax.broadcasted_iota(jnp.int32, (QUERY_ROWS, 2 * HD), 1)
    left = lane < HD

    def clear():
        dk_ref[...] = jnp.zeros(dk_ref.shape, jnp.float32)
        dv_ref[...] = jnp.zeros(dv_ref.shape, jnp.float32)

    pl.when(step == 0)(clear)

    def unrope(values, rows):
        return values * cos_ref[rows, :] - turned_pair(values) * sin_ref[rows, :]

    def attend(index):
        stop = (index + 1) * QUERY_ROWS
        rows = slice(index * QUERY_ROWS, stop)
        seen = is_visible(index * QUERY_ROWS, stop)
        for pair in range(pairs):
            at = slice(pair * 2 * HD, (pair + 1) * 2 * HD)
            parts = []
            for half in range(2):
                mine = left == (half == 0)
                query = low(jnp.where(mine, q_ref[:, at], 0.0))
                d_rows = low(jnp.where(mine, d_ref[:, at], 0.0))
                scores = contract_cols(query, k_ref[:stop, :]) * HD ** (-0.5)
                log = jnp.sum(jnp.where(lane == 2 * pair + half, log_ref[...], 0.0), -1, keepdims=True)
                probs = jnp.where(seen, jnp.exp(scores - log), 0.0)
                d_probs = contract_cols(d_rows, v_ref[:stop, :])
                delta = jnp.sum(probs * d_probs, -1, keepdims=True)
                d_scores = low(probs * (d_probs - delta))
                parts.append(matmul(d_scores, k_ref[:stop, :]) * HD ** (-0.5))
                dk_ref[:stop, :] += contract_rows(d_scores, query) * HD ** (-0.5)
                dv_ref[:stop, :] += contract_rows(low(probs), d_rows)
            out_ref[rows, at] = low(unrope(jnp.where(left, parts[0], parts[1]), rows))

    for index in range(steps):
        pl.when(step == index)(functools.partial(attend, index))

    def finish():
        def fold(chunk, carry):
            rows = pl.ds(pl.multiple_of(chunk * QUERY_ROWS, QUERY_ROWS), QUERY_ROWS)
            d_keys, d_values = dk_ref[rows, :], dv_ref[rows, :]
            d_keys = unrope(d_keys + pltpu.roll(d_keys, HD, 1), rows)
            d_values = d_values + pltpu.roll(d_values, HD, 1)
            out_ref[rows, pairs * 2 * HD :] = low(jnp.where(left, d_keys, d_values))
            return carry

        lax.fori_loop(0, steps, fold, 0)

    pl.when(step == steps - 1)(finish)


def attention_back(query, d_mixed, keys, values, logs, cos, sin, earlier, length):
    every = query.shape[0]
    pair = 2 * HD
    pairs = query.shape[1] // pair
    steps = length // QUERY_ROWS

    def rows(width):
        return pl.BlockSpec((QUERY_ROWS, width), lambda n, b: (n * steps + b, 0))

    def sequence(width):
        return pl.BlockSpec((length, width), lambda n, b: (n, 0))

    table = pl.BlockSpec((length, pair), lambda n, b: (0, 0))
    return pl.pallas_call(
        functools.partial(attention_back_kernel, pairs, steps),
        grid=(every // length, steps),
        out_shape=jax.ShapeDtypeStruct((every, (pairs + 1) * pair), jnp.bfloat16),
        in_specs=[rows(pairs * pair), rows(pairs * pair), sequence(pair), sequence(pair), rows(pair), table, table]
        + anywhere(1),
        out_specs=sequence((pairs + 1) * pair),
        scratch_shapes=[pltpu.VMEM((length, pair), jnp.float32)] * 2,
        compiler_params=pltpu.CompilerParams(vmem_limit_bytes=48 * 2**20),
        cost_estimate=cost(0, 40),
        name="attention_back",
    )(query, d_mixed, keys, values, logs, cos, sin, earlier)


def body(
    inputs,
    cotangent,
    gains,
    gain_moment,
    gain_second,
    w_query,
    w_key,
    w_value,
    w_out,
    w_gate,
    w_up,
    w_down,
    m_query,
    m_key,
    m_value,
    m_out,
    m_gate,
    m_up,
    m_down,
):
    n_ctx = lax.axis_size("ctx_hi") * lax.axis_size("ctx_lo")
    n_lo = lax.axis_size("ctx_lo")
    n_planes = lax.axis_size("z_hi") * lax.axis_size("z_lo")
    ctx, core = lax.axis_index(CTX), lax.axis_index("core")
    plane = lax.axis_index(PLANES)
    halved = n_planes == 4
    ranks = 2 * n_ctx
    tokens = inputs.shape[1]
    length = tokens * n_ctx
    rows_here = w_query.shape[0]
    sharers = ranks // KV
    head_cols = D // ranks
    chip_ff, chip_model = FF // n_ctx, D // n_ctx
    ff_cols = -(-chip_ff // 256) * 128
    transpose_pairs = [(c * n_planes + z, z * n_planes + c) for c in range(n_ctx) for z in range(n_planes)]

    def transposed(values):
        return lax.ppermute(values, CTX + PLANES, transpose_pairs)

    def for_cores(values, first, padded):
        parts = (values[:, :first], values[:, first:])
        return jnp.stack([jnp.pad(part, ((0, 0), (0, padded - part.shape[1]))) for part in parts])

    def own_columns(weight, columns, first, padded):
        part = lax.dynamic_slice_in_dim(weight, ctx * columns, columns, 1)
        return split_cores(for_cores(low(part), first, padded), core).reshape(2 * rows_here, padded)

    def over_planes(values):
        return lax.all_gather(values, PLANES, axis=0, tiled=True)

    key_value = jnp.stack([low(w_key), low(w_value)], 1)
    key_value = lax.all_gather(key_value, PLANES + ("core",), axis=0, tiled=False)
    own_head = lax.dynamic_slice_in_dim(key_value, (2 * ctx + core) // sharers * sharers, sharers, 0)
    wide_kv = jnp.transpose(own_head, (1, 2, 0, 3)).reshape(D, 2 * HD)
    out_part = transposed(low(lax.dynamic_slice_in_dim(w_out, ctx * chip_model, chip_model, 1)))
    own_query = own_columns(w_query, chip_model, head_cols, head_cols)
    wide_both = over_planes(jnp.concatenate([own_query, out_part.T], 1))
    wide_query, wide_out = wide_both[:, :head_cols], wide_both[:, head_cols:]
    wide_qkv = jnp.concatenate([wide_query, wide_kv], 1)
    own_gate = own_columns(w_gate, chip_ff, ff_cols, ff_cols)
    own_up = own_columns(w_up, chip_ff, ff_cols, ff_cols)
    wide_gate_up = over_planes(jnp.concatenate([own_gate, own_up], 1))

    shape = (n_ctx, n_lo)
    every = 2 * length

    def sum_planes(values, dimension=0):
        return lax.psum_scatter(low(values), PLANES, scatter_dimension=dimension, tiled=True)

    cos_table, sin_table = rope_tables(jnp.arange(length, dtype=jnp.float32), HD)
    stream = inputs[0].astype(jnp.float32)
    normed, inverse_one = norm_forward(stream, gains[0])
    all_normed = gather_product(low(normed), [], finish_nothing, [], shape, 1, "gather_normed")[0]
    all_cotangent = gather_product(
        cotangent[0], [], finish_nothing, [], shape, 8, "gather_cotangent", [all_normed]
    )[0]
    wide_down = over_planes(after(own_columns(w_down.T, chip_ff, ff_cols, ff_cols), all_normed))
    mixed_low, query_rot, key_rot, value_low, logs = attention(all_normed, wide_qkv, cos_table, sin_table, length)
    middle = stream + product_scatter([mixed_low], wide_out, term_one, shape, tokens, 2, "scatter_mixed", [all_cotangent])
    normed_two, inverse_two = norm_forward(middle, gains[1])
    all_two, gate_pre, upper, hidden_low = gather_product(
        low(normed_two),
        [wide_gate_up],
        finish_hidden,
        [jax.ShapeDtypeStruct((every, ff_cols), jnp.float32)] * 2
        + [jax.ShapeDtypeStruct((every, ff_cols), jnp.bfloat16)],
        shape,
        3,
        "gather_hidden",
    )
    sigmoid_gate = jax.nn.sigmoid(gate_pre)
    silu_gate = gate_pre * sigmoid_gate
    part_down = low(contract_rows(all_cotangent, hidden_low))
    sum_down = sum_planes(part_down)
    down_sum = product_scatter(
        [hidden_low], wide_down, term_one, shape, tokens, 4, "scatter_hidden", [part_down]
    )
    block_out = low(middle + down_sum)[None]

    d_hidden = matmul(all_cotangent, wide_down)
    d_up = low(d_hidden * silu_gate)
    d_gate = low(d_hidden * upper * sigmoid_gate * (1.0 + gate_pre * (1.0 - sigmoid_gate)))
    part_gate = low(contract_rows(all_two, d_gate))
    part_up = low(contract_rows(all_two, d_up))
    sum_gate, sum_up = sum_planes(part_gate), sum_planes(part_up)
    d_normed_two = product_scatter(
        [d_gate, d_up],
        wide_gate_up,
        term_two,
        shape,
        tokens,
        5,
        "scatter_d_hidden",
        [part_gate, part_up, down_sum, sum_down],
    )
    d_mid_norm, gain_two = norm_backward(middle, inverse_two, gains[1], d_normed_two)
    d_middle = cotangent[0].astype(jnp.float32) + d_mid_norm
    widths = (ff_cols, -(-(chip_ff - ff_cols) // 128) * 128, chip_model)
    grad_down, new_m_down, low_down = momentum(sum_down, m_down, ff_cols, ff_cols, core, flipped=True)
    grad_gate, new_m_gate, low_gate = momentum(sum_gate, m_gate, ff_cols, ff_cols, core)
    all_branch, d_mixed = gather_product(
        low(d_middle),
        [wide_out],
        finish_mixed,
        [jax.ShapeDtypeStruct((every, head_cols), jnp.bfloat16)],
        shape,
        6,
        "gather_d_mixed",
        [sum_gate],
    )
    grad_up, new_m_up, low_up = momentum(sum_up, m_up, ff_cols, ff_cols, core)

    part_out = low(contract_rows(all_branch, mixed_low))
    d_qkv = attention_back(
        query_rot, d_mixed, key_rot, value_low, logs, cos_table, sin_table, part_out, length
    )
    part_qkv = low(contract_rows(all_normed, d_qkv))
    part_all = jnp.concatenate([part_qkv[:, :head_cols], part_out, part_qkv[:, head_cols:]], 1)
    sum_all = sum_planes(part_all)
    d_normed = product_scatter(
        [d_qkv], wide_qkv, term_one, shape, tokens, 7, "scatter_d_project", [part_all, low_up, low_gate, low_down]
    )
    sum_query = sum_all[:, :head_cols]
    grad_rest = transposed(sum_all[:, head_cols:])
    grad_out = grad_rest[:, :head_cols].T.astype(jnp.float32)
    new_m_out = momentum_decay * m_out + grad_out
    slots = [low_gate, low_down, low_up]
    if halved:
        grad_query, new_m_query, low_query = momentum(
            sum_query, m_query, head_cols, head_cols, core, split=False
        )
        pair = jnp.stack([low_query, low(new_m_out)])
    else:
        grad_query, new_m_query, low_query = momentum(sum_query, m_query, head_cols, ff_cols, core)
        slots += [low_query, for_cores(low(new_m_out), head_cols, ff_cols)]
        slots += [jnp.zeros_like(low_gate)] * (n_planes - len(slots))
        pair = jnp.zeros((2, rows_here, chip_model), jnp.bfloat16)
    d_in_norm, gain_one = norm_backward(stream, inverse_one, gains[0], d_normed)
    input_grad = (d_middle + d_in_norm)[None]

    grad_kv = grad_rest[:, head_cols:]
    grad_kv = grad_kv.reshape(-1, 2, n_lo, 2, HD // sharers)
    theirs = swap_core(jnp.where(core == 0, grad_kv[:, :, :, 1], grad_kv[:, :, :, 0]))
    mine = jnp.where(core == 0, grad_kv[:, :, :, 0], grad_kv[:, :, :, 1])
    grad_kv = mine.astype(jnp.float32) + theirs.astype(jnp.float32)
    if n_lo > 1:
        grad_kv = lax.psum_scatter(grad_kv, "z_lo", scatter_dimension=2, tiled=True)
    grad_kv = grad_kv[:, :, 0]
    grad_key, grad_value = grad_kv[:, 0], grad_kv[:, 1]
    new_m_key = momentum_decay * m_key + grad_key
    new_m_value = momentum_decay * m_value + grad_value

    moment_kv = low(jnp.stack([new_m_key.T, new_m_value.T]))
    moment_kv = lax.all_gather(moment_kv, CTX + PLANES + ("core",), axis=0, tiled=False)
    gains_here = jnp.stack([gain_one, gain_two]).reshape(8, -1)
    polar, gain_grad = muon(slots, pair, gains_here, shape + (n_planes, n_lo, halved, widths))
    gain_grad = gain_grad.reshape(gains.shape)
    moment_one = adam_first * gain_moment + (1.0 - adam_first) * gain_grad
    moment_two = adam_second * gain_second + (1.0 - adam_second) * gain_grad * gain_grad
    adam_ratio = (
        moment_one
        / (1.0 - adam_first**STEP)
        / (jnp.sqrt(moment_two / (1.0 - adam_second**STEP)) + adam_eps)
    )
    gains_new = gains - adam_rate * adam_ratio

    new_key, new_value = small_update(
        moment_kv,
        w_key.T,
        w_value.T,
        (n_ctx, 2 * n_planes, n_lo),
        [muon_rate * D ** (-0.5) * math.sqrt(max(D, KV * HD))] * 2,
    )
    new_key, new_value = new_key.T, new_value.T
    half_ctx = n_ctx // 2

    def step_of(spread, widest):
        return muon_rate * spread * math.sqrt(widest)

    def updated(weight, spread, widest, direction):
        return weight * (1.0 - muon_rate * weight_decay) - step_of(spread, widest) * direction

    def in_parts(weight, spread, widest, columns, first, flipped, place):
        parts = 1 if first == columns else 2
        if columns % 128 == 0:
            return update(weight, polar, new_key, step_of(spread, widest), columns, first, flipped, place)
        chips = []
        for chip in range(n_ctx):
            for part in range(parts):
                width = first if part == 0 else columns - first
                chips.append(polar[place(chip, part)][:, :width])
        direction = jnp.concatenate(chips, 1).astype(jnp.float32)
        return updated(weight, spread, widest, direction.T if flipped else direction)

    def ff_update(weight, spread, slot, flipped=False):
        return in_parts(
            weight, spread, max(D, FF), chip_ff, ff_cols, flipped, lambda chip, part: (chip, slot, part)
        )

    def model_update(weight, spread, which):
        if halved:
            return in_parts(
                weight,
                spread,
                D,
                chip_model,
                chip_model,
                False,
                lambda chip, part: (chip % half_ctx + which * half_ctx, n_planes - 1, chip // half_ctx),
            )
        return in_parts(
            weight, spread, D, chip_model, chip_model // 2, False, lambda chip, part: (chip, 3 + which, part)
        )

    new_query = model_update(w_query, D ** (-0.5), 0)
    new_out = model_update(w_out, 32 ** (-0.5), 1)
    new_gate = ff_update(w_gate, D ** (-0.5), 0)
    new_up = ff_update(w_up, D ** (-0.5), 2)
    new_down = ff_update(w_down, FF ** (-0.5), 1, True)
    return (
        block_out,
        input_grad,
        gain_grad,
        moment_one,
        moment_two,
        gains_new,
        grad_query,
        new_m_query,
        new_query,
        grad_key,
        new_m_key,
        new_key,
        grad_value,
        new_m_value,
        new_value,
        grad_out,
        new_m_out,
        new_out,
        grad_gate,
        new_m_gate,
        new_gate,
        grad_up,
        new_m_up,
        new_up,
        grad_down,
        new_m_down,
        new_down,
    )


def solution(mesh):
    n_ctx, n_fsdp = mesh.shape["ctx"], mesh.shape["fsdp"]
    n_lo = 2 * n_ctx // KV // 2
    n_planes = n_fsdp // 2
    finer = Mesh(
        mesh.devices.reshape(n_ctx // n_lo, n_lo, n_planes // n_lo, n_lo, 2),
        CTX + PLANES + ("core",),
    )
    fsdp = PLANES + ("core",)
    tokens, whole = P(fsdp, CTX, None), P()
    rows, columns = P(fsdp, None), P(None, fsdp)
    row_block, column_block = P(fsdp, CTX), P(CTX, fsdp)
    matrix, transposed = (row_block, row_block, rows), (column_block, column_block, columns)
    return jax.shard_map(
        body,
        mesh=finer,
        in_specs=(tokens, tokens, whole, whole, whole)
        + (rows, columns, columns, rows, rows, rows, columns)
        + (row_block, column_block, column_block, row_block, row_block, row_block, column_block),
        out_specs=(tokens, tokens, whole, whole, whole, whole)
        + matrix
        + transposed
        + transposed
        + matrix
        + matrix
        + matrix
        + transposed,
        check_vma=False,
    )
```

```python
import functools
import math

import jax
import jax.numpy as jnp
from jax import lax
from jax.experimental import pallas as pl
from jax.experimental.pallas import tpu as pltpu
from jax.sharding import Mesh
from jax.sharding import PartitionSpec as P

D = 2048
H = 32
KV = 4
HD = 64
FF = 5632
NS = 5
STEP = 10


norm_eps = 1e-05
rope_base = 10000.0
masked_score = -1e30
poly_first = 3.4445
poly_second = -4.775
poly_third = 2.0315
momentum_decay = 0.95
muon_rate = 0.3
weight_decay = 0.1
adam_first = 0.9
adam_second = 0.95
adam_rate = 0.4
adam_eps = 1e-08

MESH = pl.DeviceIdType.MESH
CTX = ("ctx_hi", "ctx_lo")
PLANES = ("z_hi", "z_lo")


def rope_tables(positions, head_width):
    frequency = jnp.exp(
        jnp.arange(head_width // 2, dtype=jnp.float32) * (-2.0 * math.log(rope_base) / head_width)
    )
    angles = positions[:, None] * frequency[None, :]
    cos_half = jnp.cos(angles)
    sin_half = jnp.sin(angles)
    return (jnp.concatenate([cos_half] * 4, -1), jnp.concatenate([-sin_half, sin_half] * 2, -1))


def norm_forward(values, gain_row):
    inverse = lax.rsqrt(jnp.mean(values * values, -1, keepdims=True) + norm_eps)
    return (values * inverse * gain_row, inverse)


def norm_backward(values, inverse, gain_row, gradients):
    scaled = gradients * gain_row
    inner_mean = jnp.mean(scaled * values, -1, keepdims=True)
    return (
        inverse * scaled - values * inverse**3 * inner_mean,
        jnp.sum(gradients * values * inverse, 0),
    )


def matmul(first_op, second_op):
    return jnp.dot(first_op, second_op, preferred_element_type=jnp.float32)


def contract_rows(first_op, second_op):
    return lax.dot_general(
        first_op, second_op, (((0,), (0,)), ((), ())), preferred_element_type=jnp.float32
    )


def contract_cols(first_op, second_op):
    return lax.dot_general(
        first_op, second_op, (((1,), (1,)), ((), ())), preferred_element_type=jnp.float32
    )


def low(values):
    return values.astype(jnp.bfloat16)


class Exchange:
    def __init__(self, shape, sems, half=0, halved=False):
        self.n_ctx, self.n_lo = shape
        self.stages = self.n_ctx.bit_length() - 1
        self.ranks = 2 * self.n_ctx
        self.half, self.halved = half, halved
        self.ctx = lax.axis_index("ctx_hi") * self.n_lo + lax.axis_index("ctx_lo")
        self.core = lax.axis_index("core")
        self.other_core = {"core": 1 - self.core}
        turned = self.core * (1 - half)
        self.deltas = []
        for s in range(1, self.stages + 1):
            step = turned * 2 ** (self.stages - s) + (1 - turned) * 2 ** (s - 1)
            self.deltas.append(step * (1 - 2 * ((self.ctx // step) % 2)))
        (
            self.core_out,
            self.core_in,
            self.ctx_out,
            self.ctx_in,
            self.back_core_out,
            self.back_core_in,
            self.back_out,
            self.back_in,
        ) = sems

    def partner(self, s):
        there = self.ctx + self.deltas[s - 1]
        return {"ctx_hi": there // self.n_lo, "ctx_lo": there % self.n_lo}

    def place(self, other, idx):
        where = self.ctx
        for s in range(1, self.stages + 1):
            where = where + ((idx // 2 ** (self.stages - s)) % 2) * self.deltas[s - 1]
        return 2 * where + self.core + other * (1 - 2 * self.core)

    def across(self, idx):
        mirrored = 0
        for s in range(self.stages):
            mirrored = mirrored + ((idx // 2**s) % 2) * 2 ** (self.stages - 1 - s)
        return self.half * idx + (1 - self.half) * mirrored

    def whole(self, flag, run):
        if self.halved:
            pl.when(self.half == flag)(run)
        elif flag == 0:
            run()

    def greet(self, more=0):
        barrier = pltpu.get_barrier_semaphore()
        pl.semaphore_signal(barrier, inc=1, device_id=self.other_core, device_id_type=MESH)
        for s in range(1, self.stages + 1):
            pl.semaphore_signal(barrier, inc=1, device_id=self.partner(s), device_id_type=MESH)
        pl.semaphore_wait(barrier, 1 + self.stages + more)

    def copy(self, source, target, send, receive, device):
        return pltpu.make_async_remote_copy(
            src_ref=source,
            dst_ref=target,
            send_sem=send,
            recv_sem=receive,
            device_id=device,
            device_id_type=MESH,
        )


    def parts(self, size):
        middle = (size + 1) // 2
        return [(0, middle), (middle, size)]


    def sum_part(self, h):
        low_end, high_end = self.parts(self.part.shape[2])[h]
        return pl.ds(low_end, high_end - low_end)

    def core_copy(self, idx, h):
        slot = self.across(idx)
        span = self.sum_part(h)
        return self.copy(
            self.part.at[1, idx, span],
            self.from_core.at[slot, span],
            self.core_out.at[idx, h],
            self.core_in.at[slot, h],
            self.other_core,
        )

    def core_arrived(self, idx, h):
        span = self.sum_part(h)
        self.copy(
            self.part.at[1, idx, span],
            self.from_core.at[idx, span],
            self.core_out.at[idx, h],
            self.core_in.at[idx, h],
            self.other_core,
        ).wait_recv()

    def ctx_copy(self, s, idx, h):
        span = self.sum_part(h)
        return self.copy(
            self.part.at[0, idx, span],
            self.from_ctx.at[idx, span],
            self.ctx_out.at[idx, h],
            self.ctx_in.at[idx, h],
            self.partner(s),
        )

    def incoming(self, s, idx):
        return idx + 2 ** (self.stages - s)

    def add(self, idx, sources, target, h):
        def one(chunk, carry):
            total = self.part[0, idx, chunk].astype(jnp.float32)
            total = total + self.from_core[idx, chunk].astype(jnp.float32)
            for source in sources:
                total = total + self.from_ctx[source, chunk].astype(jnp.float32)
            target[chunk] = total.astype(target.dtype)
            return carry

        lax.fori_loop(*self.parts(self.part.shape[2])[h], one, 0)

    def sum_pieces(self, part, from_core, from_ctx, make, target):
        self.part, self.from_core, self.from_ctx = part, from_core, from_ctx
        n_ctx, stages = self.n_ctx, self.stages

        def pass_on(idx):
            s = stages + 1 - idx.bit_length()
            for h in range(2):
                self.core_arrived(idx, h)
                for t in range(1, s):
                    self.ctx_copy(t, self.incoming(t, idx), h).wait_recv()
                self.add(idx, [self.incoming(t, idx) for t in range(1, s)], part.at[0, idx], h)
                if s < stages:
                    self.ctx_copy(s, idx, h).start()
                else:
                    self.whole(0, lambda h=h: self.ctx_copy(s, idx, h).start())

        def fill(step, carry):
            idx = n_ctx - 1 - step
            theirs = self.across(idx)
            make(1, theirs)
            for h in range(2):
                self.core_copy(theirs, h).start()
            make(0, idx)
            for early in range(n_ctx // 2, n_ctx):
                pl.when(idx == early)(functools.partial(pass_on, early))
            return carry

        lax.fori_loop(0, n_ctx, fill, 0)
        for idx in range(n_ctx // 2 - 1, 0, -1):
            pass_on(idx)
        early = [self.incoming(t, 0) for t in range(1, stages)]
        for h in range(2):
            self.core_arrived(0, h)
            for t in range(1, stages):
                self.ctx_copy(t, self.incoming(t, 0), h).wait_recv()

            def finish_whole(h=h):
                self.ctx_copy(stages, 1, h).wait_recv()
                self.add(0, early + [1], target, h)

            self.whole(0, finish_whole)
            self.whole(1, lambda h=h: self.add(0, early, target, h))

    def sums_sent(self):
        for h in range(2):
            for idx in range(self.n_ctx):
                self.core_copy(idx, h).wait_send()
            for s in range(1, self.stages + 1):
                upper = 2 ** (self.stages - s)
                for idx in range(upper, 2 * upper):
                    if s < self.stages:
                        self.ctx_copy(s, idx, h).wait_send()
                    else:
                        self.whole(0, lambda s=s, idx=idx, h=h: self.ctx_copy(s, idx, h).wait_send())


    def block(self, rank, h):
        low_end, high_end = self.parts(self.gathered.shape[1])[h]
        return self.gathered.at[rank, pl.ds(low_end, high_end - low_end)]

    def back_copy(self, s, idx, h):
        there = idx + 2 ** (self.stages - s)
        block = self.block(self.place(0, idx), h)
        return self.copy(block, block, self.back_out.at[there, h], self.back_in.at[there, h], self.partner(s))

    def back_core_copy(self, idx, h):
        block = self.block(self.place(0, idx), h)
        return self.copy(
            block, block, self.back_core_out.at[idx, h], self.back_core_in.at[self.across(idx), h], self.other_core
        )

    def announce(self, idx, h):
        for s in range(self.stages, 0, -1):
            if idx < 2 ** (self.stages - s):
                if s < self.stages:
                    self.back_copy(s, idx, h).start()
                else:
                    self.whole(0, lambda s=s: self.back_copy(s, idx, h).start())
        self.back_core_copy(idx, h).start()

    def arrived(self, idx, h):
        block = self.block(self.place(0, idx), h)
        self.copy(block, block, self.back_out.at[idx, h], self.back_in.at[idx, h], self.other_core).wait_recv()

    def core_back_arrived(self, idx, h):
        block = self.block(self.place(1, idx), h)
        self.copy(
            block, block, self.back_core_out.at[idx, h], self.back_core_in.at[idx, h], self.other_core
        ).wait_recv()

    def gather_pieces(self, gathered, use):
        self.gathered = gathered
        for h in range(2):
            self.announce(0, h)

        def visit(step, carry):
            idx, other = step // 2, step % 2

            def on_arrival(v):
                for h in range(2):
                    if v == 1:
                        self.whole(0, lambda h=h: self.arrived(1, h))
                    else:
                        self.arrived(v, h)
                    self.announce(v, h)

            for v in range(1, self.n_ctx):
                pl.when(step == 2 * v)(functools.partial(on_arrival, v))
            idx = (1 - other) * idx + other * self.across(idx)

            def on_core_arrival():
                for h in range(2):
                    self.core_back_arrived(idx, h)

            pl.when(other == 1)(on_core_arrival)
            use(self.place(other, idx), step)
            return carry

        lax.fori_loop(0, 2 * self.n_ctx, visit, 0)

    def gathers_sent(self):
        for h in range(2):
            for idx in range(self.n_ctx):
                self.back_core_copy(idx, h).wait_send()
            for s in range(1, self.stages + 1):
                for idx in range(2 ** (self.stages - s)):
                    if s < self.stages:
                        self.back_copy(s, idx, h).wait_send()
                    else:
                        self.whole(0, lambda s=s, idx=idx, h=h: self.back_copy(s, idx, h).wait_send())


def exchange_sems(n_ctx):
    return [pltpu.SemaphoreType.DMA((n_ctx, 2))] * 8


def muon_kernel(shape, mains, *refs):
    n_ctx, n_lo, n_planes, z_lo, halved, widths = shape
    slot_refs, refs = refs[:mains], refs[mains:]
    pair_ref, gains_ref, out_ref, gains_out_ref = refs[:4]
    x_ref, y_ref, a_ref, part, from_core, from_ctx, both_gathered, landed, scale, strip, near, far = refs[4:16]
    gathered, gathered_beside = both_gathered.at[0], both_gathered.at[1]
    slots_out, pair_out, blocks_in, rows_out, rows_in, spread_out, spread_in, kept = refs[16:24]
    near_out, near_in, far_out, far_in = refs[24:28]
    sems = refs[28:]
    plane = lax.axis_index("z_hi") * z_lo + lax.axis_index("z_lo")
    ex = Exchange((n_ctx, n_lo), sems[:8], plane // (n_planes - 1) if halved else 0, halved)
    ex_beside = Exchange((n_ctx, n_lo), sems[:4] + sems[8:12], ex.half, halved)
    even = Exchange((n_ctx, n_lo), sems[:8])
    ctx, core = ex.ctx, ex.core
    own = 2 * plane + core
    shards = 2 * n_planes
    tall = D // shards
    blocks = ex.ranks
    side = D // blocks
    reach = blocks // 2 + 1
    devices = n_ctx * shards

    def device(at_ctx, at_plane, at_core):
        return {
            "ctx_hi": at_ctx // n_lo,
            "ctx_lo": at_ctx % n_lo,
            "z_hi": at_plane // z_lo,
            "z_lo": at_plane % z_lo,
            "core": at_core,
        }

    least = min(widths) if halved else min(widths[:2])
    if least < x_ref.shape[1]:
        x_ref[:, least:] = jnp.zeros((D, x_ref.shape[1] - least), x_ref.dtype)
    barrier = pltpu.get_barrier_semaphore()
    here = ctx * shards + own

    def greet(offset, carry):
        there = (here + offset) % devices
        shard = there % shards
        pl.semaphore_signal(
            barrier, inc=1, device_id=device(there // shards, shard // 2, shard % 2), device_id_type=MESH
        )
        return carry

    lax.fori_loop(1, devices, greet, 0)
    pl.semaphore_wait(barrier, devices - 1)

    def rows_of(block):
        return pl.ds(pl.multiple_of(block * side, side), side)

    def shard_rows(shard):
        return pl.ds(pl.multiple_of(shard * tall, tall), tall)

    def send(source, target, out_sem, in_sem, at_ctx, at_plane, at_core, begin):
        same = (at_ctx * n_planes + at_plane) * 2 + at_core == here
        far = ex.copy(source, target, out_sem, in_sem, device(at_ctx, at_plane, at_core))
        near = pltpu.make_async_copy(source, target, in_sem)

        def other():
            far.start() if begin else far.wait_send()

        def this():
            if begin:
                near.start()

        pl.when(same)(this)
        pl.when(jnp.logical_not(same))(other)

    def by_width(pair, at_core, run):
        if halved:
            pl.when(pair == 1)(lambda: run(widths[2]))
        for which in range(2):
            pl.when(jnp.logical_and(pair == 0, at_core == which))(functools.partial(run, widths[which]))

    def send_pair(begin):
        for which in range(2):
            send(
                pair_ref.at[which],
                x_ref.at[shard_rows(own), pl.ds(0, widths[2])],
                pair_out.at[which],
                blocks_in.at[own],
                ctx % (n_ctx // 2) + which * (n_ctx // 2),
                n_planes - 1,
                ctx // (n_ctx // 2),
                begin,
            )

    def send_blocks(begin):
        for slot in range(mains):
            for to_core in range(2):
                columns = pl.ds(0, widths[to_core])
                send(
                    slot_refs[slot].at[to_core, :, columns],
                    x_ref.at[shard_rows(own), columns],
                    slots_out.at[slot, to_core],
                    blocks_in.at[own],
                    ctx,
                    slot,
                    to_core,
                    begin,
                )

    def wait_blocks(columns):
        def one(shard, carry):
            target = x_ref.at[shard_rows(shard), pl.ds(0, columns)]
            pltpu.make_async_copy(target, target, blocks_in.at[shard]).wait()
            return carry

        lax.fori_loop(0, shards, one, 0)

    gains = AllSum(ex, n_planes, z_lo, near, far, near_out, near_in, far_out, far_in)
    if halved:
        send_pair(True)
        send_pair(False)
    send_blocks(True)
    gains.begin(gains_ref[...])
    by_width(ex.half, core, wait_blocks)
    send_blocks(False)

    def in_use(run):
        ex.whole(0, lambda: run(slice(0, x_ref.shape[1])))
        ex.whole(1, lambda: run(slice(0, widths[2])))

    def gram_piece(other, idx):
        block = ex.place(other, idx)

        def run(columns):
            left = x_ref[rows_of(block), columns]
            for offset in range(reach):
                right = x_ref[rows_of((block + offset) % blocks), columns]
                part[other, idx, offset] = low(contract_cols(left, right))

        in_use(run)

    def spread(block, step, pieces=gathered):
        del step
        for offset in range(reach):
            column = (block + offset) % blocks
            piece = pieces[block, offset]
            a_ref[rows_of(block), rows_of(column)] = piece
            if 0 < offset < reach - 1:
                a_ref[rows_of(column), rows_of(block)] = piece.T

    def gram():
        ex.sum_pieces(part, from_core, from_ctx, gram_piece, gathered.at[ex.place(0, 0)])

        def second_own():
            def one(offset, inner):
                gathered[ex.place(0, 1), offset] = part[0, 1, offset]
                return inner

            lax.fori_loop(0, reach, one, 0)

        ex.whole(1, second_own)
        ex.gather_pieces(gathered, spread)
        ex.sums_sent()
        ex.gathers_sent()

    high = 512
    halfway = D // high

    def update_step(step):
        factor = scale[0:1, 0:1]

        def first_product(columns):
            rows = pl.ds(pl.multiple_of(step * high, high), high)
            y_ref[rows, columns] = low(matmul(a_ref[rows, :], x_ref[:, columns]) * (factor * factor * factor))

        def second_product(columns):
            rows = pl.ds(pl.multiple_of((step - halfway) * high, high), high)
            second = matmul(a_ref[rows, :], y_ref[:, columns])
            x_ref[rows, columns] = low(
                (poly_first * factor) * x_ref[rows, columns].astype(jnp.float32)
                + poly_second * y_ref[rows, columns].astype(jnp.float32)
                + (poly_third * factor * factor) * second
            )

        pl.when(step < halfway)(lambda: in_use(first_product))
        pl.when(jnp.logical_and(step >= halfway, step < 2 * halfway))(lambda: in_use(second_product))

    def update_all():
        def one(step, carry):
            update_step(step)
            return carry

        lax.fori_loop(0, 2 * halfway, one, 0)

    def norm_now():
        def one(block, total):
            rows = lax.broadcasted_iota(jnp.int32, (side, side), 0)
            cols = lax.broadcasted_iota(jnp.int32, (side, side), 1)
            piece = gathered[block, 0].astype(jnp.float32)
            piece = jnp.where(rows == cols, piece, 0.0)
            return total + jnp.sum(jnp.sum(piece, 0, keepdims=True), 1, keepdims=True)

        trace = lax.fori_loop(0, blocks, one, jnp.zeros((1, 1), jnp.float32))
        scale[...] = jnp.broadcast_to(1.0 / (jnp.sqrt(trace) + 1e-07), scale.shape)

    def norm_done():
        scale[...] = jnp.ones(scale.shape, jnp.float32)

    def next_gram_rows(block):
        factor = scale[0:1, 0:1] * scale[0:1, 0:1]
        wide = 512

        def product(source, target, finish):
            def one(step, carry):
                columns = pl.ds(pl.multiple_of(step * wide, wide), wide)
                strip[target, :, columns] = low(finish(matmul(source(), a_ref[:, columns]), columns))
                return carry

            lax.fori_loop(0, D // wide, one, 0)

        def own_rows(columns=slice(None)):
            return a_ref[rows_of(block), columns]

        product(own_rows, 0, lambda value, columns: value * (factor * factor))
        product(
            lambda: strip[0],
            1,
            lambda value, columns: (poly_first * factor) * own_rows(columns).astype(jnp.float32)
            + poly_second * strip[0, :, columns].astype(jnp.float32)
            + (poly_third * factor) * value,
        )
        product(lambda: strip[1], 0, lambda value, columns: value * factor)

        def last(offset, carry):
            columns = rows_of((block + offset) % blocks)
            value = matmul(strip[0], a_ref[:, columns])
            gathered_beside[block, offset] = low(
                poly_first * strip[1, :, columns].astype(jnp.float32)
                + poly_second * strip[0, :, columns].astype(jnp.float32)
                + (poly_third * factor) * value
            )
            return carry

        lax.fori_loop(0, reach, last, 0)

    def two_sweeps(pair, carry):
        gram()
        pl.when(pair == 0)(norm_now)
        pl.when(pair == 0)(gains.between)
        pl.when(pair > 0)(norm_done)
        next_gram_rows(ex.place(0, 0))

        def update_beside(block, step):
            del block
            pl.when(step == 0)(lambda: ex.whole(1, lambda: next_gram_rows(ex.place(0, 1))))
            update_step(step)

        ex_beside.gather_pieces(gathered_beside, update_beside)
        norm_done()

        def spread_one(block, inner):
            spread(block, 0, gathered_beside)
            return inner

        lax.fori_loop(0, blocks, spread_one, 0)
        update_all()
        ex_beside.gathers_sent()
        return carry

    lax.fori_loop(0, NS // 2, two_sweeps, 0)
    if NS % 2:
        gram()
    per_step = high * n_planes // D

    def send_rows(begin, first, count):
        def run(width):
            columns = pl.ds(0, width)
            for offset in range(count):
                to_plane = first + offset
                for to_core in range(2):
                    shard = 2 * to_plane + to_core
                    send(
                        x_ref.at[shard_rows(shard), columns],
                        landed.at[ctx, plane, core, :, columns],
                        rows_out.at[shard],
                        rows_in.at[own],
                        ctx,
                        to_plane,
                        to_core,
                        begin,
                    )

        by_width(ex.half, core, run)

    def with_width(shard, run):
        by_width(shard // 2 // (n_planes - 1) if halved else 0, shard % 2, run)

    def last_update(step, carry):
        if NS % 2:
            update_step(step)
        pl.when(step >= halfway)(lambda: send_rows(True, (step - halfway) * per_step, per_step))
        return carry

    lax.fori_loop(0, 2 * halfway, last_update, 0)
    gains_out_ref[...] = gains.end()
    stages = even.stages

    def block_of(where, shard, width):
        return (where, shard // 2, shard % 2, slice(None), pl.ds(0, width))

    def spread_copy(s, idx, where, shard, width):
        block = landed.at[block_of(where, shard, width)]
        there = idx + 2 ** (stages - s)
        return even.copy(
            block, block, spread_out.at[there, shard], spread_in.at[there, shard], even.partner(s)
        )

    def keep(where, shard, idx, width):
        place = block_of(where, shard, width)
        return pltpu.make_async_copy(landed.at[place], out_ref.at[place], kept.at[idx, shard])

    def owner(idx):
        return even.place(0, idx) // 2

    def pass_on(idx, shard):
        def run(width):
            block = landed.at[block_of(owner(idx), shard, width)]
            if idx == 0:
                pltpu.make_async_copy(block, block, rows_in.at[shard]).wait()
            else:
                pltpu.make_async_copy(block, block, spread_in.at[idx, shard]).wait()
            for s in range(stages, 0, -1):
                if idx < 2 ** (stages - s):
                    spread_copy(s, idx, owner(idx), shard, width).start()
            keep(owner(idx), shard, idx, width).start()

        with_width(shard, run)

    rounds = n_planes - 1 if halved else n_planes

    def in_order(step):
        turn_of = step // 2
        last = turn_of // rounds
        return 2 * (last * rounds + (1 - last) * ((plane + turn_of) % rounds)) + step % 2

    def arrive(step, carry):
        pl.when(step < shards)(lambda: pass_on(0, in_order(step)))
        for idx in range(1, n_ctx):
            lag = idx.bit_length()
            now = step - lag
            pl.when(jnp.logical_and(now >= 0, now < shards))(
                functools.partial(pass_on, idx, in_order(jnp.maximum(now, 0)))
            )
        return carry

    lax.fori_loop(0, shards + stages, arrive, 0)
    send_rows(False, 0, n_planes)

    def finish(shard, carry):
        def run(width):
            for idx in range(n_ctx):
                keep(owner(idx), shard, idx, width).wait()
                for s in range(stages, 0, -1):
                    if idx < 2 ** (stages - s):
                        spread_copy(s, idx, owner(idx), shard, width).wait_send()

        with_width(shard, run)
        return carry

    lax.fori_loop(0, shards, finish, 0)


def in_vmem(count):
    return [pl.BlockSpec(memory_space=pltpu.VMEM)] * count


def anywhere(count):
    return [pl.BlockSpec(memory_space=pl.ANY)] * count


def cost(flops, micros):
    return pl.CostEstimate(flops=flops, bytes_accessed=int(micros * 3.0e6), transcendentals=0)


def muon(slots, pair, gains, shape):
    n_ctx, _, n_planes = shape[:3]
    rows_here, columns = slots[0].shape[1:]
    blocks = 2 * n_ctx
    side = D // blocks
    piece = (blocks // 2 + 1, side, side)
    dma = pltpu.SemaphoreType.DMA
    landed = (n_ctx, n_planes, 2, rows_here, columns)
    return pl.pallas_call(
        functools.partial(muon_kernel, shape, len(slots)),
        out_shape=[
            jax.ShapeDtypeStruct(landed, jnp.bfloat16),
            jax.ShapeDtypeStruct(gains.shape, jnp.float32),
        ],
        in_specs=anywhere(len(slots) + 1) + in_vmem(1),
        out_specs=anywhere(1) + in_vmem(1),
        scratch_shapes=[
            pltpu.VMEM((D, columns), jnp.bfloat16),
            pltpu.VMEM((D, columns), jnp.bfloat16),
            pltpu.VMEM((D, D), jnp.bfloat16),
            pltpu.VMEM((2, n_ctx) + piece, jnp.bfloat16),
            pltpu.VMEM((n_ctx,) + piece, jnp.bfloat16),
            pltpu.VMEM((n_ctx,) + piece, jnp.bfloat16),
            pltpu.VMEM((2, blocks) + piece, jnp.bfloat16),
            pltpu.VMEM(landed, jnp.bfloat16),
            pltpu.VMEM((8, 128), jnp.float32),
            pltpu.VMEM((2, side, D), jnp.bfloat16),
            pltpu.VMEM((blocks,) + gains.shape, jnp.float32),
            pltpu.VMEM((n_planes,) + gains.shape, jnp.float32),
            dma((len(slots), 2)),
            dma((2,)),
            dma((2 * n_planes,)),
            dma((2 * n_planes,)),
            dma((2 * n_planes,)),
            dma((n_ctx, 2 * n_planes)),
            dma((n_ctx, 2 * n_planes)),
            dma((n_ctx, 2 * n_planes)),
            dma((blocks,)),
            dma((blocks,)),
            dma((n_planes,)),
            dma((n_planes,)),
        ]
        + exchange_sems(n_ctx)
        + [dma((n_ctx, 2))] * 4,
        compiler_params=pltpu.CompilerParams(
            collective_id=0, has_side_effects=True, vmem_limit_bytes=60 * 2**20
        ),
        cost_estimate=cost(NS * 5 * D * D * columns, 350),
        name="muon",
    )(*slots, pair, gains)


def momentum_kernel(first, flipped, split, sum_ref, got_ref, moment_ref, grad_ref, new_ref, low_ref):
    core = lax.axis_index("core")
    tall = got_ref.shape[0]
    mine = sum_ref[pl.ds(pl.multiple_of(core * tall, tall), tall), :].astype(jnp.float32)
    got = got_ref[...].astype(jnp.float32)
    left = jnp.where(core == 0, mine, got)
    right = jnp.where(core == 0, got, mine)
    columns = moment_ref.shape[0 if flipped else 1]
    gradient = jnp.concatenate([left[:, :first], right[:, : columns - first]], 1)
    if flipped:
        grad_ref[...] = gradient.T
        new = momentum_decay * moment_ref[...] + grad_ref[...]
        new_ref[...] = new
        new = new.T
    else:
        grad_ref[...] = gradient
        new = momentum_decay * moment_ref[...] + gradient
        new_ref[...] = new
    if split:
        padded = low_ref.shape[2]
        for index, part in enumerate((low(new[:, :first]), low(new[:, first:]))):
            if part.shape[1] < padded:
                zeros = jnp.zeros((tall, padded - part.shape[1]), jnp.bfloat16)
                part = jnp.concatenate([part, zeros], 1)
            low_ref[index] = part
    else:
        low_ref[...] = low(new)


def momentum(summed, moment, first, padded, core, flipped=False, split=True):
    tall = summed.shape[0] // 2
    got = swap_core(lax.dynamic_slice_in_dim(summed, (1 - core) * tall, tall, 0))
    columns = moment.shape[0 if flipped else 1]
    out = jax.ShapeDtypeStruct(moment.shape, jnp.float32)
    low_shape = (2, tall, padded) if split else (tall, columns)
    return pl.pallas_call(
        functools.partial(momentum_kernel, first, flipped, split),
        out_shape=[out, out, jax.ShapeDtypeStruct(low_shape, jnp.bfloat16)],
        in_specs=in_vmem(3),
        out_specs=in_vmem(3),
        compiler_params=pltpu.CompilerParams(vmem_limit_bytes=48 * 2**20),
        name="momentum",
    )(summed, got, moment)


def small_kernel(shape, steps, moments_ref, key_ref, value_ref, new_key_ref, new_value_ref, x_ref, y_ref, own_ref):
    n_ctx, shards, z_lo = shape
    columns, wide = moments_ref.shape[2:]
    plane = lax.axis_index("z_hi") * z_lo + lax.axis_index("z_lo")
    own = 2 * plane + lax.axis_index("core")
    for which in range(2):
        for ctx in range(n_ctx):
            for shard in range(shards):
                x_ref[which, shard * columns : (shard + 1) * columns, ctx * wide : (ctx + 1) * wide] = moments_ref[
                    ctx * shards + shard, which
                ]
        start = x_ref[which].astype(jnp.float32)
        norm = jnp.sqrt(jnp.sum(jnp.sum(start * start, 0, keepdims=True), 1, keepdims=True))
        x_ref[which] = low(start * (1.0 / (norm + 1e-07)))

    def sweep(index, carry):
        grams = [low(contract_cols(x_ref[which], x_ref[which])) for which in range(2)]
        for which in range(2):
            y_ref[which] = low(matmul(grams[which], x_ref[which]))
        for which in range(2):
            x_ref[which] = low(
                poly_first * x_ref[which].astype(jnp.float32)
                + poly_second * y_ref[which].astype(jnp.float32)
                + poly_third * matmul(grams[which], y_ref[which])
            )
        return carry

    lax.fori_loop(0, NS, sweep, 0)
    for which, (old_ref, new_ref) in enumerate(((key_ref, new_key_ref), (value_ref, new_value_ref))):
        own_ref[...] = x_ref[which, pl.ds(pl.multiple_of(own * columns, columns), columns), :].astype(jnp.float32)
        new_ref[...] = old_ref[...] * (1.0 - muon_rate * weight_decay) - steps[which] * own_ref[...]


def small_update(moments, key, value, shape, steps):
    out = jax.ShapeDtypeStruct(key.shape, jnp.float32)
    return pl.pallas_call(
        functools.partial(small_kernel, shape, steps),
        out_shape=[out, out],
        in_specs=in_vmem(3),
        out_specs=in_vmem(2),
        scratch_shapes=[
            pltpu.VMEM((2, KV * HD, D), jnp.bfloat16),
            pltpu.VMEM((2, KV * HD, D), jnp.bfloat16),
            pltpu.VMEM(key.shape, jnp.float32),
        ],
        compiler_params=pltpu.CompilerParams(vmem_limit_bytes=48 * 2**20),
        cost_estimate=cost(0, 15),
        name="small_update",
    )(moments, key, value)


def update_kernel(step, columns, first, flipped, weight_ref, *refs):
    parts, out_ref = refs[:-2], refs[-1]
    direction = parts[0][...].reshape(parts[0].shape[-2:])[:, :first]
    if len(parts) > 1:
        second = parts[1][...].reshape(parts[1].shape[-2:])[:, : columns - first]
        direction = jnp.concatenate([direction, second], 1)
    direction = direction.astype(jnp.float32)
    if flipped:
        direction = direction.T
    out_ref[...] = weight_ref[...] * (1.0 - muon_rate * weight_decay) - step * direction


def update(weight, polar, earlier, step, columns, first, flipped, place):
    tall, wide = polar.shape[-2:]
    count = weight.shape[0 if flipped else 1] // columns
    if flipped:
        block = pl.BlockSpec((columns, tall), lambda chip: (chip, 0))
    else:
        block = pl.BlockSpec((tall, columns), lambda chip: (0, chip))
    parts = [
        pl.BlockSpec((1, 1, 1, tall, wide), lambda chip, part=part: tuple(place(chip, part)) + (0, 0))
        for part in range(1 if first == columns else 2)
    ]
    return pl.pallas_call(
        functools.partial(update_kernel, step, columns, first, flipped),
        grid=(count,),
        out_shape=jax.ShapeDtypeStruct(weight.shape, jnp.float32),
        in_specs=[block] + parts + anywhere(1),
        out_specs=block,
        compiler_params=pltpu.CompilerParams(vmem_limit_bytes=48 * 2**20),
        name="update",
    )(weight, *([polar] * len(parts)), earlier)


def scatter_kernel(shape, term, n_lhs, n_earlier, *refs):
    lhs, right = refs[:n_lhs], refs[n_lhs]
    refs = refs[n_lhs + 1 + n_earlier :]
    out, part, from_core, from_ctx = refs[:4]
    ex = Exchange(shape, refs[4:])
    ex.greet()
    chunks, tall, wide = out.shape

    def make(other, idx):
        block = ex.place(other, idx)
        start = ((block % 2) * ex.n_ctx + block // 2) * chunks * tall
        rows = pl.ds(pl.multiple_of(start, chunks * tall), chunks * tall)
        total = term([left[rows, :] for left in lhs], right)
        part[other, idx] = low(total).reshape(chunks, tall, wide)

    ex.sum_pieces(part, from_core, from_ctx, make, out)
    ex.sums_sent()


def product_scatter(lhs, right, term, shape, tokens, collective_id, name, earlier=()):
    n_ctx = shape[0]
    piece = (tokens // 32, 32, D)
    flops = sum(2 * a.shape[0] * a.shape[1] * D for a in lhs)
    out = pl.pallas_call(
        functools.partial(scatter_kernel, shape, term, len(lhs), len(earlier)),
        out_shape=jax.ShapeDtypeStruct(piece, jnp.float32),
        in_specs=in_vmem(len(lhs) + 1) + anywhere(len(earlier)),
        out_specs=pl.BlockSpec(memory_space=pltpu.VMEM),
        scratch_shapes=[
            pltpu.VMEM((2, n_ctx) + piece, jnp.bfloat16),
            pltpu.VMEM((n_ctx,) + piece, jnp.bfloat16),
            pltpu.VMEM((n_ctx,) + piece, jnp.bfloat16),
        ]
        + exchange_sems(n_ctx),
        compiler_params=pltpu.CompilerParams(
            collective_id=collective_id, has_side_effects=True, vmem_limit_bytes=56 * 2**20
        ),
        cost_estimate=cost(flops, 40),
        name=name,
    )(*lhs, right, *earlier)
    return out.reshape(tokens, D)


def gather_kernel(shape, finish, n_weights, n_outs, n_earlier, block_ref, *refs):
    weights = refs[:n_weights]
    refs = refs[n_weights + n_earlier :]
    gathered_out, outs = refs[0], refs[1 : 1 + n_outs]
    gathered, out_sems = refs[1 + n_outs : 3 + n_outs]
    ex = Exchange(shape, refs[3 + n_outs :])
    ex.greet()
    tokens = block_ref.shape[0]
    gathered[ex.place(0, 0)] = block_ref[...]

    def keep(block):
        row = (block % 2) * ex.n_ctx + block // 2
        return pltpu.make_async_copy(gathered.at[block], gathered_out.at[row], out_sems.at[block]), row

    def use(block, step):
        del step
        copy, row = keep(block)
        copy.start()
        rows = pl.ds(pl.multiple_of(row * tokens, tokens), tokens)
        finish(rows, gathered[block], weights, outs)

    ex.gather_pieces(gathered, use)
    ex.gathers_sent()
    for block in range(ex.ranks):
        keep(block)[0].wait()


def gather_product(block, weights, finish, outs, shape, collective_id, name, earlier=()):
    tokens = block.shape[0]
    ranks = 2 * shape[0]
    flops = sum(2 * ranks * tokens * w.shape[0] * w.shape[1] for w in weights)
    result = pl.pallas_call(
        functools.partial(gather_kernel, shape, finish, len(weights), len(outs), len(earlier)),
        out_shape=[jax.ShapeDtypeStruct((ranks, tokens, D), jnp.bfloat16)] + outs,
        in_specs=in_vmem(1 + len(weights)) + anywhere(len(earlier)),
        out_specs=anywhere(1) + in_vmem(len(outs)),
        scratch_shapes=[
            pltpu.VMEM((ranks, tokens, D), jnp.bfloat16),
            pltpu.SemaphoreType.DMA((ranks,)),
        ]
        + exchange_sems(shape[0]),
        compiler_params=pltpu.CompilerParams(
            collective_id=collective_id, has_side_effects=True, vmem_limit_bytes=56 * 2**20
        ),
        cost_estimate=cost(flops, 40),
        name=name,
    )(block, *weights, *earlier)
    return [result[0].reshape(ranks * tokens, D)] + list(result[1:])


def finish_nothing(rows, block, weights, outs):
    del rows, block, weights, outs


def finish_hidden(rows, block, weights, outs):
    columns = outs[0].shape[1]
    gate_pre = matmul(block, weights[0][:, :columns])
    outs[0][rows, :] = gate_pre
    upper = matmul(block, weights[0][:, columns:])
    outs[1][rows, :] = upper
    outs[2][rows, :] = low(gate_pre * jax.nn.sigmoid(gate_pre) * upper)


def finish_mixed(rows, block, weights, outs):
    outs[0][rows, :] = low(matmul(block, weights[0][...]))


def term_one(lhs, right):
    return contract_cols(lhs[0], right[...])


def term_two(lhs, right):
    columns = lhs[0].shape[1]
    return contract_cols(lhs[0], right[:, :columns]) + contract_cols(lhs[1], right[:, columns:])


class AllSum:
    def __init__(self, ex, n_planes, z_lo, near, far, near_out, near_in, far_out, far_in):
        self.ex, self.n_planes, self.z_lo = ex, n_planes, z_lo
        self.near, self.far = near, far
        self.near_sems, self.far_sems = (near_out, near_in), (far_out, far_in)
        self.rank = 2 * ex.ctx + ex.core
        self.plane = lax.axis_index("z_hi") * z_lo + lax.axis_index("z_lo")

    def rank_id(self, offset):
        there = (self.rank + offset) % self.ex.ranks
        n_lo = self.ex.n_lo
        return {"ctx_hi": there // 2 // n_lo, "ctx_lo": there // 2 % n_lo, "core": there % 2}

    def plane_id(self, offset):
        there = (self.plane + offset) % self.n_planes
        return {"z_hi": there // self.z_lo, "z_lo": there % self.z_lo}

    def copies(self, slots, own, count, device, sems):
        return [
            self.ex.copy(slots.at[own], slots.at[own], sems[0].at[offset], sems[1].at[own], device(offset))
            for offset in range(1, count)
        ]

    def total(self, slots, own, count, device, sems):
        for offset in range(1, count):
            there = (own + offset) % count
            block = slots.at[there]
            self.ex.copy(block, block, sems[0].at[offset], sems[1].at[there], device(offset)).wait_recv()
        for copy in self.copies(slots, own, count, device, sems):
            copy.wait_send()
        total = slots[0]
        for index in range(1, count):
            total = total + slots[index]
        return total

    def begin(self, value):
        self.near[self.rank] = value
        for copy in self.copies(self.near, self.rank, self.ex.ranks, self.rank_id, self.near_sems):
            copy.start()

    def between(self):
        self.far[self.plane] = self.total(self.near, self.rank, self.ex.ranks, self.rank_id, self.near_sems)
        for copy in self.copies(self.far, self.plane, self.n_planes, self.plane_id, self.far_sems):
            copy.start()

    def end(self):
        return self.total(self.far, self.plane, self.n_planes, self.plane_id, self.far_sems)


def nothing_kernel(*refs):
    del refs


def after(values, *others):
    return pl.pallas_call(
        nothing_kernel,
        out_shape=jax.ShapeDtypeStruct(values.shape, values.dtype),
        in_specs=anywhere(1 + len(others)),
        out_specs=pl.BlockSpec(memory_space=pl.ANY),
        input_output_aliases={0: 0},
        name="after",
    )(values, *others)


def swap_core(values):
    return lax.ppermute(values, "core", [(0, 1), (1, 0)])


def split_cores(values, core):
    mine = jnp.where(core == 0, values[0], values[1])
    theirs = jnp.where(core == 0, values[1], values[0])
    got = swap_core(theirs)
    return jnp.stack([jnp.where(core == 0, mine, got), jnp.where(core == 0, got, mine)])


QUERY_ROWS = 256


def turned_pair(values):
    lane = lax.broadcasted_iota(jnp.int32, values.shape, 1)
    return jnp.where(lane % HD < HD // 2, pltpu.roll(values, 2 * HD - HD // 2, 1), pltpu.roll(values, HD // 2, 1))


def is_visible(start, stop):
    rows = lax.broadcasted_iota(jnp.int32, (QUERY_ROWS, stop), 0) + start
    return lax.broadcasted_iota(jnp.int32, (QUERY_ROWS, stop), 1) <= rows


def attention_kernel(pairs, steps, normed_ref, w_ref, cos_ref, sin_ref, mixed_ref, q_ref, k_ref, v_ref, log_ref):
    step = pl.program_id(1)
    projected = matmul(normed_ref[...], w_ref[...])
    cos, sin = cos_ref[...], sin_ref[...]
    lane = lax.broadcasted_iota(jnp.int32, (QUERY_ROWS, 2 * HD), 1)
    left = lane < HD

    def pair_of(values, pair):
        return values[:, pair * 2 * HD : (pair + 1) * 2 * HD]

    def rope(values):
        return values * cos + turned_pair(values) * sin

    both = pair_of(projected, pairs)
    keys = rope(both)
    rows = pl.ds(pl.multiple_of(step * QUERY_ROWS, QUERY_ROWS), QUERY_ROWS)
    k_ref[rows, :] = low(jnp.where(left, keys, pltpu.roll(keys, HD, 1)))
    v_ref[rows, :] = low(jnp.where(left, pltpu.roll(both, HD, 1), both))
    for pair in range(pairs):
        q_ref[:, pair * 2 * HD : (pair + 1) * 2 * HD] = low(rope(pair_of(projected, pair)))

    def attend(index):
        stop = (index + 1) * QUERY_ROWS
        seen = is_visible(index * QUERY_ROWS, stop)
        logs = jnp.zeros((QUERY_ROWS, 2 * HD), jnp.float32)
        for pair in range(pairs):
            outs = []
            for half in range(2):
                query = jnp.where(left == (half == 0), pair_of(q_ref[...], pair), 0.0)
                scores = contract_cols(low(query), k_ref[:stop, :]) * HD ** (-0.5)
                scores = jnp.where(seen, scores, masked_score)
                top = jnp.max(scores, -1, keepdims=True)
                expo = jnp.exp(scores - top)
                total = jnp.sum(expo, -1, keepdims=True)
                outs.append(matmul(low(expo), v_ref[:stop, :]) / total)
                logs = jnp.where(lane == 2 * pair + half, top + jnp.log(total), logs)
            mixed_ref[:, pair * 2 * HD : (pair + 1) * 2 * HD] = low(jnp.where(left, outs[0], outs[1]))
        log_ref[...] = logs

    for index in range(steps):
        pl.when(step == index)(functools.partial(attend, index))


def attention(normed, weight, cos, sin, length):
    every, columns = normed.shape[0], weight.shape[1]
    pairs = columns // (2 * HD) - 1
    steps = length // QUERY_ROWS
    pair = 2 * HD

    def rows(width):
        return pl.BlockSpec((QUERY_ROWS, width), lambda n, b: (n * steps + b, 0))

    def sequence():
        return pl.BlockSpec((length, pair), lambda n, b: (n, 0))

    table = pl.BlockSpec((QUERY_ROWS, pair), lambda n, b: (b, 0))
    return pl.pallas_call(
        functools.partial(attention_kernel, pairs, steps),
        grid=(every // length, steps),
        out_shape=[
            jax.ShapeDtypeStruct((every, pairs * pair), jnp.bfloat16),
            jax.ShapeDtypeStruct((every, pairs * pair), jnp.bfloat16),
            jax.ShapeDtypeStruct((every, pair), jnp.bfloat16),
            jax.ShapeDtypeStruct((every, pair), jnp.bfloat16),
            jax.ShapeDtypeStruct((every, pair), jnp.float32),
        ],
        in_specs=[rows(D), pl.BlockSpec((D, columns), lambda n, b: (0, 0)), table, table],
        out_specs=[rows(pairs * pair), rows(pairs * pair), sequence(), sequence(), rows(pair)],
        compiler_params=pltpu.CompilerParams(vmem_limit_bytes=48 * 2**20),
        cost_estimate=cost(0, 25),
        name="attention",
    )(normed, weight, cos, sin)


def attention_back_kernel(
    pairs, steps, q_ref, d_ref, k_ref, v_ref, log_ref, cos_ref, sin_ref, earlier_ref, out_ref, dk_ref, dv_ref
):
    del earlier_ref
    step = pl.program_id(1)
    lane = lax.broadcasted_iota(jnp.int32, (QUERY_ROWS, 2 * HD), 1)
    left = lane < HD

    def clear():
        dk_ref[...] = jnp.zeros(dk_ref.shape, jnp.float32)
        dv_ref[...] = jnp.zeros(dv_ref.shape, jnp.float32)

    pl.when(step == 0)(clear)

    def unrope(values, rows):
        return values * cos_ref[rows, :] - turned_pair(values) * sin_ref[rows, :]

    def attend(index):
        stop = (index + 1) * QUERY_ROWS
        rows = slice(index * QUERY_ROWS, stop)
        seen = is_visible(index * QUERY_ROWS, stop)
        for pair in range(pairs):
            at = slice(pair * 2 * HD, (pair + 1) * 2 * HD)
            parts = []
            for half in range(2):
                mine = left == (half == 0)
                query = low(jnp.where(mine, q_ref[:, at], 0.0))
                d_rows = low(jnp.where(mine, d_ref[:, at], 0.0))
                scores = contract_cols(query, k_ref[:stop, :]) * HD ** (-0.5)
                log = jnp.sum(jnp.where(lane == 2 * pair + half, log_ref[...], 0.0), -1, keepdims=True)
                probs = jnp.where(seen, jnp.exp(scores - log), 0.0)
                d_probs = contract_cols(d_rows, v_ref[:stop, :])
                delta = jnp.sum(probs * d_probs, -1, keepdims=True)
                d_scores = low(probs * (d_probs - delta))
                parts.append(matmul(d_scores, k_ref[:stop, :]) * HD ** (-0.5))
                dk_ref[:stop, :] += contract_rows(d_scores, query) * HD ** (-0.5)
                dv_ref[:stop, :] += contract_rows(low(probs), d_rows)
            out_ref[rows, at] = low(unrope(jnp.where(left, parts[0], parts[1]), rows))

    for index in range(steps):
        pl.when(step == index)(functools.partial(attend, index))

    def finish():
        def fold(chunk, carry):
            rows = pl.ds(pl.multiple_of(chunk * QUERY_ROWS, QUERY_ROWS), QUERY_ROWS)
            d_keys, d_values = dk_ref[rows, :], dv_ref[rows, :]
            d_keys = unrope(d_keys + pltpu.roll(d_keys, HD, 1), rows)
            d_values = d_values + pltpu.roll(d_values, HD, 1)
            out_ref[rows, pairs * 2 * HD :] = low(jnp.where(left, d_keys, d_values))
            return carry

        lax.fori_loop(0, steps, fold, 0)

    pl.when(step == steps - 1)(finish)


def attention_back(query, d_mixed, keys, values, logs, cos, sin, earlier, length):
    every = query.shape[0]
    pair = 2 * HD
    pairs = query.shape[1] // pair
    steps = length // QUERY_ROWS

    def rows(width):
        return pl.BlockSpec((QUERY_ROWS, width), lambda n, b: (n * steps + b, 0))

    def sequence(width):
        return pl.BlockSpec((length, width), lambda n, b: (n, 0))

    table = pl.BlockSpec((length, pair), lambda n, b: (0, 0))
    return pl.pallas_call(
        functools.partial(attention_back_kernel, pairs, steps),
        grid=(every // length, steps),
        out_shape=jax.ShapeDtypeStruct((every, (pairs + 1) * pair), jnp.bfloat16),
        in_specs=[rows(pairs * pair), rows(pairs * pair), sequence(pair), sequence(pair), rows(pair), table, table]
        + anywhere(1),
        out_specs=sequence((pairs + 1) * pair),
        scratch_shapes=[pltpu.VMEM((length, pair), jnp.float32)] * 2,
        compiler_params=pltpu.CompilerParams(vmem_limit_bytes=48 * 2**20),
        cost_estimate=cost(0, 40),
        name="attention_back",
    )(query, d_mixed, keys, values, logs, cos, sin, earlier)


def body(
    inputs,
    cotangent,
    gains,
    gain_moment,
    gain_second,
    w_query,
    w_key,
    w_value,
    w_out,
    w_gate,
    w_up,
    w_down,
    m_query,
    m_key,
    m_value,
    m_out,
    m_gate,
    m_up,
    m_down,
):
    n_ctx = lax.axis_size("ctx_hi") * lax.axis_size("ctx_lo")
    n_lo = lax.axis_size("ctx_lo")
    n_planes = lax.axis_size("z_hi") * lax.axis_size("z_lo")
    ctx, core = lax.axis_index(CTX), lax.axis_index("core")
    plane = lax.axis_index(PLANES)
    halved = n_planes == 4
    ranks = 2 * n_ctx
    tokens = inputs.shape[1]
    length = tokens * n_ctx
    rows_here = w_query.shape[0]
    sharers = ranks // KV
    head_cols = D // ranks
    chip_ff, chip_model = FF // n_ctx, D // n_ctx
    ff_cols = -(-chip_ff // 256) * 128
    transpose_pairs = [(c * n_planes + z, z * n_planes + c) for c in range(n_ctx) for z in range(n_planes)]

    def transposed(values):
        return lax.ppermute(values, CTX + PLANES, transpose_pairs)

    def for_cores(values, first, padded):
        parts = (values[:, :first], values[:, first:])
        return jnp.stack([jnp.pad(part, ((0, 0), (0, padded - part.shape[1]))) for part in parts])

    def own_columns(weight, columns, first, padded):
        part = lax.dynamic_slice_in_dim(weight, ctx * columns, columns, 1)
        return split_cores(for_cores(low(part), first, padded), core).reshape(2 * rows_here, padded)

    def over_planes(values):
        return lax.all_gather(values, PLANES, axis=0, tiled=True)

    key_value = jnp.stack([low(w_key), low(w_value)], 1)
    key_value = lax.all_gather(key_value, PLANES + ("core",), axis=0, tiled=False)
    own_head = lax.dynamic_slice_in_dim(key_value, (2 * ctx + core) // sharers * sharers, sharers, 0)
    wide_kv = jnp.transpose(own_head, (1, 2, 0, 3)).reshape(D, 2 * HD)
    out_part = transposed(low(lax.dynamic_slice_in_dim(w_out, ctx * chip_model, chip_model, 1)))
    own_query = own_columns(w_query, chip_model, head_cols, head_cols)
    wide_both = over_planes(jnp.concatenate([own_query, out_part.T], 1))
    wide_query, wide_out = wide_both[:, :head_cols], wide_both[:, head_cols:]
    wide_qkv = jnp.concatenate([wide_query, wide_kv], 1)
    own_gate = own_columns(w_gate, chip_ff, ff_cols, ff_cols)
    own_up = own_columns(w_up, chip_ff, ff_cols, ff_cols)
    wide_gate_up = over_planes(jnp.concatenate([own_gate, own_up], 1))

    shape = (n_ctx, n_lo)
    every = 2 * length

    def sum_planes(values, dimension=0):
        return lax.psum_scatter(low(values), PLANES, scatter_dimension=dimension, tiled=True)

    cos_table, sin_table = rope_tables(jnp.arange(length, dtype=jnp.float32), HD)
    stream = inputs[0].astype(jnp.float32)
    normed, inverse_one = norm_forward(stream, gains[0])
    all_normed = gather_product(low(normed), [], finish_nothing, [], shape, 1, "gather_normed")[0]
    all_cotangent = gather_product(
        cotangent[0], [], finish_nothing, [], shape, 8, "gather_cotangent", [all_normed]
    )[0]
    wide_down = over_planes(after(own_columns(w_down.T, chip_ff, ff_cols, ff_cols), all_normed))
    mixed_low, query_rot, key_rot, value_low, logs = attention(all_normed, wide_qkv, cos_table, sin_table, length)
    middle = stream + product_scatter([mixed_low], wide_out, term_one, shape, tokens, 2, "scatter_mixed", [all_cotangent])
    normed_two, inverse_two = norm_forward(middle, gains[1])
    all_two, gate_pre, upper, hidden_low = gather_product(
        low(normed_two),
        [wide_gate_up],
        finish_hidden,
        [jax.ShapeDtypeStruct((every, ff_cols), jnp.float32)] * 2
        + [jax.ShapeDtypeStruct((every, ff_cols), jnp.bfloat16)],
        shape,
        3,
        "gather_hidden",
    )
    sigmoid_gate = jax.nn.sigmoid(gate_pre)
    silu_gate = gate_pre * sigmoid_gate
    part_down = low(contract_rows(all_cotangent, hidden_low))
    sum_down = sum_planes(part_down)
    down_sum = product_scatter(
        [hidden_low], wide_down, term_one, shape, tokens, 4, "scatter_hidden", [part_down]
    )
    block_out = low(middle + down_sum)[None]

    d_hidden = matmul(all_cotangent, wide_down)
    d_up = low(d_hidden * silu_gate)
    d_gate = low(d_hidden * upper * sigmoid_gate * (1.0 + gate_pre * (1.0 - sigmoid_gate)))
    part_gate = low(contract_rows(all_two, d_gate))
    part_up = low(contract_rows(all_two, d_up))
    sum_gate, sum_up = sum_planes(part_gate), sum_planes(part_up)
    d_normed_two = product_scatter(
        [d_gate, d_up],
        wide_gate_up,
        term_two,
        shape,
        tokens,
        5,
        "scatter_d_hidden",
        [part_gate, part_up, down_sum, sum_down],
    )
    d_mid_norm, gain_two = norm_backward(middle, inverse_two, gains[1], d_normed_two)
    d_middle = cotangent[0].astype(jnp.float32) + d_mid_norm
    widths = (ff_cols, -(-(chip_ff - ff_cols) // 128) * 128, chip_model)
    grad_down, new_m_down, low_down = momentum(sum_down, m_down, ff_cols, ff_cols, core, flipped=True)
    grad_gate, new_m_gate, low_gate = momentum(sum_gate, m_gate, ff_cols, ff_cols, core)
    all_branch, d_mixed = gather_product(
        low(d_middle),
        [wide_out],
        finish_mixed,
        [jax.ShapeDtypeStruct((every, head_cols), jnp.bfloat16)],
        shape,
        6,
        "gather_d_mixed",
        [sum_gate],
    )
    grad_up, new_m_up, low_up = momentum(sum_up, m_up, ff_cols, ff_cols, core)

    part_out = low(contract_rows(all_branch, mixed_low))
    d_qkv = attention_back(
        query_rot, d_mixed, key_rot, value_low, logs, cos_table, sin_table, part_out, length
    )
    part_qkv = low(contract_rows(all_normed, d_qkv))
    part_all = jnp.concatenate([part_qkv[:, :head_cols], part_out, part_qkv[:, head_cols:]], 1)
    sum_all = sum_planes(part_all)
    d_normed = product_scatter(
        [d_qkv], wide_qkv, term_one, shape, tokens, 7, "scatter_d_project", [part_all, low_up, low_gate, low_down]
    )
    sum_query = sum_all[:, :head_cols]
    grad_rest = transposed(sum_all[:, head_cols:])
    grad_out = grad_rest[:, :head_cols].T.astype(jnp.float32)
    new_m_out = momentum_decay * m_out + grad_out
    slots = [low_gate, low_down, low_up]
    if halved:
        grad_query, new_m_query, low_query = momentum(
            sum_query, m_query, head_cols, head_cols, core, split=False
        )
        pair = jnp.stack([low_query, low(new_m_out)])
    else:
        grad_query, new_m_query, low_query = momentum(sum_query, m_query, head_cols, ff_cols, core)
        slots += [low_query, for_cores(low(new_m_out), head_cols, ff_cols)]
        slots += [jnp.zeros_like(low_gate)] * (n_planes - len(slots))
        pair = jnp.zeros((2, rows_here, chip_model), jnp.bfloat16)
    d_in_norm, gain_one = norm_backward(stream, inverse_one, gains[0], d_normed)
    input_grad = (d_middle + d_in_norm)[None]

    grad_kv = grad_rest[:, head_cols:]
    grad_kv = grad_kv.reshape(-1, 2, n_lo, 2, HD // sharers)
    theirs = swap_core(jnp.where(core == 0, grad_kv[:, :, :, 1], grad_kv[:, :, :, 0]))
    mine = jnp.where(core == 0, grad_kv[:, :, :, 0], grad_kv[:, :, :, 1])
    grad_kv = mine.astype(jnp.float32) + theirs.astype(jnp.float32)
    if n_lo > 1:
        grad_kv = lax.psum_scatter(grad_kv, "z_lo", scatter_dimension=2, tiled=True)
    grad_kv = grad_kv[:, :, 0]
    grad_key, grad_value = grad_kv[:, 0], grad_kv[:, 1]
    new_m_key = momentum_decay * m_key + grad_key
    new_m_value = momentum_decay * m_value + grad_value

    moment_kv = low(jnp.stack([new_m_key.T, new_m_value.T]))
    moment_kv = lax.all_gather(moment_kv, CTX + PLANES + ("core",), axis=0, tiled=False)
    gains_here = jnp.stack([gain_one, gain_two]).reshape(8, -1)
    polar, gain_grad = muon(slots, pair, gains_here, shape + (n_planes, n_lo, halved, widths))
    gain_grad = gain_grad.reshape(gains.shape)
    moment_one = adam_first * gain_moment + (1.0 - adam_first) * gain_grad
    moment_two = adam_second * gain_second + (1.0 - adam_second) * gain_grad * gain_grad
    adam_ratio = (
        moment_one
        / (1.0 - adam_first**STEP)
        / (jnp.sqrt(moment_two / (1.0 - adam_second**STEP)) + adam_eps)
    )
    gains_new = gains - adam_rate * adam_ratio

    new_key, new_value = small_update(
        moment_kv,
        w_key.T,
        w_value.T,
        (n_ctx, 2 * n_planes, n_lo),
        [muon_rate * D ** (-0.5) * math.sqrt(max(D, KV * HD))] * 2,
    )
    new_key, new_value = new_key.T, new_value.T
    half_ctx = n_ctx // 2

    def step_of(spread, widest):
        return muon_rate * spread * math.sqrt(widest)

    def updated(weight, spread, widest, direction):
        return weight * (1.0 - muon_rate * weight_decay) - step_of(spread, widest) * direction

    def in_parts(weight, spread, widest, columns, first, flipped, place):
        parts = 1 if first == columns else 2
        if columns % 128 == 0:
            return update(weight, polar, new_key, step_of(spread, widest), columns, first, flipped, place)
        chips = []
        for chip in range(n_ctx):
            for part in range(parts):
                width = first if part == 0 else columns - first
                chips.append(polar[place(chip, part)][:, :width])
        direction = jnp.concatenate(chips, 1).astype(jnp.float32)
        return updated(weight, spread, widest, direction.T if flipped else direction)

    def ff_update(weight, spread, slot, flipped=False):
        return in_parts(
            weight, spread, max(D, FF), chip_ff, ff_cols, flipped, lambda chip, part: (chip, slot, part)
        )

    def model_update(weight, spread, which):
        if halved:
            return in_parts(
                weight,
                spread,
                D,
                chip_model,
                chip_model,
                False,
                lambda chip, part: (chip % half_ctx + which * half_ctx, n_planes - 1, chip // half_ctx),
            )
        return in_parts(
            weight, spread, D, chip_model, chip_model // 2, False, lambda chip, part: (chip, 3 + which, part)
        )

    new_query = model_update(w_query, D ** (-0.5), 0)
    new_out = model_update(w_out, 32 ** (-0.5), 1)
    new_gate = ff_update(w_gate, D ** (-0.5), 0)
    new_up = ff_update(w_up, D ** (-0.5), 2)
    new_down = ff_update(w_down, FF ** (-0.5), 1, True)
    return (
        block_out,
        input_grad,
        gain_grad,
        moment_one,
        moment_two,
        gains_new,
        grad_query,
        new_m_query,
        new_query,
        grad_key,
        new_m_key,
        new_key,
        grad_value,
        new_m_value,
        new_value,
        grad_out,
        new_m_out,
        new_out,
        grad_gate,
        new_m_gate,
        new_gate,
        grad_up,
        new_m_up,
        new_up,
        grad_down,
        new_m_down,
        new_down,
    )


def solution(mesh):
    n_ctx, n_fsdp = mesh.shape["ctx"], mesh.shape["fsdp"]
    n_lo = 2 * n_ctx // KV // 2
    n_planes = n_fsdp // 2
    finer = Mesh(
        mesh.devices.reshape(n_ctx // n_lo, n_lo, n_planes // n_lo, n_lo, 2),
        CTX + PLANES + ("core",),
    )
    fsdp = PLANES + ("core",)
    tokens, whole = P(fsdp, CTX, None), P()
    rows, columns = P(fsdp, None), P(None, fsdp)
    row_block, column_block = P(fsdp, CTX), P(CTX, fsdp)
    matrix, transposed = (row_block, row_block, rows), (column_block, column_block, columns)
    return jax.shard_map(
        body,
        mesh=finer,
        in_specs=(tokens, tokens, whole, whole, whole)
        + (rows, columns, columns, rows, rows, rows, columns)
        + (row_block, column_block, column_block, row_block, row_block, row_block, column_block),
        out_specs=(tokens, tokens, whole, whole, whole, whole)
        + matrix
        + transposed
        + transposed
        + matrix
        + matrix
        + matrix
        + transposed,
        check_vma=False,
    )
```

```python
import functools
import math

import jax
import jax.numpy as jnp
from jax import lax
from jax.experimental import pallas as pl
from jax.experimental.pallas import tpu as pltpu
from jax.sharding import Mesh
from jax.sharding import PartitionSpec as P

D = 2048
H = 32
KV = 4
HD = 64
FF = 5632
NS = 5
STEP = 10


norm_eps = 1e-05
rope_base = 10000.0
masked_score = -1e30
poly_first = 3.4445
poly_second = -4.775
poly_third = 2.0315
momentum_decay = 0.95
muon_rate = 0.3
weight_decay = 0.1
adam_first = 0.9
adam_second = 0.95
adam_rate = 0.4
adam_eps = 1e-08

MESH = pl.DeviceIdType.MESH
CTX = ("ctx_hi", "ctx_lo")
PLANES = ("z_hi", "z_lo")


def rope_tables(positions, head_width):
    frequency = jnp.exp(
        jnp.arange(head_width // 2, dtype=jnp.float32) * (-2.0 * math.log(rope_base) / head_width)
    )
    angles = positions[:, None] * frequency[None, :]
    cos_half = jnp.cos(angles)
    sin_half = jnp.sin(angles)
    return (jnp.concatenate([cos_half] * 4, -1), jnp.concatenate([-sin_half, sin_half] * 2, -1))


def norm_forward(values, gain_row):
    inverse = lax.rsqrt(jnp.mean(values * values, -1, keepdims=True) + norm_eps)
    return (values * inverse * gain_row, inverse)


def norm_backward(values, inverse, gain_row, gradients):
    scaled = gradients * gain_row
    inner_mean = jnp.mean(scaled * values, -1, keepdims=True)
    return (
        inverse * scaled - values * inverse**3 * inner_mean,
        jnp.sum(gradients * values * inverse, 0),
    )


def matmul(first_op, second_op):
    return jnp.dot(first_op, second_op, preferred_element_type=jnp.float32)


def contract_rows(first_op, second_op):
    return lax.dot_general(
        first_op, second_op, (((0,), (0,)), ((), ())), preferred_element_type=jnp.float32
    )


def contract_cols(first_op, second_op):
    return lax.dot_general(
        first_op, second_op, (((1,), (1,)), ((), ())), preferred_element_type=jnp.float32
    )


def low(values):
    return values.astype(jnp.bfloat16)


class Exchange:
    def __init__(self, shape, sems, half=0, halved=False):
        self.n_ctx, self.n_lo = shape
        self.stages = self.n_ctx.bit_length() - 1
        self.ranks = 2 * self.n_ctx
        self.half, self.halved = half, halved
        self.ctx = lax.axis_index("ctx_hi") * self.n_lo + lax.axis_index("ctx_lo")
        self.core = lax.axis_index("core")
        self.other_core = {"core": 1 - self.core}
        turned = self.core * (1 - half)
        self.deltas = []
        for s in range(1, self.stages + 1):
            step = turned * 2 ** (self.stages - s) + (1 - turned) * 2 ** (s - 1)
            self.deltas.append(step * (1 - 2 * ((self.ctx // step) % 2)))
        (
            self.core_out,
            self.core_in,
            self.ctx_out,
            self.ctx_in,
            self.back_core_out,
            self.back_core_in,
            self.back_out,
            self.back_in,
        ) = sems

    def partner(self, s):
        there = self.ctx + self.deltas[s - 1]
        return {"ctx_hi": there // self.n_lo, "ctx_lo": there % self.n_lo}

    def place(self, other, idx):
        where = self.ctx
        for s in range(1, self.stages + 1):
            where = where + ((idx // 2 ** (self.stages - s)) % 2) * self.deltas[s - 1]
        return 2 * where + self.core + other * (1 - 2 * self.core)

    def across(self, idx):
        mirrored = 0
        for s in range(self.stages):
            mirrored = mirrored + ((idx // 2**s) % 2) * 2 ** (self.stages - 1 - s)
        return self.half * idx + (1 - self.half) * mirrored

    def whole(self, flag, run):
        if self.halved:
            pl.when(self.half == flag)(run)
        elif flag == 0:
            run()

    def greet(self, more=0):
        barrier = pltpu.get_barrier_semaphore()
        pl.semaphore_signal(barrier, inc=1, device_id=self.other_core, device_id_type=MESH)
        for s in range(1, self.stages + 1):
            pl.semaphore_signal(barrier, inc=1, device_id=self.partner(s), device_id_type=MESH)
        pl.semaphore_wait(barrier, 1 + self.stages + more)

    def copy(self, source, target, send, receive, device):
        return pltpu.make_async_remote_copy(
            src_ref=source,
            dst_ref=target,
            send_sem=send,
            recv_sem=receive,
            device_id=device,
            device_id_type=MESH,
        )


    def parts(self, size):
        middle = (size + 1) // 2
        return [(0, middle), (middle, size)]


    def sum_part(self, h):
        low_end, high_end = self.parts(self.part.shape[2])[h]
        return pl.ds(low_end, high_end - low_end)

    def core_copy(self, idx, h):
        slot = self.across(idx)
        span = self.sum_part(h)
        return self.copy(
            self.part.at[1, idx, span],
            self.from_core.at[slot, span],
            self.core_out.at[idx, h],
            self.core_in.at[slot, h],
            self.other_core,
        )

    def core_arrived(self, idx, h):
        span = self.sum_part(h)
        self.copy(
            self.part.at[1, idx, span],
            self.from_core.at[idx, span],
            self.core_out.at[idx, h],
            self.core_in.at[idx, h],
            self.other_core,
        ).wait_recv()

    def ctx_copy(self, s, idx, h):
        span = self.sum_part(h)
        return self.copy(
            self.part.at[0, idx, span],
            self.from_ctx.at[idx, span],
            self.ctx_out.at[idx, h],
            self.ctx_in.at[idx, h],
            self.partner(s),
        )

    def incoming(self, s, idx):
        return idx + 2 ** (self.stages - s)

    def add(self, idx, sources, target, h):
        def one(chunk, carry):
            total = self.part[0, idx, chunk].astype(jnp.float32)
            total = total + self.from_core[idx, chunk].astype(jnp.float32)
            for source in sources:
                total = total + self.from_ctx[source, chunk].astype(jnp.float32)
            target[chunk] = total.astype(target.dtype)
            return carry

        lax.fori_loop(*self.parts(self.part.shape[2])[h], one, 0)

    def sum_pieces(self, part, from_core, from_ctx, make, target):
        self.part, self.from_core, self.from_ctx = part, from_core, from_ctx
        n_ctx, stages = self.n_ctx, self.stages

        def pass_on(idx):
            s = stages + 1 - idx.bit_length()
            for h in range(2):
                self.core_arrived(idx, h)
                for t in range(1, s):
                    self.ctx_copy(t, self.incoming(t, idx), h).wait_recv()
                self.add(idx, [self.incoming(t, idx) for t in range(1, s)], part.at[0, idx], h)
                if s < stages:
                    self.ctx_copy(s, idx, h).start()
                else:
                    self.whole(0, lambda h=h: self.ctx_copy(s, idx, h).start())

        def fill(step, carry):
            idx = n_ctx - 1 - step
            theirs = self.across(idx)
            make(1, theirs)
            for h in range(2):
                self.core_copy(theirs, h).start()
            make(0, idx)
            for early in range(n_ctx // 2, n_ctx):
                pl.when(idx == early)(functools.partial(pass_on, early))
            return carry

        lax.fori_loop(0, n_ctx, fill, 0)
        for idx in range(n_ctx // 2 - 1, 0, -1):
            pass_on(idx)
        early = [self.incoming(t, 0) for t in range(1, stages)]
        for h in range(2):
            self.core_arrived(0, h)
            for t in range(1, stages):
                self.ctx_copy(t, self.incoming(t, 0), h).wait_recv()

            def finish_whole(h=h):
                self.ctx_copy(stages, 1, h).wait_recv()
                self.add(0, early + [1], target, h)

            self.whole(0, finish_whole)
            self.whole(1, lambda h=h: self.add(0, early, target, h))

    def sums_sent(self):
        for h in range(2):
            for idx in range(self.n_ctx):
                self.core_copy(idx, h).wait_send()
            for s in range(1, self.stages + 1):
                upper = 2 ** (self.stages - s)
                for idx in range(upper, 2 * upper):
                    if s < self.stages:
                        self.ctx_copy(s, idx, h).wait_send()
                    else:
                        self.whole(0, lambda s=s, idx=idx, h=h: self.ctx_copy(s, idx, h).wait_send())


    def block(self, rank, h):
        low_end, high_end = self.parts(self.gathered.shape[1])[h]
        return self.gathered.at[rank, pl.ds(low_end, high_end - low_end)]

    def back_copy(self, s, idx, h):
        there = idx + 2 ** (self.stages - s)
        block = self.block(self.place(0, idx), h)
        return self.copy(block, block, self.back_out.at[there, h], self.back_in.at[there, h], self.partner(s))

    def back_core_copy(self, idx, h):
        block = self.block(self.place(0, idx), h)
        return self.copy(
            block, block, self.back_core_out.at[idx, h], self.back_core_in.at[self.across(idx), h], self.other_core
        )

    def announce(self, idx, h):
        for s in range(self.stages, 0, -1):
            if idx < 2 ** (self.stages - s):
                if s < self.stages:
                    self.back_copy(s, idx, h).start()
                else:
                    self.whole(0, lambda s=s: self.back_copy(s, idx, h).start())
        self.back_core_copy(idx, h).start()

    def arrived(self, idx, h):
        block = self.block(self.place(0, idx), h)
        self.copy(block, block, self.back_out.at[idx, h], self.back_in.at[idx, h], self.other_core).wait_recv()

    def core_back_arrived(self, idx, h):
        block = self.block(self.place(1, idx), h)
        self.copy(
            block, block, self.back_core_out.at[idx, h], self.back_core_in.at[idx, h], self.other_core
        ).wait_recv()

    def gather_pieces(self, gathered, use):
        self.gathered = gathered
        for h in range(2):
            self.announce(0, h)

        def visit(step, carry):
            idx, other = step // 2, step % 2

            def on_arrival(v):
                for h in range(2):
                    if v == 1:
                        self.whole(0, lambda h=h: self.arrived(1, h))
                    else:
                        self.arrived(v, h)
                    self.announce(v, h)

            for v in range(1, self.n_ctx):
                pl.when(step == 2 * v)(functools.partial(on_arrival, v))
            idx = (1 - other) * idx + other * self.across(idx)

            def on_core_arrival():
                for h in range(2):
                    self.core_back_arrived(idx, h)

            pl.when(other == 1)(on_core_arrival)
            use(self.place(other, idx), step)
            return carry

        lax.fori_loop(0, 2 * self.n_ctx, visit, 0)

    def gathers_sent(self):
        for h in range(2):
            for idx in range(self.n_ctx):
                self.back_core_copy(idx, h).wait_send()
            for s in range(1, self.stages + 1):
                for idx in range(2 ** (self.stages - s)):
                    if s < self.stages:
                        self.back_copy(s, idx, h).wait_send()
                    else:
                        self.whole(0, lambda s=s, idx=idx, h=h: self.back_copy(s, idx, h).wait_send())


def exchange_sems(n_ctx):
    return [pltpu.SemaphoreType.DMA((n_ctx, 2))] * 8


def muon_kernel(shape, mains, *refs):
    n_ctx, n_lo, n_planes, z_lo, halved, widths = shape
    slot_refs, refs = refs[:mains], refs[mains:]
    pair_ref, gains_ref, out_ref, gains_out_ref = refs[:4]
    x_ref, y_ref, a_ref, part, from_core, from_ctx, both_gathered, landed, scale, strip, near, far = refs[4:16]
    gathered, gathered_beside = both_gathered.at[0], both_gathered.at[1]
    slots_out, pair_out, blocks_in, rows_out, rows_in, spread_out, spread_in, kept = refs[16:24]
    near_out, near_in, far_out, far_in = refs[24:28]
    sems = refs[28:]
    plane = lax.axis_index("z_hi") * z_lo + lax.axis_index("z_lo")
    ex = Exchange((n_ctx, n_lo), sems[:8], plane // (n_planes - 1) if halved else 0, halved)
    ex_beside = Exchange((n_ctx, n_lo), sems[:4] + sems[8:12], ex.half, halved)
    even = Exchange((n_ctx, n_lo), sems[:8])
    ctx, core = ex.ctx, ex.core
    own = 2 * plane + core
    shards = 2 * n_planes
    tall = D // shards
    blocks = ex.ranks
    side = D // blocks
    reach = blocks // 2 + 1
    devices = n_ctx * shards

    def device(at_ctx, at_plane, at_core):
        return {
            "ctx_hi": at_ctx // n_lo,
            "ctx_lo": at_ctx % n_lo,
            "z_hi": at_plane // z_lo,
            "z_lo": at_plane % z_lo,
            "core": at_core,
        }

    least = min(widths) if halved else min(widths[:2])
    if least < x_ref.shape[1]:
        x_ref[:, least:] = jnp.zeros((D, x_ref.shape[1] - least), x_ref.dtype)
    barrier = pltpu.get_barrier_semaphore()
    here = ctx * shards + own

    def greet(offset, carry):
        there = (here + offset) % devices
        shard = there % shards
        pl.semaphore_signal(
            barrier, inc=1, device_id=device(there // shards, shard // 2, shard % 2), device_id_type=MESH
        )
        return carry

    lax.fori_loop(1, devices, greet, 0)
    pl.semaphore_wait(barrier, devices - 1)

    def rows_of(block):
        return pl.ds(pl.multiple_of(block * side, side), side)

    def shard_rows(shard):
        return pl.ds(pl.multiple_of(shard * tall, tall), tall)

    def send(source, target, out_sem, in_sem, at_ctx, at_plane, at_core, begin):
        same = (at_ctx * n_planes + at_plane) * 2 + at_core == here
        far = ex.copy(source, target, out_sem, in_sem, device(at_ctx, at_plane, at_core))
        near = pltpu.make_async_copy(source, target, in_sem)

        def other():
            far.start() if begin else far.wait_send()

        def this():
            if begin:
                near.start()

        pl.when(same)(this)
        pl.when(jnp.logical_not(same))(other)

    def by_width(pair, at_core, run):
        if halved:
            pl.when(pair == 1)(lambda: run(widths[2]))
        for which in range(2):
            pl.when(jnp.logical_and(pair == 0, at_core == which))(functools.partial(run, widths[which]))

    def send_pair(begin):
        for which in range(2):
            send(
                pair_ref.at[which],
                x_ref.at[shard_rows(own), pl.ds(0, widths[2])],
                pair_out.at[which],
                blocks_in.at[own],
                ctx % (n_ctx // 2) + which * (n_ctx // 2),
                n_planes - 1,
                ctx // (n_ctx // 2),
                begin,
            )

    def send_blocks(begin):
        for slot in range(mains):
            for to_core in range(2):
                columns = pl.ds(0, widths[to_core])
                send(
                    slot_refs[slot].at[to_core, :, columns],
                    x_ref.at[shard_rows(own), columns],
                    slots_out.at[slot, to_core],
                    blocks_in.at[own],
                    ctx,
                    slot,
                    to_core,
                    begin,
                )

    def wait_blocks(columns):
        def one(shard, carry):
            target = x_ref.at[shard_rows(shard), pl.ds(0, columns)]
            pltpu.make_async_copy(target, target, blocks_in.at[shard]).wait()
            return carry

        lax.fori_loop(0, shards, one, 0)

    gains = AllSum(ex, n_planes, z_lo, near, far, near_out, near_in, far_out, far_in)
    if halved:
        send_pair(True)
        send_pair(False)
    send_blocks(True)
    gains.begin(gains_ref[...])
    by_width(ex.half, core, wait_blocks)
    send_blocks(False)

    def in_use(run):
        ex.whole(0, lambda: run(slice(0, x_ref.shape[1])))
        ex.whole(1, lambda: run(slice(0, widths[2])))

    def gram_piece(other, idx):
        block = ex.place(other, idx)

        def run(columns):
            left = x_ref[rows_of(block), columns]
            for offset in range(reach):
                right = x_ref[rows_of((block + offset) % blocks), columns]
                part[other, idx, offset] = low(contract_cols(left, right))

        in_use(run)

    def spread(block, step, pieces=gathered):
        del step
        for offset in range(reach):
            column = (block + offset) % blocks
            piece = pieces[block, offset]
            a_ref[rows_of(block), rows_of(column)] = piece
            if 0 < offset < reach - 1:
                a_ref[rows_of(column), rows_of(block)] = piece.T

    def gram():
        ex.sum_pieces(part, from_core, from_ctx, gram_piece, gathered.at[ex.place(0, 0)])

        def second_own():
            def one(offset, inner):
                gathered[ex.place(0, 1), offset] = part[0, 1, offset]
                return inner

            lax.fori_loop(0, reach, one, 0)

        ex.whole(1, second_own)
        ex.gather_pieces(gathered, spread)
        ex.sums_sent()
        ex.gathers_sent()

    high = 512
    halfway = D // high

    def update_step(step):
        factor = scale[0:1, 0:1]

        def first_product(columns):
            rows = pl.ds(pl.multiple_of(step * high, high), high)
            y_ref[rows, columns] = low(matmul(a_ref[rows, :], x_ref[:, columns]) * (factor * factor * factor))

        def second_product(columns):
            rows = pl.ds(pl.multiple_of((step - halfway) * high, high), high)
            second = matmul(a_ref[rows, :], y_ref[:, columns])
            x_ref[rows, columns] = low(
                (poly_first * factor) * x_ref[rows, columns].astype(jnp.float32)
                + poly_second * y_ref[rows, columns].astype(jnp.float32)
                + (poly_third * factor * factor) * second
            )

        pl.when(step < halfway)(lambda: in_use(first_product))
        pl.when(jnp.logical_and(step >= halfway, step < 2 * halfway))(lambda: in_use(second_product))

    def update_all():
        def one(step, carry):
            update_step(step)
            return carry

        lax.fori_loop(0, 2 * halfway, one, 0)

    def norm_now():
        def one(block, total):
            rows = lax.broadcasted_iota(jnp.int32, (side, side), 0)
            cols = lax.broadcasted_iota(jnp.int32, (side, side), 1)
            piece = gathered[block, 0].astype(jnp.float32)
            piece = jnp.where(rows == cols, piece, 0.0)
            return total + jnp.sum(jnp.sum(piece, 0, keepdims=True), 1, keepdims=True)

        trace = lax.fori_loop(0, blocks, one, jnp.zeros((1, 1), jnp.float32))
        scale[...] = jnp.broadcast_to(1.0 / (jnp.sqrt(trace) + 1e-07), scale.shape)

    def norm_done():
        scale[...] = jnp.ones(scale.shape, jnp.float32)

    def next_gram_rows(block):
        factor = scale[0:1, 0:1] * scale[0:1, 0:1]
        wide = 512

        def product(source, target, finish):
            def one(step, carry):
                columns = pl.ds(pl.multiple_of(step * wide, wide), wide)
                strip[target, :, columns] = low(finish(matmul(source(), a_ref[:, columns]), columns))
                return carry

            lax.fori_loop(0, D // wide, one, 0)

        def own_rows(columns=slice(None)):
            return a_ref[rows_of(block), columns]

        product(own_rows, 0, lambda value, columns: value * (factor * factor))
        product(
            lambda: strip[0],
            1,
            lambda value, columns: (poly_first * factor) * own_rows(columns).astype(jnp.float32)
            + poly_second * strip[0, :, columns].astype(jnp.float32)
            + (poly_third * factor) * value,
        )
        product(lambda: strip[1], 0, lambda value, columns: value * factor)

        def last(offset, carry):
            columns = rows_of((block + offset) % blocks)
            value = matmul(strip[0], a_ref[:, columns])
            gathered_beside[block, offset] = low(
                poly_first * strip[1, :, columns].astype(jnp.float32)
                + poly_second * strip[0, :, columns].astype(jnp.float32)
                + (poly_third * factor) * value
            )
            return carry

        lax.fori_loop(0, reach, last, 0)

    def two_sweeps(pair, carry):
        gram()
        pl.when(pair == 0)(norm_now)
        pl.when(pair == 0)(gains.between)
        pl.when(pair > 0)(norm_done)
        next_gram_rows(ex.place(0, 0))

        def update_beside(block, step):
            del block
            pl.when(step == 0)(lambda: ex.whole(1, lambda: next_gram_rows(ex.place(0, 1))))
            update_step(step)

        ex_beside.gather_pieces(gathered_beside, update_beside)
        norm_done()

        def spread_one(block, inner):
            spread(block, 0, gathered_beside)
            return inner

        lax.fori_loop(0, blocks, spread_one, 0)
        update_all()
        ex_beside.gathers_sent()
        return carry

    lax.fori_loop(0, NS // 2, two_sweeps, 0)
    if NS % 2:
        gram()
    per_step = high * n_planes // D

    def send_rows(begin, first, count):
        def run(width):
            columns = pl.ds(0, width)
            for offset in range(count):
                to_plane = first + offset
                for to_core in range(2):
                    shard = 2 * to_plane + to_core
                    send(
                        x_ref.at[shard_rows(shard), columns],
                        landed.at[ctx, plane, core, :, columns],
                        rows_out.at[shard],
                        rows_in.at[own],
                        ctx,
                        to_plane,
                        to_core,
                        begin,
                    )

        by_width(ex.half, core, run)

    def with_width(shard, run):
        by_width(shard // 2 // (n_planes - 1) if halved else 0, shard % 2, run)

    def last_update(step, carry):
        if NS % 2:
            update_step(step)
        pl.when(step >= halfway)(lambda: send_rows(True, (step - halfway) * per_step, per_step))
        return carry

    lax.fori_loop(0, 2 * halfway, last_update, 0)
    gains_out_ref[...] = gains.end()
    stages = even.stages

    def block_of(where, shard, width):
        return (where, shard // 2, shard % 2, slice(None), pl.ds(0, width))

    def spread_copy(s, idx, where, shard, width):
        block = landed.at[block_of(where, shard, width)]
        there = idx + 2 ** (stages - s)
        return even.copy(
            block, block, spread_out.at[there, shard], spread_in.at[there, shard], even.partner(s)
        )

    def keep(where, shard, idx, width):
        place = block_of(where, shard, width)
        return pltpu.make_async_copy(landed.at[place], out_ref.at[place], kept.at[idx, shard])

    def owner(idx):
        return even.place(0, idx) // 2

    def pass_on(idx, shard):
        def run(width):
            block = landed.at[block_of(owner(idx), shard, width)]
            if idx == 0:
                pltpu.make_async_copy(block, block, rows_in.at[shard]).wait()
            else:
                pltpu.make_async_copy(block, block, spread_in.at[idx, shard]).wait()
            for s in range(stages, 0, -1):
                if idx < 2 ** (stages - s):
                    spread_copy(s, idx, owner(idx), shard, width).start()
            keep(owner(idx), shard, idx, width).start()

        with_width(shard, run)

    rounds = n_planes - 1 if halved else n_planes

    def in_order(step):
        turn_of = step // 2
        last = turn_of // rounds
        return 2 * (last * rounds + (1 - last) * ((plane + turn_of) % rounds)) + step % 2

    def arrive(step, carry):
        pl.when(step < shards)(lambda: pass_on(0, in_order(step)))
        for idx in range(1, n_ctx):
            lag = idx.bit_length()
            now = step - lag
            pl.when(jnp.logical_and(now >= 0, now < shards))(
                functools.partial(pass_on, idx, in_order(jnp.maximum(now, 0)))
            )
        return carry

    lax.fori_loop(0, shards + stages, arrive, 0)
    send_rows(False, 0, n_planes)

    def finish(shard, carry):
        def run(width):
            for idx in range(n_ctx):
                keep(owner(idx), shard, idx, width).wait()
                for s in range(stages, 0, -1):
                    if idx < 2 ** (stages - s):
                        spread_copy(s, idx, owner(idx), shard, width).wait_send()

        with_width(shard, run)
        return carry

    lax.fori_loop(0, shards, finish, 0)


def in_vmem(count):
    return [pl.BlockSpec(memory_space=pltpu.VMEM)] * count


def anywhere(count):
    return [pl.BlockSpec(memory_space=pl.ANY)] * count


def cost(flops, micros):
    return pl.CostEstimate(flops=flops, bytes_accessed=int(micros * 3.0e6), transcendentals=0)


def muon(slots, pair, gains, shape):
    n_ctx, _, n_planes = shape[:3]
    rows_here, columns = slots[0].shape[1:]
    blocks = 2 * n_ctx
    side = D // blocks
    piece = (blocks // 2 + 1, side, side)
    dma = pltpu.SemaphoreType.DMA
    landed = (n_ctx, n_planes, 2, rows_here, columns)
    return pl.pallas_call(
        functools.partial(muon_kernel, shape, len(slots)),
        out_shape=[
            jax.ShapeDtypeStruct(landed, jnp.bfloat16),
            jax.ShapeDtypeStruct(gains.shape, jnp.float32),
        ],
        in_specs=anywhere(len(slots) + 1) + in_vmem(1),
        out_specs=anywhere(1) + in_vmem(1),
        scratch_shapes=[
            pltpu.VMEM((D, columns), jnp.bfloat16),
            pltpu.VMEM((D, columns), jnp.bfloat16),
            pltpu.VMEM((D, D), jnp.bfloat16),
            pltpu.VMEM((2, n_ctx) + piece, jnp.bfloat16),
            pltpu.VMEM((n_ctx,) + piece, jnp.bfloat16),
            pltpu.VMEM((n_ctx,) + piece, jnp.bfloat16),
            pltpu.VMEM((2, blocks) + piece, jnp.bfloat16),
            pltpu.VMEM(landed, jnp.bfloat16),
            pltpu.VMEM((8, 128), jnp.float32),
            pltpu.VMEM((2, side, D), jnp.bfloat16),
            pltpu.VMEM((blocks,) + gains.shape, jnp.float32),
            pltpu.VMEM((n_planes,) + gains.shape, jnp.float32),
            dma((len(slots), 2)),
            dma((2,)),
            dma((2 * n_planes,)),
            dma((2 * n_planes,)),
            dma((2 * n_planes,)),
            dma((n_ctx, 2 * n_planes)),
            dma((n_ctx, 2 * n_planes)),
            dma((n_ctx, 2 * n_planes)),
            dma((blocks,)),
            dma((blocks,)),
            dma((n_planes,)),
            dma((n_planes,)),
        ]
        + exchange_sems(n_ctx)
        + [dma((n_ctx, 2))] * 4,
        compiler_params=pltpu.CompilerParams(
            collective_id=0, has_side_effects=True, vmem_limit_bytes=60 * 2**20
        ),
        cost_estimate=cost(NS * 5 * D * D * columns, 350),
        name="muon",
    )(*slots, pair, gains)


def momentum_kernel(first, flipped, split, sum_ref, got_ref, moment_ref, grad_ref, new_ref, low_ref):
    core = lax.axis_index("core")
    tall = got_ref.shape[0]
    mine = sum_ref[pl.ds(pl.multiple_of(core * tall, tall), tall), :].astype(jnp.float32)
    got = got_ref[...].astype(jnp.float32)
    left = jnp.where(core == 0, mine, got)
    right = jnp.where(core == 0, got, mine)
    columns = moment_ref.shape[0 if flipped else 1]
    gradient = jnp.concatenate([left[:, :first], right[:, : columns - first]], 1)
    if flipped:
        grad_ref[...] = gradient.T
        new = momentum_decay * moment_ref[...] + grad_ref[...]
        new_ref[...] = new
        new = new.T
    else:
        grad_ref[...] = gradient
        new = momentum_decay * moment_ref[...] + gradient
        new_ref[...] = new
    if split:
        padded = low_ref.shape[2]
        for index, part in enumerate((low(new[:, :first]), low(new[:, first:]))):
            if part.shape[1] < padded:
                zeros = jnp.zeros((tall, padded - part.shape[1]), jnp.bfloat16)
                part = jnp.concatenate([part, zeros], 1)
            low_ref[index] = part
    else:
        low_ref[...] = low(new)


def momentum(summed, moment, first, padded, core, flipped=False, split=True):
    tall = summed.shape[0] // 2
    got = swap_core(lax.dynamic_slice_in_dim(summed, (1 - core) * tall, tall, 0))
    columns = moment.shape[0 if flipped else 1]
    out = jax.ShapeDtypeStruct(moment.shape, jnp.float32)
    low_shape = (2, tall, padded) if split else (tall, columns)
    return pl.pallas_call(
        functools.partial(momentum_kernel, first, flipped, split),
        out_shape=[out, out, jax.ShapeDtypeStruct(low_shape, jnp.bfloat16)],
        in_specs=in_vmem(3),
        out_specs=in_vmem(3),
        compiler_params=pltpu.CompilerParams(vmem_limit_bytes=48 * 2**20),
        name="momentum",
    )(summed, got, moment)


def small_start(shape, moments_ref, x_ref):
    n_ctx, shards, _ = shape
    columns, wide = moments_ref.shape[2:]
    for which in range(2):
        for ctx in range(n_ctx):
            for shard in range(shards):
                x_ref[which, shard * columns : (shard + 1) * columns, ctx * wide : (ctx + 1) * wide] = moments_ref[
                    ctx * shards + shard, which
                ]
        start = x_ref[which].astype(jnp.float32)
        norm = jnp.sqrt(jnp.sum(jnp.sum(start * start, 0, keepdims=True), 1, keepdims=True))
        x_ref[which] = low(start * (1.0 / (norm + 1e-07)))


def small_sweep(x_ref, y_ref):
    grams = [low(contract_cols(x_ref[which], x_ref[which])) for which in range(2)]
    for which in range(2):
        y_ref[which] = low(matmul(grams[which], x_ref[which]))
    for which in range(2):
        x_ref[which] = low(
            poly_first * x_ref[which].astype(jnp.float32)
            + poly_second * y_ref[which].astype(jnp.float32)
            + poly_third * matmul(grams[which], y_ref[which])
        )


def small_finish(shape, steps, olds, news, x_ref, own_ref):
    columns = own_ref.shape[0]
    plane = lax.axis_index("z_hi") * shape[2] + lax.axis_index("z_lo")
    own = 2 * plane + lax.axis_index("core")
    for which, (old_ref, new_ref) in enumerate(zip(olds, news)):
        own_ref[...] = x_ref[which, pl.ds(pl.multiple_of(own * columns, columns), columns), :].astype(jnp.float32)
        new_ref[...] = old_ref[...] * (1.0 - muon_rate * weight_decay) - steps[which] * own_ref[...]


def small_kernel(shape, steps, moments_ref, key_ref, value_ref, new_key_ref, new_value_ref, x_ref, y_ref, own_ref):
    small_start(shape, moments_ref, x_ref)

    def sweep(index, carry):
        small_sweep(x_ref, y_ref)
        return carry

    lax.fori_loop(0, NS, sweep, 0)
    small_finish(shape, steps, (key_ref, value_ref), (new_key_ref, new_value_ref), x_ref, own_ref)


def small_update(moments, key, value, shape, steps):
    out = jax.ShapeDtypeStruct(key.shape, jnp.float32)
    return pl.pallas_call(
        functools.partial(small_kernel, shape, steps),
        out_shape=[out, out],
        in_specs=in_vmem(3),
        out_specs=in_vmem(2),
        scratch_shapes=[
            pltpu.VMEM((2, KV * HD, D), jnp.bfloat16),
            pltpu.VMEM((2, KV * HD, D), jnp.bfloat16),
            pltpu.VMEM(key.shape, jnp.float32),
        ],
        compiler_params=pltpu.CompilerParams(vmem_limit_bytes=48 * 2**20),
        cost_estimate=cost(0, 15),
        name="small_update",
    )(moments, key, value)


def update_one(step, columns, first, flipped, weight_ref, parts, out_ref):
    direction = parts[0][...].reshape(parts[0].shape[-2:])[:, :first]
    if len(parts) > 1:
        second = parts[1][...].reshape(parts[1].shape[-2:])[:, : columns - first]
        direction = jnp.concatenate([direction, second], 1)
    direction = direction.astype(jnp.float32)
    if flipped:
        direction = direction.T
    out_ref[...] = weight_ref[...] * (1.0 - muon_rate * weight_decay) - step * direction


def update_kernel(step, columns, first, flipped, weight_ref, *refs):
    update_one(step, columns, first, flipped, weight_ref, refs[:-2], refs[-1])


def update_all_kernel(plans, halves, shape, small_steps, *refs):
    count = len(plans)
    weights, refs = refs[:count], refs[count:]
    parts = []
    for _, columns, first, _ in plans:
        used = 1 if first == columns else 2
        parts.append(refs[:used])
        refs = refs[used:]
    moments_ref, key_ref, value_ref = refs[:3]
    outs, (new_key_ref, new_value_ref) = refs[3 : 3 + count], refs[3 + count : 5 + count]
    x_ref, y_ref, own_ref = refs[5 + count :]
    step = pl.program_id(0) * halves + pl.program_id(1)
    for plan, weight_ref, part, out_ref in zip(plans, weights, parts, outs):
        update_one(*plan, weight_ref, part, out_ref)
    pl.when(step == 0)(lambda: small_start(shape, moments_ref, x_ref))
    pl.when(step < NS)(lambda: small_sweep(x_ref, y_ref))

    def finish():
        small_finish(shape, small_steps, (key_ref, value_ref), (new_key_ref, new_value_ref), x_ref, own_ref)

    pl.when(step == NS)(finish)


def update_all_weights(weights, plans, places, polar, moments, key, value, shape, small_steps):
    tall, wide = polar.shape[-2:]
    halves = 2
    rows = tall // halves
    blocks, parts = [], []
    for (_, columns, first, flipped), place in zip(plans, places):
        if flipped:
            blocks.append(pl.BlockSpec((columns, rows), lambda chip, half: (chip, half)))
        else:
            blocks.append(pl.BlockSpec((rows, columns), lambda chip, half: (half, chip)))
        for part in range(1 if first == columns else 2):
            parts.append(
                pl.BlockSpec(
                    (1, 1, 1, rows, wide),
                    lambda chip, half, place=place, part=part: tuple(place(chip, part)) + (half, 0),
                )
            )
    small = [
        pl.BlockSpec(moments.shape, lambda chip, half: (0, 0, 0, 0)),
        pl.BlockSpec(key.shape, lambda chip, half: (0, 0)),
        pl.BlockSpec(key.shape, lambda chip, half: (0, 0)),
    ]
    return pl.pallas_call(
        functools.partial(update_all_kernel, plans, halves, shape, small_steps),
        grid=(shape[0], halves),
        out_shape=[jax.ShapeDtypeStruct(weight.shape, jnp.float32) for weight in (*weights, key, value)],
        in_specs=blocks + parts + small,
        out_specs=blocks + small[1:],
        scratch_shapes=[
            pltpu.VMEM((2, KV * HD, D), jnp.bfloat16),
            pltpu.VMEM((2, KV * HD, D), jnp.bfloat16),
            pltpu.VMEM(key.shape, jnp.float32),
        ],
        compiler_params=pltpu.CompilerParams(vmem_limit_bytes=56 * 2**20),
        cost_estimate=cost(0, 25),
        name="update_all",
    )(*weights, *([polar] * len(parts)), moments, key, value)


def update(weight, polar, earlier, step, columns, first, flipped, place):
    tall, wide = polar.shape[-2:]
    count = weight.shape[0 if flipped else 1] // columns
    if flipped:
        block = pl.BlockSpec((columns, tall), lambda chip: (chip, 0))
    else:
        block = pl.BlockSpec((tall, columns), lambda chip: (0, chip))
    parts = [
        pl.BlockSpec((1, 1, 1, tall, wide), lambda chip, part=part: tuple(place(chip, part)) + (0, 0))
        for part in range(1 if first == columns else 2)
    ]
    return pl.pallas_call(
        functools.partial(update_kernel, step, columns, first, flipped),
        grid=(count,),
        out_shape=jax.ShapeDtypeStruct(weight.shape, jnp.float32),
        in_specs=[block] + parts + anywhere(1),
        out_specs=block,
        compiler_params=pltpu.CompilerParams(vmem_limit_bytes=48 * 2**20),
        name="update",
    )(weight, *([polar] * len(parts)), earlier)


def scatter_kernel(shape, term, n_lhs, n_earlier, *refs):
    lhs, right = refs[:n_lhs], refs[n_lhs]
    refs = refs[n_lhs + 1 + n_earlier :]
    out, part, from_core, from_ctx = refs[:4]
    ex = Exchange(shape, refs[4:])
    ex.greet()
    chunks, tall, wide = out.shape

    def make(other, idx):
        block = ex.place(other, idx)
        start = ((block % 2) * ex.n_ctx + block // 2) * chunks * tall
        rows = pl.ds(pl.multiple_of(start, chunks * tall), chunks * tall)
        total = term([left[rows, :] for left in lhs], right)
        part[other, idx] = low(total).reshape(chunks, tall, wide)

    ex.sum_pieces(part, from_core, from_ctx, make, out)
    ex.sums_sent()


def product_scatter(lhs, right, term, shape, tokens, collective_id, name, earlier=()):
    n_ctx = shape[0]
    piece = (tokens // 32, 32, D)
    flops = sum(2 * a.shape[0] * a.shape[1] * D for a in lhs)
    out = pl.pallas_call(
        functools.partial(scatter_kernel, shape, term, len(lhs), len(earlier)),
        out_shape=jax.ShapeDtypeStruct(piece, jnp.float32),
        in_specs=in_vmem(len(lhs) + 1) + anywhere(len(earlier)),
        out_specs=pl.BlockSpec(memory_space=pltpu.VMEM),
        scratch_shapes=[
            pltpu.VMEM((2, n_ctx) + piece, jnp.bfloat16),
            pltpu.VMEM((n_ctx,) + piece, jnp.bfloat16),
            pltpu.VMEM((n_ctx,) + piece, jnp.bfloat16),
        ]
        + exchange_sems(n_ctx),
        compiler_params=pltpu.CompilerParams(
            collective_id=collective_id, has_side_effects=True, vmem_limit_bytes=56 * 2**20
        ),
        cost_estimate=cost(flops, 40),
        name=name,
    )(*lhs, right, *earlier)
    return out.reshape(tokens, D)


def gather_kernel(shape, finish, n_weights, n_outs, n_earlier, block_ref, *refs):
    weights = refs[:n_weights]
    refs = refs[n_weights + n_earlier :]
    gathered_out, outs = refs[0], refs[1 : 1 + n_outs]
    gathered, out_sems = refs[1 + n_outs : 3 + n_outs]
    ex = Exchange(shape, refs[3 + n_outs :])
    ex.greet()
    tokens = block_ref.shape[0]
    gathered[ex.place(0, 0)] = block_ref[...]

    def keep(block):
        row = (block % 2) * ex.n_ctx + block // 2
        return pltpu.make_async_copy(gathered.at[block], gathered_out.at[row], out_sems.at[block]), row

    def use(block, step):
        del step
        copy, row = keep(block)
        copy.start()
        rows = pl.ds(pl.multiple_of(row * tokens, tokens), tokens)
        finish(rows, gathered[block], weights, outs)

    ex.gather_pieces(gathered, use)
    ex.gathers_sent()
    for block in range(ex.ranks):
        keep(block)[0].wait()


def gather_product(block, weights, finish, outs, shape, collective_id, name, earlier=()):
    tokens = block.shape[0]
    ranks = 2 * shape[0]
    flops = sum(2 * ranks * tokens * w.shape[0] * w.shape[1] for w in weights)
    result = pl.pallas_call(
        functools.partial(gather_kernel, shape, finish, len(weights), len(outs), len(earlier)),
        out_shape=[jax.ShapeDtypeStruct((ranks, tokens, D), jnp.bfloat16)] + outs,
        in_specs=in_vmem(1 + len(weights)) + anywhere(len(earlier)),
        out_specs=anywhere(1) + in_vmem(len(outs)),
        scratch_shapes=[
            pltpu.VMEM((ranks, tokens, D), jnp.bfloat16),
            pltpu.SemaphoreType.DMA((ranks,)),
        ]
        + exchange_sems(shape[0]),
        compiler_params=pltpu.CompilerParams(
            collective_id=collective_id, has_side_effects=True, vmem_limit_bytes=56 * 2**20
        ),
        cost_estimate=cost(flops, 40),
        name=name,
    )(block, *weights, *earlier)
    return [result[0].reshape(ranks * tokens, D)] + list(result[1:])


def finish_nothing(rows, block, weights, outs):
    del rows, block, weights, outs


def finish_hidden(rows, block, weights, outs):
    columns = outs[0].shape[1]
    gate_pre = matmul(block, weights[0][:, :columns])
    outs[0][rows, :] = gate_pre
    upper = matmul(block, weights[0][:, columns:])
    outs[1][rows, :] = upper
    outs[2][rows, :] = low(gate_pre * jax.nn.sigmoid(gate_pre) * upper)


def finish_mixed(rows, block, weights, outs):
    outs[0][rows, :] = low(matmul(block, weights[0][...]))


def term_one(lhs, right):
    return contract_cols(lhs[0], right[...])


def term_two(lhs, right):
    columns = lhs[0].shape[1]
    return contract_cols(lhs[0], right[:, :columns]) + contract_cols(lhs[1], right[:, columns:])


class AllSum:
    def __init__(self, ex, n_planes, z_lo, near, far, near_out, near_in, far_out, far_in):
        self.ex, self.n_planes, self.z_lo = ex, n_planes, z_lo
        self.near, self.far = near, far
        self.near_sems, self.far_sems = (near_out, near_in), (far_out, far_in)
        self.rank = 2 * ex.ctx + ex.core
        self.plane = lax.axis_index("z_hi") * z_lo + lax.axis_index("z_lo")

    def rank_id(self, offset):
        there = (self.rank + offset) % self.ex.ranks
        n_lo = self.ex.n_lo
        return {"ctx_hi": there // 2 // n_lo, "ctx_lo": there // 2 % n_lo, "core": there % 2}

    def plane_id(self, offset):
        there = (self.plane + offset) % self.n_planes
        return {"z_hi": there // self.z_lo, "z_lo": there % self.z_lo}

    def copies(self, slots, own, count, device, sems):
        return [
            self.ex.copy(slots.at[own], slots.at[own], sems[0].at[offset], sems[1].at[own], device(offset))
            for offset in range(1, count)
        ]

    def total(self, slots, own, count, device, sems):
        for offset in range(1, count):
            there = (own + offset) % count
            block = slots.at[there]
            self.ex.copy(block, block, sems[0].at[offset], sems[1].at[there], device(offset)).wait_recv()
        for copy in self.copies(slots, own, count, device, sems):
            copy.wait_send()
        total = slots[0]
        for index in range(1, count):
            total = total + slots[index]
        return total

    def begin(self, value):
        self.near[self.rank] = value
        for copy in self.copies(self.near, self.rank, self.ex.ranks, self.rank_id, self.near_sems):
            copy.start()

    def between(self):
        self.far[self.plane] = self.total(self.near, self.rank, self.ex.ranks, self.rank_id, self.near_sems)
        for copy in self.copies(self.far, self.plane, self.n_planes, self.plane_id, self.far_sems):
            copy.start()

    def end(self):
        return self.total(self.far, self.plane, self.n_planes, self.plane_id, self.far_sems)


def nothing_kernel(*refs):
    del refs


def after(values, *others):
    return pl.pallas_call(
        nothing_kernel,
        out_shape=jax.ShapeDtypeStruct(values.shape, values.dtype),
        in_specs=anywhere(1 + len(others)),
        out_specs=pl.BlockSpec(memory_space=pl.ANY),
        input_output_aliases={0: 0},
        name="after",
    )(values, *others)


def swap_core(values):
    return lax.ppermute(values, "core", [(0, 1), (1, 0)])


def split_cores(values, core):
    mine = jnp.where(core == 0, values[0], values[1])
    theirs = jnp.where(core == 0, values[1], values[0])
    got = swap_core(theirs)
    return jnp.stack([jnp.where(core == 0, mine, got), jnp.where(core == 0, got, mine)])


QUERY_ROWS = 256


def turned_pair(values):
    lane = lax.broadcasted_iota(jnp.int32, values.shape, 1)
    return jnp.where(lane % HD < HD // 2, pltpu.roll(values, 2 * HD - HD // 2, 1), pltpu.roll(values, HD // 2, 1))


def is_visible(start, stop):
    rows = lax.broadcasted_iota(jnp.int32, (QUERY_ROWS, stop), 0) + start
    return lax.broadcasted_iota(jnp.int32, (QUERY_ROWS, stop), 1) <= rows


def attention_kernel(pairs, steps, normed_ref, w_ref, cos_ref, sin_ref, mixed_ref, q_ref, k_ref, v_ref, log_ref):
    step = pl.program_id(1)
    projected = matmul(normed_ref[...], w_ref[...])
    cos, sin = cos_ref[...], sin_ref[...]
    lane = lax.broadcasted_iota(jnp.int32, (QUERY_ROWS, 2 * HD), 1)
    left = lane < HD

    def pair_of(values, pair):
        return values[:, pair * 2 * HD : (pair + 1) * 2 * HD]

    def rope(values):
        return values * cos + turned_pair(values) * sin

    both = pair_of(projected, pairs)
    keys = rope(both)
    rows = pl.ds(pl.multiple_of(step * QUERY_ROWS, QUERY_ROWS), QUERY_ROWS)
    k_ref[rows, :] = low(jnp.where(left, keys, pltpu.roll(keys, HD, 1)))
    v_ref[rows, :] = low(jnp.where(left, pltpu.roll(both, HD, 1), both))
    for pair in range(pairs):
        q_ref[:, pair * 2 * HD : (pair + 1) * 2 * HD] = low(rope(pair_of(projected, pair)))

    def attend(index):
        stop = (index + 1) * QUERY_ROWS
        seen = is_visible(index * QUERY_ROWS, stop)
        logs = jnp.zeros((QUERY_ROWS, 2 * HD), jnp.float32)
        for pair in range(pairs):
            outs = []
            for half in range(2):
                query = jnp.where(left == (half == 0), pair_of(q_ref[...], pair), 0.0)
                scores = contract_cols(low(query), k_ref[:stop, :]) * HD ** (-0.5)
                scores = jnp.where(seen, scores, masked_score)
                top = jnp.max(scores, -1, keepdims=True)
                expo = jnp.exp(scores - top)
                total = jnp.sum(expo, -1, keepdims=True)
                outs.append(matmul(low(expo), v_ref[:stop, :]) / total)
                logs = jnp.where(lane == 2 * pair + half, top + jnp.log(total), logs)
            mixed_ref[:, pair * 2 * HD : (pair + 1) * 2 * HD] = low(jnp.where(left, outs[0], outs[1]))
        log_ref[...] = logs

    for index in range(steps):
        pl.when(step == index)(functools.partial(attend, index))


def attention(normed, weight, cos, sin, length):
    every, columns = normed.shape[0], weight.shape[1]
    pairs = columns // (2 * HD) - 1
    steps = length // QUERY_ROWS
    pair = 2 * HD

    def rows(width):
        return pl.BlockSpec((QUERY_ROWS, width), lambda n, b: (n * steps + b, 0))

    def sequence():
        return pl.BlockSpec((length, pair), lambda n, b: (n, 0))

    table = pl.BlockSpec((QUERY_ROWS, pair), lambda n, b: (b, 0))
    return pl.pallas_call(
        functools.partial(attention_kernel, pairs, steps),
        grid=(every // length, steps),
        out_shape=[
            jax.ShapeDtypeStruct((every, pairs * pair), jnp.bfloat16),
            jax.ShapeDtypeStruct((every, pairs * pair), jnp.bfloat16),
            jax.ShapeDtypeStruct((every, pair), jnp.bfloat16),
            jax.ShapeDtypeStruct((every, pair), jnp.bfloat16),
            jax.ShapeDtypeStruct((every, pair), jnp.float32),
        ],
        in_specs=[rows(D), pl.BlockSpec((D, columns), lambda n, b: (0, 0)), table, table],
        out_specs=[rows(pairs * pair), rows(pairs * pair), sequence(), sequence(), rows(pair)],
        compiler_params=pltpu.CompilerParams(vmem_limit_bytes=48 * 2**20),
        cost_estimate=cost(0, 25),
        name="attention",
    )(normed, weight, cos, sin)


def attention_back_kernel(
    pairs, steps, q_ref, d_ref, k_ref, v_ref, log_ref, cos_ref, sin_ref, earlier_ref, out_ref, dk_ref, dv_ref
):
    del earlier_ref
    step = pl.program_id(1)
    lane = lax.broadcasted_iota(jnp.int32, (QUERY_ROWS, 2 * HD), 1)
    left = lane < HD

    def clear():
        dk_ref[...] = jnp.zeros(dk_ref.shape, jnp.float32)
        dv_ref[...] = jnp.zeros(dv_ref.shape, jnp.float32)

    pl.when(step == 0)(clear)

    def unrope(values, rows):
        return values * cos_ref[rows, :] - turned_pair(values) * sin_ref[rows, :]

    def attend(index):
        stop = (index + 1) * QUERY_ROWS
        rows = slice(index * QUERY_ROWS, stop)
        seen = is_visible(index * QUERY_ROWS, stop)
        for pair in range(pairs):
            at = slice(pair * 2 * HD, (pair + 1) * 2 * HD)
            parts = []
            for half in range(2):
                mine = left == (half == 0)
                query = low(jnp.where(mine, q_ref[:, at], 0.0))
                d_rows = low(jnp.where(mine, d_ref[:, at], 0.0))
                scores = contract_cols(query, k_ref[:stop, :]) * HD ** (-0.5)
                log = jnp.sum(jnp.where(lane == 2 * pair + half, log_ref[...], 0.0), -1, keepdims=True)
                probs = jnp.where(seen, jnp.exp(scores - log), 0.0)
                d_probs = contract_cols(d_rows, v_ref[:stop, :])
                delta = jnp.sum(probs * d_probs, -1, keepdims=True)
                d_scores = low(probs * (d_probs - delta))
                parts.append(matmul(d_scores, k_ref[:stop, :]) * HD ** (-0.5))
                dk_ref[:stop, :] += contract_rows(d_scores, query) * HD ** (-0.5)
                dv_ref[:stop, :] += contract_rows(low(probs), d_rows)
            out_ref[rows, at] = low(unrope(jnp.where(left, parts[0], parts[1]), rows))

    for index in range(steps):
        pl.when(step == index)(functools.partial(attend, index))

    def finish():
        def fold(chunk, carry):
            rows = pl.ds(pl.multiple_of(chunk * QUERY_ROWS, QUERY_ROWS), QUERY_ROWS)
            d_keys, d_values = dk_ref[rows, :], dv_ref[rows, :]
            d_keys = unrope(d_keys + pltpu.roll(d_keys, HD, 1), rows)
            d_values = d_values + pltpu.roll(d_values, HD, 1)
            out_ref[rows, pairs * 2 * HD :] = low(jnp.where(left, d_keys, d_values))
            return carry

        lax.fori_loop(0, steps, fold, 0)

    pl.when(step == steps - 1)(finish)


def attention_back(query, d_mixed, keys, values, logs, cos, sin, earlier, length):
    every = query.shape[0]
    pair = 2 * HD
    pairs = query.shape[1] // pair
    steps = length // QUERY_ROWS

    def rows(width):
        return pl.BlockSpec((QUERY_ROWS, width), lambda n, b: (n * steps + b, 0))

    def sequence(width):
        return pl.BlockSpec((length, width), lambda n, b: (n, 0))

    table = pl.BlockSpec((length, pair), lambda n, b: (0, 0))
    return pl.pallas_call(
        functools.partial(attention_back_kernel, pairs, steps),
        grid=(every // length, steps),
        out_shape=jax.ShapeDtypeStruct((every, (pairs + 1) * pair), jnp.bfloat16),
        in_specs=[rows(pairs * pair), rows(pairs * pair), sequence(pair), sequence(pair), rows(pair), table, table]
        + anywhere(1),
        out_specs=sequence((pairs + 1) * pair),
        scratch_shapes=[pltpu.VMEM((length, pair), jnp.float32)] * 2,
        compiler_params=pltpu.CompilerParams(vmem_limit_bytes=48 * 2**20),
        cost_estimate=cost(0, 40),
        name="attention_back",
    )(query, d_mixed, keys, values, logs, cos, sin, earlier)


def body(
    inputs,
    cotangent,
    gains,
    gain_moment,
    gain_second,
    w_query,
    w_key,
    w_value,
    w_out,
    w_gate,
    w_up,
    w_down,
    m_query,
    m_key,
    m_value,
    m_out,
    m_gate,
    m_up,
    m_down,
):
    n_ctx = lax.axis_size("ctx_hi") * lax.axis_size("ctx_lo")
    n_lo = lax.axis_size("ctx_lo")
    n_planes = lax.axis_size("z_hi") * lax.axis_size("z_lo")
    ctx, core = lax.axis_index(CTX), lax.axis_index("core")
    plane = lax.axis_index(PLANES)
    halved = n_planes == 4
    ranks = 2 * n_ctx
    tokens = inputs.shape[1]
    length = tokens * n_ctx
    rows_here = w_query.shape[0]
    sharers = ranks // KV
    head_cols = D // ranks
    chip_ff, chip_model = FF // n_ctx, D // n_ctx
    ff_cols = -(-chip_ff // 256) * 128
    transpose_pairs = [(c * n_planes + z, z * n_planes + c) for c in range(n_ctx) for z in range(n_planes)]

    def transposed(values):
        return lax.ppermute(values, CTX + PLANES, transpose_pairs)

    def for_cores(values, first, padded):
        parts = (values[:, :first], values[:, first:])
        return jnp.stack([jnp.pad(part, ((0, 0), (0, padded - part.shape[1]))) for part in parts])

    def own_columns(weight, columns, first, padded):
        part = lax.dynamic_slice_in_dim(weight, ctx * columns, columns, 1)
        return split_cores(for_cores(low(part), first, padded), core).reshape(2 * rows_here, padded)

    def over_planes(values):
        return lax.all_gather(values, PLANES, axis=0, tiled=True)

    key_value = jnp.stack([low(w_key), low(w_value)], 1)
    key_value = lax.all_gather(key_value, PLANES + ("core",), axis=0, tiled=False)
    own_head = lax.dynamic_slice_in_dim(key_value, (2 * ctx + core) // sharers * sharers, sharers, 0)
    wide_kv = jnp.transpose(own_head, (1, 2, 0, 3)).reshape(D, 2 * HD)
    out_part = transposed(low(lax.dynamic_slice_in_dim(w_out, ctx * chip_model, chip_model, 1)))
    own_query = own_columns(w_query, chip_model, head_cols, head_cols)
    wide_both = over_planes(jnp.concatenate([own_query, out_part.T], 1))
    wide_query, wide_out = wide_both[:, :head_cols], wide_both[:, head_cols:]
    wide_qkv = jnp.concatenate([wide_query, wide_kv], 1)
    own_gate = own_columns(w_gate, chip_ff, ff_cols, ff_cols)
    own_up = own_columns(w_up, chip_ff, ff_cols, ff_cols)
    wide_gate_up = over_planes(jnp.concatenate([own_gate, own_up], 1))

    shape = (n_ctx, n_lo)
    every = 2 * length

    def sum_planes(values, dimension=0):
        return lax.psum_scatter(low(values), PLANES, scatter_dimension=dimension, tiled=True)

    cos_table, sin_table = rope_tables(jnp.arange(length, dtype=jnp.float32), HD)
    stream = inputs[0].astype(jnp.float32)
    normed, inverse_one = norm_forward(stream, gains[0])
    all_normed = gather_product(low(normed), [], finish_nothing, [], shape, 1, "gather_normed")[0]
    all_cotangent = gather_product(
        cotangent[0], [], finish_nothing, [], shape, 8, "gather_cotangent", [all_normed]
    )[0]
    wide_down = over_planes(after(own_columns(w_down.T, chip_ff, ff_cols, ff_cols), all_normed))
    mixed_low, query_rot, key_rot, value_low, logs = attention(all_normed, wide_qkv, cos_table, sin_table, length)
    middle = stream + product_scatter([mixed_low], wide_out, term_one, shape, tokens, 2, "scatter_mixed", [all_cotangent])
    normed_two, inverse_two = norm_forward(middle, gains[1])
    all_two, gate_pre, upper, hidden_low = gather_product(
        low(normed_two),
        [wide_gate_up],
        finish_hidden,
        [jax.ShapeDtypeStruct((every, ff_cols), jnp.float32)] * 2
        + [jax.ShapeDtypeStruct((every, ff_cols), jnp.bfloat16)],
        shape,
        3,
        "gather_hidden",
    )
    sigmoid_gate = jax.nn.sigmoid(gate_pre)
    silu_gate = gate_pre * sigmoid_gate
    part_down = low(contract_rows(all_cotangent, hidden_low))
    sum_down = sum_planes(part_down)
    down_sum = product_scatter(
        [hidden_low], wide_down, term_one, shape, tokens, 4, "scatter_hidden", [part_down]
    )
    block_out = low(middle + down_sum)[None]

    d_hidden = matmul(all_cotangent, wide_down)
    d_up = low(d_hidden * silu_gate)
    d_gate = low(d_hidden * upper * sigmoid_gate * (1.0 + gate_pre * (1.0 - sigmoid_gate)))
    part_gate = low(contract_rows(all_two, d_gate))
    part_up = low(contract_rows(all_two, d_up))
    sum_gate, sum_up = sum_planes(part_gate), sum_planes(part_up)
    d_normed_two = product_scatter(
        [d_gate, d_up],
        wide_gate_up,
        term_two,
        shape,
        tokens,
        5,
        "scatter_d_hidden",
        [part_gate, part_up, down_sum, sum_down],
    )
    d_mid_norm, gain_two = norm_backward(middle, inverse_two, gains[1], d_normed_two)
    d_middle = cotangent[0].astype(jnp.float32) + d_mid_norm
    widths = (ff_cols, -(-(chip_ff - ff_cols) // 128) * 128, chip_model)
    grad_down, new_m_down, low_down = momentum(sum_down, m_down, ff_cols, ff_cols, core, flipped=True)
    grad_gate, new_m_gate, low_gate = momentum(sum_gate, m_gate, ff_cols, ff_cols, core)
    all_branch, d_mixed = gather_product(
        low(d_middle),
        [wide_out],
        finish_mixed,
        [jax.ShapeDtypeStruct((every, head_cols), jnp.bfloat16)],
        shape,
        6,
        "gather_d_mixed",
        [sum_gate],
    )
    grad_up, new_m_up, low_up = momentum(sum_up, m_up, ff_cols, ff_cols, core)

    part_out = low(contract_rows(all_branch, mixed_low))
    d_qkv = attention_back(
        query_rot, d_mixed, key_rot, value_low, logs, cos_table, sin_table, part_out, length
    )
    part_qkv = low(contract_rows(all_normed, d_qkv))
    part_all = jnp.concatenate([part_qkv[:, :head_cols], part_out, part_qkv[:, head_cols:]], 1)
    sum_all = sum_planes(part_all)
    d_normed = product_scatter(
        [d_qkv], wide_qkv, term_one, shape, tokens, 7, "scatter_d_project", [part_all, low_up, low_gate, low_down]
    )
    sum_query = sum_all[:, :head_cols]
    grad_rest = transposed(sum_all[:, head_cols:])
    grad_out = grad_rest[:, :head_cols].T.astype(jnp.float32)
    new_m_out = momentum_decay * m_out + grad_out
    slots = [low_gate, low_down, low_up]
    if halved:
        grad_query, new_m_query, low_query = momentum(
            sum_query, m_query, head_cols, head_cols, core, split=False
        )
        pair = jnp.stack([low_query, low(new_m_out)])
    else:
        grad_query, new_m_query, low_query = momentum(sum_query, m_query, head_cols, ff_cols, core)
        slots += [low_query, for_cores(low(new_m_out), head_cols, ff_cols)]
        slots += [jnp.zeros_like(low_gate)] * (n_planes - len(slots))
        pair = jnp.zeros((2, rows_here, chip_model), jnp.bfloat16)
    d_in_norm, gain_one = norm_backward(stream, inverse_one, gains[0], d_normed)
    input_grad = (d_middle + d_in_norm)[None]

    grad_kv = grad_rest[:, head_cols:]
    grad_kv = grad_kv.reshape(-1, 2, n_lo, 2, HD // sharers)
    theirs = swap_core(jnp.where(core == 0, grad_kv[:, :, :, 1], grad_kv[:, :, :, 0]))
    mine = jnp.where(core == 0, grad_kv[:, :, :, 0], grad_kv[:, :, :, 1])
    grad_kv = mine.astype(jnp.float32) + theirs.astype(jnp.float32)
    if n_lo > 1:
        grad_kv = lax.psum_scatter(grad_kv, "z_lo", scatter_dimension=2, tiled=True)
    grad_kv = grad_kv[:, :, 0]
    grad_key, grad_value = grad_kv[:, 0], grad_kv[:, 1]
    new_m_key = momentum_decay * m_key + grad_key
    new_m_value = momentum_decay * m_value + grad_value

    moment_kv = low(jnp.stack([new_m_key.T, new_m_value.T]))
    moment_kv = lax.all_gather(moment_kv, CTX + PLANES + ("core",), axis=0, tiled=False)
    gains_here = jnp.stack([gain_one, gain_two]).reshape(8, -1)
    polar, gain_grad = muon(slots, pair, gains_here, shape + (n_planes, n_lo, halved, widths))
    gain_grad = gain_grad.reshape(gains.shape)
    moment_one = adam_first * gain_moment + (1.0 - adam_first) * gain_grad
    moment_two = adam_second * gain_second + (1.0 - adam_second) * gain_grad * gain_grad
    adam_ratio = (
        moment_one
        / (1.0 - adam_first**STEP)
        / (jnp.sqrt(moment_two / (1.0 - adam_second**STEP)) + adam_eps)
    )
    gains_new = gains - adam_rate * adam_ratio

    small_shape = (n_ctx, 2 * n_planes, n_lo)
    small_steps = [muon_rate * D ** (-0.5) * math.sqrt(max(D, KV * HD))] * 2
    fused = halved and chip_ff % 128 == 0 and chip_model % 128 == 0 and rows_here % 256 == 0
    fused = fused and n_ctx * 2 > NS
    if not fused:
        new_key, new_value = small_update(moment_kv, w_key.T, w_value.T, small_shape, small_steps)
        new_key, new_value = new_key.T, new_value.T
    half_ctx = n_ctx // 2

    def step_of(spread, widest):
        return muon_rate * spread * math.sqrt(widest)

    def updated(weight, spread, widest, direction):
        return weight * (1.0 - muon_rate * weight_decay) - step_of(spread, widest) * direction

    def in_parts(weight, spread, widest, columns, first, flipped, place):
        parts = 1 if first == columns else 2
        if columns % 128 == 0:
            return update(weight, polar, new_key, step_of(spread, widest), columns, first, flipped, place)
        chips = []
        for chip in range(n_ctx):
            for part in range(parts):
                width = first if part == 0 else columns - first
                chips.append(polar[place(chip, part)][:, :width])
        direction = jnp.concatenate(chips, 1).astype(jnp.float32)
        return updated(weight, spread, widest, direction.T if flipped else direction)

    def ff_update(weight, spread, slot, flipped=False):
        return in_parts(
            weight, spread, max(D, FF), chip_ff, ff_cols, flipped, lambda chip, part: (chip, slot, part)
        )

    def model_update(weight, spread, which):
        if halved:
            return in_parts(
                weight,
                spread,
                D,
                chip_model,
                chip_model,
                False,
                lambda chip, part: (chip % half_ctx + which * half_ctx, n_planes - 1, chip // half_ctx),
            )
        return in_parts(
            weight, spread, D, chip_model, chip_model // 2, False, lambda chip, part: (chip, 3 + which, part)
        )

    if fused:

        def pair_place(which):
            return lambda chip, part: (chip % half_ctx + which * half_ctx, n_planes - 1, chip // half_ctx)

        def ff_place(slot):
            return lambda chip, part: (chip, slot, part)

        new_query, new_out, new_gate, new_down, new_up, new_key, new_value = update_all_weights(
            (w_query, w_out, w_gate, w_down, w_up),
            (
                (step_of(D ** (-0.5), D), chip_model, chip_model, False),
                (step_of(32 ** (-0.5), D), chip_model, chip_model, False),
                (step_of(D ** (-0.5), max(D, FF)), chip_ff, ff_cols, False),
                (step_of(FF ** (-0.5), max(D, FF)), chip_ff, ff_cols, True),
                (step_of(D ** (-0.5), max(D, FF)), chip_ff, ff_cols, False),
            ),
            (pair_place(0), pair_place(1), ff_place(0), ff_place(1), ff_place(2)),
            polar,
            moment_kv,
            w_key.T,
            w_value.T,
            small_shape,
            small_steps,
        )
        new_key, new_value = new_key.T, new_value.T
    else:
        new_query = model_update(w_query, D ** (-0.5), 0)
        new_out = model_update(w_out, 32 ** (-0.5), 1)
        new_gate = ff_update(w_gate, D ** (-0.5), 0)
        new_up = ff_update(w_up, D ** (-0.5), 2)
        new_down = ff_update(w_down, FF ** (-0.5), 1, True)
    return (
        block_out,
        input_grad,
        gain_grad,
        moment_one,
        moment_two,
        gains_new,
        grad_query,
        new_m_query,
        new_query,
        grad_key,
        new_m_key,
        new_key,
        grad_value,
        new_m_value,
        new_value,
        grad_out,
        new_m_out,
        new_out,
        grad_gate,
        new_m_gate,
        new_gate,
        grad_up,
        new_m_up,
        new_up,
        grad_down,
        new_m_down,
        new_down,
    )


def solution(mesh):
    n_ctx, n_fsdp = mesh.shape["ctx"], mesh.shape["fsdp"]
    n_lo = 2 * n_ctx // KV // 2
    n_planes = n_fsdp // 2
    finer = Mesh(
        mesh.devices.reshape(n_ctx // n_lo, n_lo, n_planes // n_lo, n_lo, 2),
        CTX + PLANES + ("core",),
    )
    fsdp = PLANES + ("core",)
    tokens, whole = P(fsdp, CTX, None), P()
    rows, columns = P(fsdp, None), P(None, fsdp)
    row_block, column_block = P(fsdp, CTX), P(CTX, fsdp)
    matrix, transposed = (row_block, row_block, rows), (column_block, column_block, columns)
    return jax.shard_map(
        body,
        mesh=finer,
        in_specs=(tokens, tokens, whole, whole, whole)
        + (rows, columns, columns, rows, rows, rows, columns)
        + (row_block, column_block, column_block, row_block, row_block, row_block, column_block),
        out_specs=(tokens, tokens, whole, whole, whole, whole)
        + matrix
        + transposed
        + transposed
        + matrix
        + matrix
        + matrix
        + transposed,
        check_vma=False,
    )
```
